128 devices in a mesh: gx: 8 (over x, core), gy: 16 (over y, z).
Axes of the slice: x: 4, y: 4, z: 4, core: 2. Of those that a mesh axis runs over, the one named last changes fastest.
Arguments:
- conductivity: float32 [16, 512, 2048], P(None, 'gx', 'gy'), may hold values from 0.2 to 5
- storage: float32 [16, 512, 2048], P(None, 'gx', 'gy'), may hold values from 0.5 to 5
- recharge: float32 [16, 512, 2048], P(None, 'gx', 'gy'), may hold values from -30 to 30
- block_ids: int32 [16384], replicated, may hold values from 0 to 131071, as said below
- neighbours: int32 [16384, 6], P(('gx', 'gy')), may hold values from -1 to 16383, as said below
- concentration: float32 [16384, 128], P(('gx', 'gy')), may hold values from 0.1 to 3
- sorption: float32 [16384, 128], P(('gx', 'gy')), may hold values from 0.3 to 3
Outputs:
- head: float32 [16, 512, 2048], P(None, 'gx', 'gy')
- solute: float32 [16384, 128], P(('gx', 'gy'))
The draws below stay inside these ranges and needn't reach their ends.
Inputs may be any that keep to these rules, and one draw needn't show every extreme that they name: `block_ids`: distinct block numbers in the layout above. The blocks of one owner lie in 64 of the bricks, exactly 2 in each of those; the order of an owner's entries is arbitrary. `neighbours`: entry j of row i is the active block that shares block i's west, east, south, north, lower or upper side (j = 0 to 5), or -1; the relation is symmetric.
All inputs are finite; a program needn't handle non-finite values.
Results may differ from the reference program's by a relative error of at most 0.0003.
Values sent between devices are 32-bit elements; how exact they have to be, the bound alone decides.
No kernel may reach another device: no remote copies, remote signals or barrier semaphores. Data moves between devices by JAX's collectives and lax.ppermute only.
A program may use at most 128 MiB of HBM per device.

```python
import math
import jax
import jax.numpy as jnp
from jax import lax

NZ = 16
CX = 64
CY = 128
ITERS = 2
STEPS = 2
PICARD = 3
ACT_DEV = 128
CAP = 2
ACTIVE = 16384
NX = 512
NY = 2048
N_GX = 8
N_GY = 16


def block_layout(key):
    bricks = ACTIVE // ACT_DEV
    sources = ACT_DEV // CAP
    line_count = NZ * CX
    patch_rows = 2 * ACT_DEV // NZ
    keys = jax.random.split(key, 4)
    heat = jax.random.permutation(keys[0], bricks) % 4
    noise = jax.random.randint(keys[1], (bricks, bricks), 0, 65536)
    score = (noise + heat[None, :] * 32768) * bricks + jnp.arange(bricks)[None, :]
    chosen_score, chosen = lax.top_k(score, sources)
    picked = jnp.zeros((bricks, bricks), jnp.int32).at[jnp.arange(bricks)[:, None], chosen].set(1)
    before = jnp.cumsum(picked, 0) - picked
    rank = jnp.take_along_axis(before, chosen, 1)
    first_row = jax.random.randint(keys[2], (), 0, CX)
    offsets = rank[:, :, None] * CAP + jnp.arange(CAP)[None, None, :]
    picked_lines = offsets // patch_rows * CX + (first_row + offsets % patch_rows) % CX
    blocks = (chosen[:, :, None] * line_count + picked_lines).reshape(bricks, ACT_DEV)
    shuffle = jax.vmap(lambda single: jax.random.permutation(single, ACT_DEV))(jax.random.split(keys[3], bricks))
    return jnp.take_along_axis(blocks, shuffle, 1).reshape(ACTIVE).astype(jnp.int32)


def draw_block_ids(key, part):
    blocks = block_layout(key)
    return blocks


def draw_neighbours(key, part):
    blocks = block_layout(key)
    bricks = ACTIVE // ACT_DEV
    across = NY // CY
    downward = NX // CX
    line_count = NZ * CX
    index_of = jnp.full((bricks * line_count,), -1, jnp.int32).at[blocks].set(jnp.arange(ACTIVE, dtype=jnp.int32))
    brick = blocks // line_count
    line = blocks % line_count
    layer = line // CX
    row = line % CX
    brick_row = brick // across
    brick_col = brick % across
    west = jnp.where(row > 0, blocks - 1, jnp.where(brick_row > 0, blocks - across * line_count + CX - 1, -1))
    east = jnp.where(row < CX - 1, blocks + 1, jnp.where(brick_row < downward - 1, blocks + across * line_count - (CX - 1), -1))
    south = jnp.where(brick_col > 0, blocks - line_count, -1)
    north = jnp.where(brick_col < across - 1, blocks + line_count, -1)
    below = jnp.where(layer > 0, blocks - CX, -1)
    above = jnp.where(layer < NZ - 1, blocks + CX, -1)
    target = jnp.stack([west, east, south, north, below, above], 1)
    found = index_of[jnp.clip(target, 0, bricks * line_count - 1)]
    return jnp.where(target >= 0, found, -1).astype(jnp.int32)


def draw_recharge(key, part):
    key = jax.random.fold_in(key, 11)
    keys = jax.random.split(key, 3)
    row_scale = jnp.exp(jax.random.uniform(keys[0], (1, NX, 1), jnp.float32, 0.0, math.log(10.0)))
    column_scale = jnp.exp(jax.random.uniform(keys[1], (1, 1, NY), jnp.float32, 0.0, math.log(10.0)))
    ramp = 1.0 + 2.0 * jnp.arange(NX, dtype=jnp.float32)[None, :, None] / NX
    base = jnp.clip(jax.random.normal(keys[2], (NZ, NX, NY), jnp.float32), -4.0, 4.0)
    return 0.02 * row_scale * column_scale * ramp * base


def level_of(stream_key, shape, pieces, least, top_value):
    gain = 1.0
    for axis_at, shards_of in pieces:
        heights = jax.random.uniform(jax.random.fold_in(jax.random.fold_in(stream_key, 6), axis_at), (shards_of,), jnp.float32, least / len(pieces), top_value / len(pieces))
        gain = gain * jnp.repeat(jnp.exp(heights), shape[axis_at] // shards_of).reshape((-1,) + (1,) * (len(shape) - 1 - axis_at))
    return gain


def setup_inputs(seed: int = 0) -> dict:
    arg_keys = jax.random.split(jax.random.key(seed), 8)
    return {
        "conductivity": jnp.clip(jnp.exp(math.log(5.0) - 3.218876 * jax.random.uniform(arg_keys[0], (NZ, NX, NY), jnp.float32) ** level_of(arg_keys[0], (NZ, NX, NY), ((1, 8), (2, 16)), -0.2, 0.2)), 0.2, 5.0),
        "storage": jnp.clip(jnp.exp(math.log(5.0) - 2.3025851 * jax.random.uniform(arg_keys[1], (NZ, NX, NY), jnp.float32) ** level_of(arg_keys[1], (NZ, NX, NY), ((1, 8), (2, 16)), -0.2, 0.2)), 0.5, 5.0),
        "recharge": draw_recharge(jax.random.fold_in(arg_keys[7], 71), 0),
        "block_ids": draw_block_ids(jax.random.fold_in(arg_keys[7], 71), 0),
        "neighbours": draw_neighbours(jax.random.fold_in(arg_keys[7], 71), 0),
        "concentration": jnp.clip(jnp.exp(math.log(3.0) - 3.4011974 * jax.random.uniform(arg_keys[5], (ACTIVE, CY), jnp.float32) ** level_of(arg_keys[5], (ACTIVE, CY), ((0, 128),), -0.2, 0.2)), 0.1, 3.0),
        "sorption": jnp.clip(jnp.exp(math.log(3.0) - 2.3025851 * jax.random.uniform(arg_keys[6], (ACTIVE, CY), jnp.float32) ** level_of(arg_keys[6], (ACTIVE, CY), ((0, 128),), -0.2, 0.2)), 0.3, 3.0),
    }


POROSITY = 0.35
BULK_DENSITY = 1.6
EXPONENT = 0.7
SOFTEN = 0.05
DISPERSION = 0.5
TIME_STEP = 0.1
ADVECT = 1.0
VERTICAL = 2.0

def harmonic(own, other):
    return 2.0 * own * other / (own + other) + jnp.where(other == 0.0, own, 0.0)

def shift_down(field):
    return jnp.concatenate([jnp.zeros_like(field[:1]), field[:-1]], 0)

def shift_up(field):
    return jnp.concatenate([field[1:], jnp.zeros_like(field[:1])], 0)

def pad_plane(field):
    return jnp.pad(field, ((0, 0), (1, 1), (1, 1)))

def face_terms(conductivity, padded):
    west = harmonic(conductivity, padded[:, :-2, 1:-1])
    east = harmonic(conductivity, padded[:, 2:, 1:-1])
    south = harmonic(conductivity, padded[:, 1:-1, :-2])
    north = harmonic(conductivity, padded[:, 1:-1, 2:])
    inner = VERTICAL * 2.0 * conductivity[:-1] * conductivity[1:] / (conductivity[:-1] + conductivity[1:])
    zeros = jnp.zeros_like(conductivity[:1])
    below = jnp.concatenate([zeros, inner], 0)
    above = jnp.concatenate([inner, zeros], 0)
    return (west, east, south, north, below, above)

def apply_operator(faces, diagonal, field, padded):
    west, east, south, north, below, above = faces
    beside = west * padded[:, :-2, 1:-1] + east * padded[:, 2:, 1:-1]
    beside = beside + south * padded[:, 1:-1, :-2] + north * padded[:, 1:-1, 2:]
    beside = beside + below * shift_down(field) + above * shift_up(field)
    return diagonal * field - beside

def face_fluxes(faces, head, padded):
    west, east, south, north, below, above = faces
    flux_west = west * (padded[:, :-2, 1:-1] - head)
    flux_east = east * (head - padded[:, 2:, 1:-1])
    flux_below = below * (shift_down(head) - head)
    flux_above = above * (head - shift_up(head))
    flux_south = south * (padded[:, 1:-1, :-2] - head)
    flux_north = north * (head - padded[:, 1:-1, 2:])
    return (jnp.stack([flux_west, flux_east, flux_below, flux_above, flux_south], 0), flux_north)

def minmod(first, second):
    return 0.5 * (jnp.sign(first) + jnp.sign(second)) * jnp.minimum(jnp.abs(first), jnp.abs(second))

def sorbed_mass(values, sorption):
    return POROSITY * values + BULK_DENSITY * sorption * jnp.power(values * values + SOFTEN * SOFTEN, 0.5 * EXPONENT)

def transport_step(solute, sorption, fluxes, north_end, lateral, ends):
    width = solute.shape[1]
    extended = jnp.concatenate([ends[0][:, None], ends[1][:, None], solute, ends[2][:, None], ends[3][:, None]], 1)
    face_flow = jnp.concatenate([fluxes[4], north_end[:, None]], 1)
    left = extended[:, 1:width + 2]
    right = extended[:, 2:width + 3]
    upwind_pos = left + 0.5 * minmod(right - left, left - extended[:, 0:width + 1])
    upwind_neg = right + 0.5 * minmod(left - right, right - extended[:, 3:width + 4])
    along = jnp.maximum(face_flow, 0.0) * upwind_pos + jnp.minimum(face_flow, 0.0) * upwind_neg
    advect = along[:, :-1] - along[:, 1:]
    advect = advect + jnp.maximum(fluxes[0], 0.0) * lateral[0] + jnp.minimum(fluxes[0], 0.0) * solute
    advect = advect - jnp.maximum(fluxes[1], 0.0) * solute - jnp.minimum(fluxes[1], 0.0) * lateral[1]
    advect = advect + jnp.maximum(fluxes[2], 0.0) * lateral[2] + jnp.minimum(fluxes[2], 0.0) * solute
    advect = advect - jnp.maximum(fluxes[3], 0.0) * solute - jnp.minimum(fluxes[3], 0.0) * lateral[3]
    coupling = TIME_STEP * DISPERSION
    source = sorbed_mass(solute, sorption) + ADVECT * advect
    source = source.at[:, 0].add(coupling * extended[:, 1]).at[:, -1].add(coupling * extended[:, width + 2])
    column = jnp.arange(width)
    lower_band = jnp.where(column[None, :] == 0, 0.0, -coupling) * jnp.ones_like(solute)
    upper_band = jnp.where(column[None, :] == width - 1, 0.0, -coupling) * jnp.ones_like(solute)
    iterate = solute
    for sweep in range(PICARD):
        retard = POROSITY + BULK_DENSITY * sorption * jnp.power(iterate * iterate + SOFTEN * SOFTEN, 0.5 * (EXPONENT - 1.0))
        target = retard * iterate - sorbed_mass(iterate, sorption) + source
        iterate = lax.linalg.tridiagonal_solve(lower_band, retard + 2.0 * coupling, upper_band, target[:, :, None])[:, :, 0]
    return iterate

def block_lines(stack):
    parts = stack.reshape(stack.shape[0], NZ, N_GX, CX, N_GY, CY)
    return parts.transpose(0, 2, 4, 1, 3, 5).reshape(stack.shape[0], -1, CY)

def neighbour_data(solute, neighbours):
    present = neighbours >= 0
    rows = jnp.where(present[:, :, None], solute[jnp.clip(neighbours, 0, solute.shape[0] - 1)], 0.0)
    lateral = jnp.stack([rows[:, 0], rows[:, 1], rows[:, 4], rows[:, 5]], 0)
    ends = jnp.stack([rows[:, 2, -2], rows[:, 2, -1], rows[:, 3, 0], rows[:, 3, 1]], 0)
    return (lateral, ends)

def reference(conductivity, storage, recharge, block_ids, neighbours, concentration, sorption):
    faces = face_terms(conductivity, pad_plane(conductivity))
    diagonal = storage + faces[0] + faces[1] + faces[2] + faces[3] + faces[4] + faces[5]
    head = jnp.zeros_like(recharge)
    residual = recharge
    scaled = residual / diagonal
    direction = scaled
    gamma = jnp.sum(residual * scaled)
    for sweep in range(ITERS):
        image = apply_operator(faces, diagonal, direction, pad_plane(direction))
        alpha = gamma / jnp.sum(direction * image)
        head = head + alpha * direction
        if sweep + 1 < ITERS:
            residual = residual - alpha * image
            scaled = residual / diagonal
            gamma_next = jnp.sum(residual * scaled)
            direction = scaled + gamma_next / gamma * direction
            gamma = gamma_next
    fluxes, flux_north = face_fluxes(faces, head, pad_plane(head))
    flux_lines = jnp.take(block_lines(fluxes), block_ids, axis=1)
    north_end = jnp.take(block_lines(flux_north[None])[0, :, -1], block_ids)
    solute = concentration
    for sweep in range(STEPS):
        lateral, ends = neighbour_data(solute, neighbours)
        solute = transport_step(solute, sorption, flux_lines, north_end, lateral, ends)
    return (head, solute)
```

```python
import functools

import jax
import jax.numpy as jnp
from jax import lax
from jax.experimental import pallas as pl
from jax.experimental.pallas import tpu as pltpu
from jax.sharding import PartitionSpec as P

PICARD = 3
POROSITY = 0.35
BULK_DENSITY = 1.6
EXPONENT = 0.7
SOFTEN = 0.05
DISPERSION = 0.5
TIME_STEP = 0.1
ADVECT = 1.0
VERTICAL = 2.0
COUPLING = TIME_STEP * DISPERSION

AXES = ("gx", "gy")
ROWS = 9
NONE = -5000
F32 = jnp.float32
BF16 = jnp.bfloat16


def params(mib):
    return pltpu.CompilerParams(vmem_limit_bytes=mib * 1024 * 1024)


def iota(shape, dim):
    return lax.broadcasted_iota(jnp.int32, shape, dim)


def roll(x, shift, axis):
    return pltpu.roll(x, shift % x.shape[axis] if isinstance(shift, int) else shift, axis)


def split(x):
    high = x.astype(BF16)
    rest = x - high.astype(F32)
    middle = rest.astype(BF16)
    low = (rest - middle.astype(F32)).astype(BF16)
    return high, middle, low


def pick(mask, parts):
    chosen = jnp.where(mask, 1.0, 0.0).astype(BF16)
    high, middle, low = (jnp.dot(chosen, part, preferred_element_type=F32) for part in parts)
    return (low + middle) + high


def rows_of(parts, start, stop):
    return tuple(part[start:stop] for part in parts)


def place():
    across = lax.axis_size("gy")
    return lax.axis_index("gx") * across + lax.axis_index("gy")


def edges_kernel(k_low, k_high, s_low, s_high, r_low, r_high, east_ref, west_ref):
    shape = k_low.shape[1:]
    sub = iota(shape, 0)
    for z in range(k_low.shape[0]):
        east_ref[z] = jnp.where(
            sub >= 5,
            k_high[z],
            jnp.where(sub >= 3, roll(s_high[z], -3, 0), roll(r_high[z], -5, 0)),
        )
        west_ref[z] = jnp.where(
            sub < 3, k_low[z], jnp.where(sub < 5, roll(s_low[z], 3, 0), roll(r_low[z], 5, 0))
        )


def pack_edges(conductivity, storage, recharge):
    layers, rows, width = conductivity.shape
    low = pl.BlockSpec((layers, 8, width), lambda i: (0, 0, 0))
    high = pl.BlockSpec((layers, 8, width), lambda i: (0, rows // 8 - 1, 0))
    tile = jax.ShapeDtypeStruct((layers, 8, width), F32)
    return pl.pallas_call(
        edges_kernel,
        grid=(1,),
        in_specs=[low, high] * 3,
        out_specs=[pl.BlockSpec((layers, 8, width), lambda i: (0, 0, 0))] * 2,
        out_shape=[tile, tile],
        name="pack_edges",
    )(conductivity, conductivity, storage, storage, recharge, recharge)


def widened(index, z, own_ref, west_ref, east_ref):
    shift = (0, 3, 5)[index]
    top, bottom = west_ref[z], east_ref[z]
    if shift:
        top, bottom = roll(top, shift, 0), roll(bottom, -shift, 0)
    return jnp.concatenate([top, own_ref[z], bottom], 0)


def strip_kernel(k_ref, s_ref, r_ref, west_ref, east_ref, out_ref):
    layers = k_ref.shape[0]
    for index, own in enumerate((k_ref, s_ref, r_ref)):
        strip = None
        for z in range(layers):
            wide = roll(widened(index, z, own, west_ref, east_ref), z * 8 + 4, 1)
            if strip is None:
                strip = wide
            else:
                strip = jnp.where(iota(wide.shape, 1) >= z * 8, wide, strip)
        out_ref[index] = strip


def pack_strip(conductivity, storage, recharge, west, east):
    layers, rows, width = conductivity.shape
    return pl.pallas_call(
        strip_kernel,
        out_shape=jax.ShapeDtypeStruct((3, rows + 16, width), F32),
        compiler_params=params(16),
        name="pack_strip",
    )(conductivity, storage, recharge, west, east)


def column(row):
    n = row.shape[1]
    return jnp.sum(jnp.where(iota((n, n), 0) == iota((n, n), 1), row, 0.0), 1, keepdims=True)


def as_row(col):
    n = col.shape[0]
    return jnp.sum(jnp.where(iota((n, n), 0) == iota((n, n), 1), col, 0.0), 0, keepdims=True)


def send_kernel(down, across, rows_x, layers, ids_ref, conc_ref, sorp_ref, out_ref, col_ref, row_ref):
    devices, owned = ids_ref.shape
    lines = layers * rows_x
    me = place()
    ids = ids_ref[...]
    brick = ids // lines
    key = iota(ids.shape, 1) * lines + ids % lines
    gx, gy = me // across, me % across
    cols, rows = [], []
    for target, ok, edge in (
        (me, None, None),
        (me - across, gx > 0, rows_x - 1),
        (me + across, gx < down - 1, 0),
        (me - 1, gy > 0, None),
        (me + 1, gy < across - 1, None),
    ):
        if ok is not None:
            target = jnp.where(ok, target, -1)
        mine = brick == target
        first = jnp.min(jnp.where(mine, key, owned * lines).astype(F32), 1, keepdims=True)
        second = jnp.max(jnp.where(mine, key, -1).astype(F32), 1, keepdims=True)
        for code in (first, second):
            line = code.astype(jnp.int32) % lines
            keep = second >= 0.0
            if edge is not None:
                keep = keep & (line % rows_x == edge)
                line = line // rows_x
            value = jnp.where(keep, line, NONE).astype(F32)
            cols.append(value)
            rows.append(as_row(value))
    lane = iota((devices, 128), 1)
    packed = jnp.zeros((devices, 128), F32)
    for at, value in enumerate(cols):
        packed = jnp.where(lane == at, value, packed)
    col_ref[...] = packed.astype(jnp.int32)
    row_ref[...] = jnp.concatenate(
        rows + [jnp.zeros((16 - len(rows), devices), F32)], 0
    ).astype(jnp.int32)
    own = ids_ref[pl.ds(me, 1), :]
    own_brick = own // lines
    own_row = own % lines % rows_x
    brick_col = column(own_brick.astype(F32)).astype(jnp.int32)
    square = (owned, owned)
    same = (brick_col == own_brick) & (iota(square, 0) < iota(square, 1))
    rank = jnp.sum(jnp.where(same, 1.0, 0.0), 0, keepdims=True).astype(jnp.int32)
    dest = iota((devices, owned), 0)
    conc = conc_ref[...]
    conc_parts = split(conc)
    sorp_parts = split(sorp_ref[...])
    lane = iota((owned, conc.shape[1]), 1)
    misc = jnp.zeros((devices, conc.shape[1]), F32)
    for k in range(2):
        ranked = rank == k
        home = (dest == own_brick) & ranked
        out_ref[pl.ds(k, devices, stride=ROWS), :] = pick(home, conc_parts)
        out_ref[pl.ds(2 + k, devices, stride=ROWS), :] = pick(home, sorp_parts)
        after = (dest == own_brick + across) & ranked & (own_row == rows_x - 1)
        out_ref[pl.ds(4 + k, devices, stride=ROWS), :] = pick(after, conc_parts)
        before = (dest == own_brick - across) & ranked & (own_row == 0)
        out_ref[pl.ds(6 + k, devices, stride=ROWS), :] = pick(before, conc_parts)
        tails = jnp.where(lane // 2 == k, roll(conc, 2 + 2 * k, 1), 0.0)
        heads = jnp.where(lane // 2 == 2 + k, roll(conc, 4 + 2 * k, 1), 0.0)
        north = (dest == own_brick + 1) & ranked & (own_brick % across < across - 1)
        south = (dest == own_brick - 1) & ranked & (own_brick % across > 0)
        misc = misc + pick(north, split(tails)) + pick(south, split(heads))
    out_ref[pl.ds(8, devices, stride=ROWS), :] = misc


def pack_send(ids, concentration, sorption, layers, rows_x):
    devices, owned = ids.shape
    width = concentration.shape[1]
    kernel = functools.partial(
        send_kernel, lax.axis_size("gx"), lax.axis_size("gy"), rows_x, layers
    )
    return pl.pallas_call(
        kernel,
        out_shape=[
            jax.ShapeDtypeStruct((devices * ROWS, width), F32),
            jax.ShapeDtypeStruct((devices, 128), jnp.int32),
            jax.ShapeDtypeStruct((16, devices), jnp.int32),
        ],
        compiler_params=params(16),
        name="pack_send",
    )(ids, concentration, sorption)


def harmonic(a, c):
    return jnp.where(jnp.minimum(a, c) > 0.0, 2.0 * a * c / (a + c), jnp.maximum(a, c))


def flow_kernel(
    k_ref, s_ref, r_ref, west_ref, east_ref, strip_ref, south_ref, north_ref, send_ref,
    d_out, w_out, x_out, send_out,
    kx, sx, fw, fs, fb, rd, dd, ww,
):
    layers, rows, width = k_ref.shape
    tall = rows + 16
    shape = (tall, width)
    lane = iota(shape, 1)
    slot = lane % 8
    devices = send_ref.shape[0] // ROWS

    send_out[...] = send_ref[...]

    def side(low):
        def joined(index):
            if low:
                return jnp.where(slot < 4, south_ref[index], strip_ref[index])
            return jnp.where(slot < 4, strip_ref[index], north_ref[index])

        k, s, r = joined(0), joined(1), joined(2)
        face_w = harmonic(k, roll(k, 1, 0))
        face_s = harmonic(k, roll(k, 1, 1))
        face_b = jnp.where(lane >= 8, VERTICAL * harmonic(k, roll(k, 8, 1)), 0.0)
        diagonal = (
            s + face_w + roll(face_w, -1, 0) + face_s + roll(face_s, -1, 1) + face_b + roll(face_b, -8, 1)
        )
        inverse = jnp.where(k > 0.0, 1.0 / diagonal, 0.0)
        d = r * inverse
        flux_w = face_w * (roll(d, 1, 0) - d)
        flux_s = face_s * (roll(d, 1, 1) - d)
        flux_b = face_b * (roll(d, 8, 1) - d)
        image = (
            s * d
            + (roll(flux_w, -1, 0) - flux_w)
            + (roll(flux_s, -1, 1) - flux_s)
            + (roll(flux_b, -8, 1) - flux_b)
        )
        w = image * inverse
        return face_s, flux_s, face_s * (roll(w, 1, 1) - w)

    low_face, low_d, low_w = side(True)
    high_face, high_d, high_w = side(False)

    def with_low(z, field, strip):
        return jnp.where(lane == 0, roll(strip, width - 4 - z * 8, 1), field)

    def north_of(z, field, strip):
        shift = lax.rem(width - 5 + width - z * 8, width)
        return jnp.where(lane == width - 1, roll(strip, shift, 1), roll(field, -1, 1))

    def widen(z, carry):
        kx[z] = widened(0, z, k_ref, west_ref, east_ref)
        return carry

    lax.fori_loop(0, layers, widen, 0)
    fb[0] = jnp.zeros(shape, F32)

    def faces(z, carry):
        k = kx[z]
        face_w = harmonic(k, roll(k, 1, 0))
        face_s = with_low(z, harmonic(k, roll(k, 1, 1)), low_face)
        face_n = north_of(z, face_s, high_face)
        upper = kx[jnp.minimum(z + 1, layers - 1)]
        face_a = jnp.where(z < layers - 1, VERTICAL * harmonic(k, upper), 0.0)
        s = widened(1, z, s_ref, west_ref, east_ref)
        r = widened(2, z, r_ref, west_ref, east_ref)
        diagonal = s + face_w + roll(face_w, -1, 0) + face_s + face_n + fb[z] + face_a
        inverse = jnp.where(k > 0.0, 1.0 / diagonal, 0.0)
        fw[z] = face_w
        fs[z] = face_s
        fb[z + 1] = face_a
        rd[z] = inverse
        dd[z] = r * inverse
        sx[z] = s
        return carry

    lax.fori_loop(0, layers, faces, 0)

    def total(x):
        return jnp.sum(x[8 : 8 + rows].reshape(rows // 8, 8, width), 0)

    def apply(z, field, low, high, block):
        h = field[z]
        below = field[jnp.maximum(z - 1, 0)]
        above = field[jnp.minimum(z + 1, layers - 1)]
        flux_w = fw[z] * (roll(h, 1, 0) - h)
        flux_e = roll(flux_w, -1, 0)
        flux_b = fb[z] * (below - h)
        flux_a = fb[z + 1] * (h - above)
        flux_s = with_low(z, fs[z] * (roll(h, 1, 1) - h), low)
        flux_n = north_of(z, flux_s, high)
        for at, flux in enumerate((flux_w, flux_e, flux_b, flux_a, flux_s, flux_n)):
            x_out[block + at, pl.ds(pl.multiple_of(z * rows, rows), rows), :] = flux[8 : 8 + rows]
        return h, sx[z] * h + (flux_e - flux_w) + (flux_a - flux_b) + (flux_n - flux_s)

    zero = jnp.zeros((8, width), F32)

    def first(z, sums):
        d, image = apply(z, dd, low_d, high_d, 0)
        w = image * rd[z]
        ww[z] = w
        d_out[z] = d[8 : 8 + rows]
        w_out[z] = w[8 : 8 + rows]
        r = r_ref[z]
        gamma = jnp.sum((r * d[8 : 8 + rows]).reshape(rows // 8, 8, width), 0)
        return sums[0] + gamma, sums[1] + total(d * image), sums[2] + total(image * w)

    gamma, bend, curve = lax.fori_loop(0, layers, first, (zero, zero, zero))

    def second(z, acc):
        w, image = apply(z, ww, low_w, high_w, 6)
        return acc + total(w * image)

    twist = lax.fori_loop(0, layers, second, zero)
    lane_row = iota((devices, width), 1)
    misc = send_ref[pl.ds(8, devices, stride=ROWS), :]
    for at, part in enumerate((gamma, bend, curve, twist)):
        value = jnp.sum(jnp.sum(part, 0, keepdims=True), 1, keepdims=True)
        misc = jnp.where(lane_row == 8 + at, value, misc)
    send_out[pl.ds(8, devices, stride=ROWS), :] = misc


def flow(conductivity, storage, recharge, west, east, strip, south, north, send):
    layers, rows, width = conductivity.shape
    tall = pltpu.VMEM((layers, rows + 16, width), F32)
    return pl.pallas_call(
        flow_kernel,
        out_shape=[
            jax.ShapeDtypeStruct(conductivity.shape, F32),
            jax.ShapeDtypeStruct(conductivity.shape, F32),
            jax.ShapeDtypeStruct((12, layers * rows, width), F32),
            jax.ShapeDtypeStruct(send.shape, F32),
        ],
        scratch_shapes=[tall] * 4
        + [pltpu.VMEM((layers + 1, rows + 16, width), F32)]
        + [tall] * 3,
        compiler_params=params(28),
        name="flow",
    )(conductivity, storage, recharge, west, east, strip, south, north, send)


def gather_kernel(x_ref, col_ref, out_ref):
    lines = x_ref.shape[1]
    cols = col_ref[...]
    own = jnp.concatenate([cols[:, 0:1], cols[:, 1:2]], 0)
    mask = own == iota((own.shape[0], lines), 1)
    chosen = jnp.where(mask, 1.0, 0.0).astype(BF16)
    for at in range(x_ref.shape[0]):
        parts = split(x_ref[at])
        high, middle, low = (jnp.dot(chosen, part, preferred_element_type=F32) for part in parts)
        out_ref[at] = (low + middle) + high


def gather_fluxes(fluxes, cols):
    count, lines, width = fluxes.shape
    return pl.pallas_call(
        gather_kernel,
        out_shape=jax.ShapeDtypeStruct((count, 2 * cols.shape[0], width), F32),
        compiler_params=params(28),
        name="gather_fluxes",
    )(fluxes, cols)


def minmod(a, d):
    return jnp.maximum(jnp.minimum(a, d), 0.0) + jnp.minimum(jnp.maximum(a, d), 0.0)


def tridiagonal(diagonal, right):
    width = diagonal.shape[1]
    side = jnp.where(iota(diagonal.shape, 1) == 0, 0.0, -COUPLING)
    step = 1
    while step < width:
        inverse = 1.0 / diagonal
        scaled = side * inverse
        value = right * inverse
        before = roll(inverse, step, 1)
        right = right - side * roll(value, step, 1) - roll(side * value, -step, 1)
        diagonal = diagonal - side * (side * before) - roll(side * scaled, -step, 1)
        side = -side * roll(scaled, step, 1)
        step *= 2
    return right / diagonal


def transport(c, sorption, fluxes, west, east, lower, upper, ends):
    lane = iota(c.shape, 1)
    width = c.shape[1]
    last = lane == width - 1
    south_one = roll(ends, -1, 1)
    north_one = roll(ends, width - 5, 1)
    back = jnp.where(lane == 0, south_one, roll(c, 1, 1))
    back2 = jnp.where(lane < 2, ends, roll(c, 2, 1))
    ahead = jnp.where(last, north_one, roll(c, -1, 1))
    ahead2 = jnp.where(lane >= width - 2, roll(ends, width - 6, 1), roll(c, -2, 1))
    q_w, q_e, q_b, q_a, q_s, q_n = fluxes

    def face(q, far_left, left, right, far_right):
        rise = right - left
        positive = left + 0.5 * minmod(rise, left - far_left)
        negative = right + 0.5 * minmod(-rise, right - far_right)
        return jnp.maximum(q, 0.0) * positive + jnp.minimum(q, 0.0) * negative

    along = face(q_s, back2, back, c, ahead)
    beyond = face(q_n, back, c, ahead, ahead2)
    advect = along - jnp.where(last, beyond, roll(along, -1, 1))
    advect = advect + jnp.maximum(q_w, 0.0) * west + jnp.minimum(q_w, 0.0) * c
    advect = advect - jnp.maximum(q_e, 0.0) * c - jnp.minimum(q_e, 0.0) * east
    advect = advect + jnp.maximum(q_b, 0.0) * lower + jnp.minimum(q_b, 0.0) * c
    advect = advect - jnp.maximum(q_a, 0.0) * c - jnp.minimum(q_a, 0.0) * upper
    advect = ADVECT * advect
    advect = advect + COUPLING * (
        jnp.where(lane == 0, south_one, 0.0) + jnp.where(last, north_one, 0.0)
    )
    weight = BULK_DENSITY * sorption
    v = c
    source = None
    for sweep in range(PICARD):
        square = v * v + SOFTEN * SOFTEN
        power = weight * jnp.exp((0.5 * (EXPONENT - 1.0)) * jnp.log(square))
        retard = POROSITY + power
        root = jnp.sqrt(square)
        if sweep == 0:
            source = POROSITY * c + power * root + advect
            target = retard * c + advect
        else:
            target = power * (v - root) + source
        v = tridiagonal(retard + 2.0 * COUPLING, target)
    return v


def neighbour_values(c, cols, rows, west_edge, east_edge, south_misc, north_misc, rows_x):
    own_c = jnp.concatenate([cols[:, 0:1], cols[:, 1:2]], 0)
    own_r = jnp.concatenate([rows[0:1], rows[1:2]], 1)
    layers = west_edge.shape[0]
    active = own_c >= 0
    row_c = own_c % rows_x
    layer_c = own_c // rows_x
    first = active & (row_c == 0)
    final = active & (row_c == rows_x - 1)
    at_layer = iota((own_c.shape[0], layers), 1) == layer_c
    parts = split(c)
    west = pick((own_r == own_c - 1) & (row_c != 0), parts) + pick(
        at_layer & first, split(west_edge)
    )
    east = pick((own_r == own_c + 1) & (row_c != rows_x - 1), parts) + pick(
        at_layer & final, split(east_edge)
    )
    lower = pick(own_r == own_c - rows_x, parts)
    upper = pick(own_r == own_c + rows_x, parts)
    lane = iota(south_misc.shape, 1)
    ends = None
    for k in range(2):
        tails = split(jnp.where(lane // 2 == k, south_misc, 0.0))
        heads = split(jnp.where(lane // 2 == 2 + k, north_misc, 0.0))
        part = pick((rows[6 + k : 7 + k] == own_c) & active, tails)
        part = part + pick((rows[8 + k : 9 + k] == own_c) & active, heads)
        ends = part if ends is None else ends + part
    return west, east, lower, upper, ends + roll(ends, -2, 1)


def first_kernel(
    rows_x, recv_ref, gath_ref, col_ref, row_ref, c_out, s_out, flux_out, east_out, west_out, misc_out, scal_out
):
    devices = recv_ref.shape[0] // ROWS
    width = recv_ref.shape[1]

    def received(at):
        return recv_ref[pl.ds(at, devices, stride=ROWS), :]

    cols, rows = col_ref[...], row_ref[...]
    layers = east_out.shape[0]
    misc = received(8)
    sums = jnp.sum(misc, 0, keepdims=True)
    at = iota(sums.shape, 1)
    gamma, bend, curve, twist = (
        jnp.sum(jnp.where(at == 8 + i, sums, 0.0), 1, keepdims=True) for i in range(4)
    )
    alpha = gamma / bend
    gamma_next = alpha * alpha * curve - gamma
    beta = gamma_next / gamma
    cross = bend - alpha * curve
    bend_next = bend - 2.0 * alpha * curve + alpha * alpha * twist + 2.0 * beta * cross + beta * beta * bend
    alpha_next = gamma_next / bend_next
    on_d = alpha + alpha_next * (1.0 + beta)
    on_w = -alpha * alpha_next
    lane8 = iota((8, width), 1)
    scal_out[...] = jnp.where(lane8 == 0, on_d, on_w)

    c = jnp.concatenate([received(0), received(1)], 0)
    s = jnp.concatenate([received(2), received(3)], 0)
    layer = iota((layers, 2 * devices), 0)
    west_codes = jnp.concatenate([rows[2:3], rows[3:4]], 1)
    east_codes = jnp.concatenate([rows[4:5], rows[5:6]], 1)
    west_edge = pick(layer == west_codes, split(jnp.concatenate([received(4), received(5)], 0)))
    east_edge = pick(layer == east_codes, split(jnp.concatenate([received(6), received(7)], 0)))
    fluxes = []
    for i in range(6):
        flux = on_d * gath_ref[i] + on_w * gath_ref[6 + i]
        flux_out[i] = flux
        fluxes.append(flux)
    beside = neighbour_values(c, cols, rows, west_edge, east_edge, misc, misc, rows_x)
    c = transport(c, s, fluxes, *beside)
    c_out[...] = c
    s_out[...] = s
    own_r = jnp.concatenate([rows[0:1], rows[1:2]], 1)
    here = (own_r // rows_x == layer) & (own_r >= 0)
    parts = split(c)
    east_out[...] = pick(here & (own_r % rows_x == rows_x - 1), parts)
    west_out[...] = pick(here & (own_r % rows_x == 0), parts)
    lane = iota((devices, width), 1)
    c0, c1 = c[:devices], c[devices:]
    misc_out[...] = jnp.where(
        lane < 2,
        roll(c0, 2, 1),
        jnp.where(lane < 4, roll(c1, 4, 1), jnp.where(lane < 6, roll(c0, 4, 1), roll(c1, 6, 1))),
    )


def first_step(received, gathered, cols, rows, layers, rows_x):
    width = received.shape[1]
    devices = cols.shape[0]
    lines = jax.ShapeDtypeStruct((2 * devices, width), F32)
    edge = jax.ShapeDtypeStruct((layers, width), F32)
    return pl.pallas_call(
        functools.partial(first_kernel, rows_x),
        out_shape=[
            lines,
            lines,
            jax.ShapeDtypeStruct((6, 2 * devices, width), F32),
            edge,
            edge,
            jax.ShapeDtypeStruct((devices, width), F32),
            jax.ShapeDtypeStruct((8, width), F32),
        ],
        compiler_params=params(16),
        name="first_step",
    )(received, gathered, cols, rows)


def second_kernel(
    rows_x, c_ref, s_ref, flux_ref, col_ref, row_ref, west_ref, east_ref, south_ref, north_ref, out_ref
):
    c, s = c_ref[...], s_ref[...]
    devices = c.shape[0] // 2
    beside = neighbour_values(
        c, col_ref[...], row_ref[...], west_ref[...], east_ref[...], south_ref[...], north_ref[...], rows_x
    )
    c = transport(c, s, [flux_ref[i] for i in range(6)], *beside)
    for k in range(2):
        out_ref[pl.ds(k, devices, stride=2), :] = c[k * devices : (k + 1) * devices]


def second_step(c, s, fluxes, cols, rows, west, east, south, north, rows_x):
    return pl.pallas_call(
        functools.partial(second_kernel, rows_x),
        out_shape=jax.ShapeDtypeStruct(c.shape, F32),
        compiler_params=params(16),
        name="second_step",
    )(c, s, fluxes, cols, rows, west, east, south, north)


def owner_kernel(lines, ids_ref, recv_ref, out_ref):
    devices, owned = ids_ref.shape
    own = ids_ref[pl.ds(place(), 1), :]
    brick = own // lines
    brick_col = column(brick.astype(F32)).astype(jnp.int32)
    square = (owned, owned)
    same = (brick_col == brick) & (iota(square, 1) < iota(square, 0))
    rank = jnp.sum(jnp.where(same, 1.0, 0.0), 1, keepdims=True).astype(jnp.int32)
    mask = brick_col * 2 + rank == iota((owned, 2 * devices), 1)
    out_ref[...] = pick(mask, split(recv_ref[...]))


def to_owner(ids, received, lines):
    return pl.pallas_call(
        functools.partial(owner_kernel, lines),
        out_shape=jax.ShapeDtypeStruct((ids.shape[1], received.shape[1]), F32),
        compiler_params=params(16),
        name="to_owner",
    )(ids, received)


def exchange(low_side, high_side, axis):
    count = lax.axis_size(axis)
    forward = [(i, i + 1) for i in range(count - 1)]
    backward = [(i + 1, i) for i in range(count - 1)]
    return lax.ppermute(high_side, axis, forward), lax.ppermute(low_side, axis, backward)


def body(conductivity, storage, recharge, block_ids, neighbours, concentration, sorption):
    layers, rows_x, width = conductivity.shape
    devices = lax.axis_size(AXES)
    owned = concentration.shape[0]
    ids = block_ids.reshape(devices, owned)
    to_east, to_west = pack_edges(conductivity, storage, recharge)
    west, east = exchange(to_west, to_east, "gx")
    send, cols, rows = pack_send(ids, concentration, sorption, layers, rows_x)
    strip = pack_strip(conductivity, storage, recharge, west, east)
    south, north = exchange(strip, strip, "gy")
    base, image, fluxes, send = flow(
        conductivity, storage, recharge, west, east, strip, south, north, send
    )
    received = lax.all_to_all(
        send.reshape(devices, 1, ROWS * width), AXES, split_axis=0, concat_axis=0, tiled=True
    ).reshape(devices * ROWS, width)
    gathered = gather_fluxes(fluxes, cols)
    c, s, flux, to_east, to_west, misc, scal = first_step(
        received, gathered, cols, rows, layers, rows_x
    )
    west, east = exchange(to_west, to_east, "gx")
    south, north = exchange(misc, misc, "gy")
    head = scal[0, 0] * base + scal[0, 1] * image
    result = second_step(c, s, flux, cols, rows, west, east, south, north, rows_x)
    returned = lax.all_to_all(
        result.reshape(devices, 2, width), AXES, split_axis=0, concat_axis=0, tiled=True
    ).reshape(devices * 2, width)
    return head, to_owner(ids, returned, layers * rows_x)


def solution(mesh):
    return jax.shard_map(
        body,
        mesh=mesh,
        in_specs=(
            P(None, "gx", "gy"),
            P(None, "gx", "gy"),
            P(None, "gx", "gy"),
            P(),
            P(("gx", "gy"), None),
            P(("gx", "gy"), None),
            P(("gx", "gy"), None),
        ),
        out_specs=(P(None, "gx", "gy"), P(("gx", "gy"), None)),
        check_vma=False,
    )
```

```python
import functools

import jax
import jax.numpy as jnp
from jax import lax
from jax.experimental import pallas as pl
from jax.experimental.pallas import tpu as pltpu
from jax.sharding import PartitionSpec as P

PICARD = 3
POROSITY = 0.35
BULK_DENSITY = 1.6
EXPONENT = 0.7
SOFTEN = 0.05
DISPERSION = 0.5
TIME_STEP = 0.1
ADVECT = 1.0
VERTICAL = 2.0
COUPLING = TIME_STEP * DISPERSION

AXES = ("gx", "gy")
ROWS = 9
NONE = -5000
F32 = jnp.float32
BF16 = jnp.bfloat16


def params(mib):
    return pltpu.CompilerParams(vmem_limit_bytes=int(mib * 1024 * 1024))


def iota(shape, dim):
    return lax.broadcasted_iota(jnp.int32, shape, dim)


def roll(x, shift, axis):
    return pltpu.roll(x, shift % x.shape[axis] if isinstance(shift, int) else shift, axis)


def split(x):
    high = x.astype(BF16)
    rest = x - high.astype(F32)
    middle = rest.astype(BF16)
    low = (rest - middle.astype(F32)).astype(BF16)
    return high, middle, low


def pick(mask, parts):
    chosen = jnp.where(mask, 1.0, 0.0).astype(BF16)
    high, middle, low = (jnp.dot(chosen, part, preferred_element_type=F32) for part in parts)
    return (low + middle) + high


def rows_of(parts, start, stop):
    return tuple(part[start:stop] for part in parts)


def place():
    across = lax.axis_size("gy")
    return lax.axis_index("gx") * across + lax.axis_index("gy")


HBM = pl.BlockSpec(memory_space=pltpu.HBM)
SMEM = pl.BlockSpec(memory_space=pltpu.SMEM)
VMEM = pl.BlockSpec(memory_space=pltpu.VMEM)


def fetch(pairs, sems):
    copies = [pltpu.make_async_copy(src, dst, sems.at[i]) for i, (src, dst) in enumerate(pairs)]
    for copy in copies:
        copy.start()
    return copies


def load_kernel(
    k_hbm, s_hbm, r_hbm, ids_hbm, conc_hbm, sorp_hbm,
    east_ref, west_ref, k_ref, s_ref, r_ref, ids_ref, conc_ref, sorp_ref, sems,
):
    copies = fetch(
        [
            (k_hbm, k_ref),
            (s_hbm, s_ref),
            (r_hbm, r_ref),
            (ids_hbm, ids_ref),
            (conc_hbm, conc_ref),
            (sorp_hbm, sorp_ref),
        ],
        sems,
    )
    for copy in copies:
        copy.wait()
    high = k_ref.shape[1] - 8
    sub = iota(east_ref.shape[1:], 0)
    for z in range(east_ref.shape[0]):
        east_ref[z] = jnp.where(
            sub >= 5,
            k_ref[z, high:],
            jnp.where(sub >= 3, roll(s_ref[z, high:], -3, 0), roll(r_ref[z, high:], -5, 0)),
        )
        west_ref[z] = jnp.where(
            sub < 3,
            k_ref[z, :8],
            jnp.where(sub < 5, roll(s_ref[z, :8], 3, 0), roll(r_ref[z, :8], 5, 0)),
        )


def load(*arrays):
    layers, rows, width = arrays[0].shape
    tile = jax.ShapeDtypeStruct((layers, 8, width), F32)
    return pl.pallas_call(
        load_kernel,
        in_specs=[HBM] * 6,
        out_specs=[VMEM] * 8,
        out_shape=[tile, tile] + [jax.ShapeDtypeStruct(x.shape, x.dtype) for x in arrays],
        scratch_shapes=[pltpu.SemaphoreType.DMA((6,))],
        compiler_params=params(8),
        name="load",
    )(*(pltpu.with_memory_space_constraint(x, pltpu.HBM) for x in arrays))


def beside(index, z, west_ref, east_ref):
    shift = (0, 3, 5)[index]
    top, bottom = west_ref[z], east_ref[z]
    if shift:
        top, bottom = roll(top, shift, 0), roll(bottom, -shift, 0)
    return top, bottom


def widened(index, z, own_ref, west_ref, east_ref):
    top, bottom = beside(index, z, west_ref, east_ref)
    return jnp.concatenate([top, own_ref[z], bottom], 0)


def strip_of(layers, layer):
    strip = None
    for z in range(layers):
        turned = roll(layer(z), z * 8 + 4, 1)
        strip = turned if strip is None else jnp.where(iota(turned.shape, 1) >= z * 8, turned, strip)
    return strip


def strip_kernel(inner_ref, west_ref, east_ref, out_ref):
    layers = west_ref.shape[0]
    rows = inner_ref.shape[1]
    for index in range(3):
        out_ref[index, 8 : 8 + rows] = inner_ref[index]
        out_ref[index, 0:8] = strip_of(layers, lambda z: beside(index, z, west_ref, east_ref)[0])
        out_ref[index, 8 + rows :] = strip_of(layers, lambda z: beside(index, z, west_ref, east_ref)[1])


def pack_strip(inner, west, east):
    rows, width = inner.shape[1:]
    return pl.pallas_call(
        strip_kernel,
        out_shape=jax.ShapeDtypeStruct((3, rows + 16, width), F32),
        compiler_params=params(4),
        name="pack_strip",
    )(inner, west, east)


def column(row):
    n = row.shape[1]
    return jnp.sum(jnp.where(iota((n, n), 0) == iota((n, n), 1), row, 0.0), 1, keepdims=True)


def as_row(col):
    n = col.shape[0]
    return jnp.sum(jnp.where(iota((n, n), 0) == iota((n, n), 1), col, 0.0), 0, keepdims=True)


def prepare_kernel(
    down, across, k_ref, s_ref, r_ref, ids_ref, conc_ref, sorp_ref, inner_ref, out_ref, col_ref, row_ref
):
    layers, rows_x = k_ref.shape[:2]
    devices, owned = ids_ref.shape
    lines = layers * rows_x
    me = place()
    ids = ids_ref[...]
    brick = ids // lines
    key = iota(ids.shape, 1) * lines + ids % lines
    gx, gy = me // across, me % across
    cols, rows = [], []
    for target, ok, edge in (
        (me, None, None),
        (me - across, gx > 0, rows_x - 1),
        (me + across, gx < down - 1, 0),
        (me - 1, gy > 0, None),
        (me + 1, gy < across - 1, None),
    ):
        if ok is not None:
            target = jnp.where(ok, target, -1)
        mine = brick == target
        first = jnp.min(jnp.where(mine, key, owned * lines).astype(F32), 1, keepdims=True)
        second = jnp.max(jnp.where(mine, key, -1).astype(F32), 1, keepdims=True)
        for code in (first, second):
            line = code.astype(jnp.int32) % lines
            keep = second >= 0.0
            if edge is not None:
                keep = keep & (line % rows_x == edge)
                line = line // rows_x
            value = jnp.where(keep, line, NONE).astype(F32)
            cols.append(value)
            rows.append(as_row(value))
    lane = iota((devices, 128), 1)
    packed = jnp.zeros((devices, 128), F32)
    for at, value in enumerate(cols):
        packed = jnp.where(lane == at, value, packed)
    col_ref[...] = packed.astype(jnp.int32)
    row_ref[...] = jnp.concatenate(
        rows + [jnp.zeros((16 - len(rows), devices), F32)], 0
    ).astype(jnp.int32)
    own = ids_ref[pl.ds(me, 1), :]
    own_brick = own // lines
    own_row = own % lines % rows_x
    brick_col = column(own_brick.astype(F32)).astype(jnp.int32)
    square = (owned, owned)
    same = (brick_col == own_brick) & (iota(square, 0) < iota(square, 1))
    rank = jnp.sum(jnp.where(same, 1.0, 0.0), 0, keepdims=True).astype(jnp.int32)
    dest = iota((devices, owned), 0)
    conc = conc_ref[...]
    conc_parts = split(conc)
    sorp_parts = split(sorp_ref[...])
    lane = iota((owned, conc.shape[1]), 1)
    misc = jnp.zeros((devices, conc.shape[1]), F32)
    for k in range(2):
        ranked = rank == k
        home = (dest == own_brick) & ranked
        out_ref[pl.ds(k, devices, stride=ROWS), :] = pick(home, conc_parts)
        out_ref[pl.ds(2 + k, devices, stride=ROWS), :] = pick(home, sorp_parts)
        after = (dest == own_brick + across) & ranked & (own_row == rows_x - 1)
        out_ref[pl.ds(4 + k, devices, stride=ROWS), :] = pick(after, conc_parts)
        before = (dest == own_brick - across) & ranked & (own_row == 0)
        out_ref[pl.ds(6 + k, devices, stride=ROWS), :] = pick(before, conc_parts)
        tails = jnp.where(lane // 2 == k, roll(conc, 2 + 2 * k, 1), 0.0)
        heads = jnp.where(lane // 2 == 2 + k, roll(conc, 4 + 2 * k, 1), 0.0)
        north = (dest == own_brick + 1) & ranked & (own_brick % across < across - 1)
        south = (dest == own_brick - 1) & ranked & (own_brick % across > 0)
        misc = misc + pick(north, split(tails)) + pick(south, split(heads))
    out_ref[pl.ds(8, devices, stride=ROWS), :] = misc
    for index, ref in enumerate((k_ref, s_ref, r_ref)):
        inner_ref[index] = strip_of(layers, lambda z: ref[z])


def prepare(conductivity, storage, recharge, ids, concentration, sorption):
    devices, owned = ids.shape
    layers, rows_x, width = conductivity.shape
    kernel = functools.partial(prepare_kernel, lax.axis_size("gx"), lax.axis_size("gy"))
    return pl.pallas_call(
        kernel,
        out_shape=[
            jax.ShapeDtypeStruct((3, rows_x, width), F32),
            jax.ShapeDtypeStruct((devices * ROWS, width), F32),
            jax.ShapeDtypeStruct((devices, 128), jnp.int32),
            jax.ShapeDtypeStruct((16, devices), jnp.int32),
        ],
        compiler_params=params(8),
        name="prepare",
    )(conductivity, storage, recharge, ids, concentration, sorption)


def harmonic(a, c):
    return jnp.where(jnp.minimum(a, c) > 0.0, 2.0 * a * c / (a + c), jnp.maximum(a, c))


def flow_kernel(
    k_ref, s_ref, r_ref, west_ref, east_ref, strip_ref, south_ref, north_ref, send_ref, slots_ref,
    d_out, w_out, gath_out, send_out,
    kx, sx, fw, fs, fb, rd, dd, ww, lines_ref,
):
    layers, rows, width = k_ref.shape
    tall = rows + 16
    shape = (tall, width)
    lane = iota(shape, 1)
    slot = lane % 8
    devices = send_ref.shape[0] // ROWS

    send_out[...] = send_ref[...]

    def side(low):
        def joined(index):
            if low:
                return jnp.where(slot < 4, south_ref[index], strip_ref[index])
            return jnp.where(slot < 4, strip_ref[index], north_ref[index])

        k, s, r = joined(0), joined(1), joined(2)
        face_w = harmonic(k, roll(k, 1, 0))
        face_s = harmonic(k, roll(k, 1, 1))
        face_b = jnp.where(lane >= 8, VERTICAL * harmonic(k, roll(k, 8, 1)), 0.0)
        diagonal = (
            s + face_w + roll(face_w, -1, 0) + face_s + roll(face_s, -1, 1) + face_b + roll(face_b, -8, 1)
        )
        inverse = jnp.where(k > 0.0, 1.0 / diagonal, 0.0)
        d = r * inverse
        flux_w = face_w * (roll(d, 1, 0) - d)
        flux_s = face_s * (roll(d, 1, 1) - d)
        flux_b = face_b * (roll(d, 8, 1) - d)
        image = (
            s * d
            + (roll(flux_w, -1, 0) - flux_w)
            + (roll(flux_s, -1, 1) - flux_s)
            + (roll(flux_b, -8, 1) - flux_b)
        )
        w = image * inverse
        return face_s, flux_s, face_s * (roll(w, 1, 1) - w)

    low_face, low_d, low_w = side(True)
    high_face, high_d, high_w = side(False)

    def with_low(z, field, strip):
        return jnp.where(lane == 0, roll(strip, width - 4 - z * 8, 1), field)

    def north_of(z, field, strip):
        shift = lax.rem(width - 5 + width - z * 8, width)
        return jnp.where(lane == width - 1, roll(strip, shift, 1), roll(field, -1, 1))

    def widen(z, carry):
        kx[z] = widened(0, z, k_ref, west_ref, east_ref)
        return carry

    lax.fori_loop(0, layers, widen, 0, unroll=4)
    fb[0] = jnp.zeros(shape, F32)

    def faces(z, carry):
        k = kx[z]
        face_w = harmonic(k, roll(k, 1, 0))
        face_s = with_low(z, harmonic(k, roll(k, 1, 1)), low_face)
        face_n = north_of(z, face_s, high_face)
        upper = kx[jnp.minimum(z + 1, layers - 1)]
        face_a = jnp.where(z < layers - 1, VERTICAL * harmonic(k, upper), 0.0)
        s = widened(1, z, s_ref, west_ref, east_ref)
        r = widened(2, z, r_ref, west_ref, east_ref)
        diagonal = s + face_w + roll(face_w, -1, 0) + face_s + face_n + fb[z] + face_a
        inverse = jnp.where(k > 0.0, 1.0 / diagonal, 0.0)
        fw[z] = face_w
        fs[z] = face_s
        fb[z + 1] = face_a
        rd[z] = inverse
        dd[z] = r * inverse
        sx[z] = s
        return carry

    lax.fori_loop(0, layers, faces, 0, unroll=2)

    def total(x):
        return jnp.sum(x[8 : 8 + rows].reshape(rows // 8, 8, width), 0)

    def apply(z, field, low, high, block):
        h = field[z]
        below = field[jnp.maximum(z - 1, 0)]
        above = field[jnp.minimum(z + 1, layers - 1)]
        flux_w = fw[z] * (roll(h, 1, 0) - h)
        flux_e = roll(flux_w, -1, 0)
        flux_b = fb[z] * (below - h)
        flux_a = fb[z + 1] * (h - above)
        flux_s = with_low(z, fs[z] * (roll(h, 1, 1) - h), low)
        flux_n = north_of(z, flux_s, high)
        for at, flux in enumerate((flux_w, flux_e, flux_b, flux_a, flux_s, flux_n)):
            start = z * (rows * 16) + (block + at)
            lines_ref[pl.ds(start, rows, stride=16), :] = flux[8 : 8 + rows]
        return h, sx[z] * h + (flux_e - flux_w) + (flux_a - flux_b) + (flux_n - flux_s)

    zero = jnp.zeros((8, width), F32)

    def first(z, sums):
        d, image = apply(z, dd, low_d, high_d, 0)
        w = image * rd[z]
        ww[z] = w
        d_out[z] = d[8 : 8 + rows]
        w_out[z] = w[8 : 8 + rows]
        r = r_ref[z]
        gamma = jnp.sum((r * d[8 : 8 + rows]).reshape(rows // 8, 8, width), 0)
        return sums[0] + gamma, sums[1] + total(d * image), sums[2] + total(image * w)

    gamma, bend, curve = lax.fori_loop(0, layers, first, (zero, zero, zero), unroll=2)

    def second(z, acc):
        w, image = apply(z, ww, low_w, high_w, 6)
        return acc + total(w * image)

    twist = lax.fori_loop(0, layers, second, zero, unroll=2)
    lane_row = iota((devices, width), 1)
    misc = send_ref[pl.ds(8, devices, stride=ROWS), :]
    for at, part in enumerate((gamma, bend, curve, twist)):
        value = jnp.sum(jnp.sum(part, 0, keepdims=True), 1, keepdims=True)
        misc = jnp.where(lane_row == 8 + at, value, misc)
    send_out[pl.ds(8, devices, stride=ROWS), :] = misc
    for k in range(2):

        def gather(i, carry):
            line = pl.multiple_of(jnp.maximum(slots_ref[k, i], 0) * 16, 16)
            slot = pl.multiple_of((k * devices + i) * 16, 16)
            gath_out[pl.ds(slot, 16), :] = lines_ref[pl.ds(line, 16), :]
            return carry

        lax.fori_loop(0, devices, gather, 0, unroll=8)


def flow(conductivity, storage, recharge, west, east, strip, south, north, send, slots):
    layers, rows, width = conductivity.shape
    tall = pltpu.VMEM((layers, rows + 16, width), F32)
    return pl.pallas_call(
        flow_kernel,
        out_shape=[
            jax.ShapeDtypeStruct(conductivity.shape, F32),
            jax.ShapeDtypeStruct(conductivity.shape, F32),
            jax.ShapeDtypeStruct((2 * slots.shape[1] * 16, width), F32),
            jax.ShapeDtypeStruct(send.shape, F32),
        ],
        in_specs=[VMEM] * 9 + [SMEM],
        out_specs=[VMEM] * 4,
        scratch_shapes=[tall] * 4
        + [pltpu.VMEM((layers + 1, rows + 16, width), F32)]
        + [tall] * 3
        + [pltpu.VMEM((layers * rows * 16, width), F32)],
        compiler_params=params(30),
        name="flow",
    )(conductivity, storage, recharge, west, east, strip, south, north, send, slots)


def minmod(a, d):
    return jnp.maximum(jnp.minimum(a, d), 0.0) + jnp.minimum(jnp.maximum(a, d), 0.0)


def tridiagonal(diagonal, right):
    width = diagonal.shape[1]
    side = jnp.where(iota(diagonal.shape, 1) == 0, 0.0, -COUPLING)
    step = 1
    while step < width:
        inverse = 1.0 / diagonal
        scaled = side * inverse
        value = right * inverse
        before = roll(inverse, step, 1)
        right = right - side * roll(value, step, 1) - roll(side * value, -step, 1)
        diagonal = diagonal - side * (side * before) - roll(side * scaled, -step, 1)
        side = -side * roll(scaled, step, 1)
        step *= 2
    return right / diagonal


def transport(c, sorption, fluxes, west, east, lower, upper, ends):
    lane = iota(c.shape, 1)
    width = c.shape[1]
    last = lane == width - 1
    south_one = roll(ends, -1, 1)
    north_one = roll(ends, width - 5, 1)
    back = jnp.where(lane == 0, south_one, roll(c, 1, 1))
    back2 = jnp.where(lane < 2, ends, roll(c, 2, 1))
    ahead = jnp.where(last, north_one, roll(c, -1, 1))
    ahead2 = jnp.where(lane >= width - 2, roll(ends, width - 6, 1), roll(c, -2, 1))
    q_w, q_e, q_b, q_a, q_s, q_n = fluxes

    def face(q, far_left, left, right, far_right):
        rise = right - left
        positive = left + 0.5 * minmod(rise, left - far_left)
        negative = right + 0.5 * minmod(-rise, right - far_right)
        return jnp.maximum(q, 0.0) * positive + jnp.minimum(q, 0.0) * negative

    along = face(q_s, back2, back, c, ahead)
    beyond = face(q_n, back, c, ahead, ahead2)
    advect = along - jnp.where(last, beyond, roll(along, -1, 1))
    advect = advect + jnp.maximum(q_w, 0.0) * west + jnp.minimum(q_w, 0.0) * c
    advect = advect - jnp.maximum(q_e, 0.0) * c - jnp.minimum(q_e, 0.0) * east
    advect = advect + jnp.maximum(q_b, 0.0) * lower + jnp.minimum(q_b, 0.0) * c
    advect = advect - jnp.maximum(q_a, 0.0) * c - jnp.minimum(q_a, 0.0) * upper
    advect = ADVECT * advect
    advect = advect + COUPLING * (
        jnp.where(lane == 0, south_one, 0.0) + jnp.where(last, north_one, 0.0)
    )
    weight = BULK_DENSITY * sorption
    v = c
    source = None
    for sweep in range(PICARD):
        square = v * v + SOFTEN * SOFTEN
        power = weight * jnp.exp((0.5 * (EXPONENT - 1.0)) * jnp.log(square))
        retard = POROSITY + power
        root = jnp.sqrt(square)
        if sweep == 0:
            source = POROSITY * c + power * root + advect
            target = retard * c + advect
        else:
            target = power * (v - root) + source
        v = tridiagonal(retard + 2.0 * COUPLING, target)
    return v


def neighbour_values(c, cols, rows, west_edge, east_edge, south_misc, north_misc, rows_x):
    own_c = jnp.concatenate([cols[:, 0:1], cols[:, 1:2]], 0)
    own_r = jnp.concatenate([rows[0:1], rows[1:2]], 1)
    layers = west_edge.shape[0]
    active = own_c >= 0
    row_c = own_c % rows_x
    layer_c = own_c // rows_x
    first = active & (row_c == 0)
    final = active & (row_c == rows_x - 1)
    at_layer = iota((own_c.shape[0], layers), 1) == layer_c
    parts = split(c)
    west = pick((own_r == own_c - 1) & (row_c != 0), parts) + pick(
        at_layer & first, split(west_edge)
    )
    east = pick((own_r == own_c + 1) & (row_c != rows_x - 1), parts) + pick(
        at_layer & final, split(east_edge)
    )
    lower = pick(own_r == own_c - rows_x, parts)
    upper = pick(own_r == own_c + rows_x, parts)
    lane = iota(south_misc.shape, 1)
    ends = None
    for k in range(2):
        tails = split(jnp.where(lane // 2 == k, south_misc, 0.0))
        heads = split(jnp.where(lane // 2 == 2 + k, north_misc, 0.0))
        part = pick((rows[6 + k : 7 + k] == own_c) & active, tails)
        part = part + pick((rows[8 + k : 9 + k] == own_c) & active, heads)
        ends = part if ends is None else ends + part
    return west, east, lower, upper, ends + roll(ends, -2, 1)


def first_kernel(
    rows_x, recv_ref, gath_ref, col_ref, row_ref, c_out, s_out, flux_out, east_out, west_out, misc_out, scal_out
):
    devices = recv_ref.shape[0] // ROWS
    width = recv_ref.shape[1]

    def received(at):
        return recv_ref[pl.ds(at, devices, stride=ROWS), :]

    cols, rows = col_ref[...], row_ref[...]
    layers = east_out.shape[0]
    misc = received(8)
    sums = jnp.sum(misc, 0, keepdims=True)
    at = iota(sums.shape, 1)
    gamma, bend, curve, twist = (
        jnp.sum(jnp.where(at == 8 + i, sums, 0.0), 1, keepdims=True) for i in range(4)
    )
    alpha = gamma / bend
    gamma_next = alpha * alpha * curve - gamma
    beta = gamma_next / gamma
    cross = bend - alpha * curve
    bend_next = bend - 2.0 * alpha * curve + alpha * alpha * twist + 2.0 * beta * cross + beta * beta * bend
    alpha_next = gamma_next / bend_next
    on_d = alpha + alpha_next * (1.0 + beta)
    on_w = -alpha * alpha_next
    lane8 = iota((8, width), 1)
    scal_out[...] = jnp.where(lane8 == 0, on_d, on_w)

    c = jnp.concatenate([received(0), received(1)], 0)
    s = jnp.concatenate([received(2), received(3)], 0)
    layer = iota((layers, 2 * devices), 0)
    west_codes = jnp.concatenate([rows[2:3], rows[3:4]], 1)
    east_codes = jnp.concatenate([rows[4:5], rows[5:6]], 1)
    west_edge = pick(layer == west_codes, split(jnp.concatenate([received(4), received(5)], 0)))
    east_edge = pick(layer == east_codes, split(jnp.concatenate([received(6), received(7)], 0)))
    fluxes = []
    for i in range(6):
        slots = 2 * devices
        flux = on_d * gath_ref[pl.ds(i, slots, stride=16), :]
        flux = flux + on_w * gath_ref[pl.ds(6 + i, slots, stride=16), :]
        flux_out[i] = flux
        fluxes.append(flux)
    beside = neighbour_values(c, cols, rows, west_edge, east_edge, misc, misc, rows_x)
    c = transport(c, s, fluxes, *beside)
    c_out[...] = c
    s_out[...] = s
    own_r = jnp.concatenate([rows[0:1], rows[1:2]], 1)
    here = (own_r // rows_x == layer) & (own_r >= 0)
    parts = split(c)
    east_out[...] = pick(here & (own_r % rows_x == rows_x - 1), parts)
    west_out[...] = pick(here & (own_r % rows_x == 0), parts)
    lane = iota((devices, width), 1)
    c0, c1 = c[:devices], c[devices:]
    misc_out[...] = jnp.where(
        lane < 2,
        roll(c0, 2, 1),
        jnp.where(lane < 4, roll(c1, 4, 1), jnp.where(lane < 6, roll(c0, 4, 1), roll(c1, 6, 1))),
    )


def first_step(received, gathered, cols, rows, layers, rows_x):
    width = received.shape[1]
    devices = cols.shape[0]
    lines = jax.ShapeDtypeStruct((2 * devices, width), F32)
    edge = jax.ShapeDtypeStruct((layers, width), F32)
    return pl.pallas_call(
        functools.partial(first_kernel, rows_x),
        out_shape=[
            lines,
            lines,
            jax.ShapeDtypeStruct((6, 2 * devices, width), F32),
            edge,
            edge,
            jax.ShapeDtypeStruct((devices, width), F32),
            jax.ShapeDtypeStruct((8, width), F32),
        ],
        compiler_params=params(16),
        name="first_step",
    )(received, gathered, cols, rows)


def second_kernel(
    rows_x, c_ref, s_ref, flux_ref, col_ref, row_ref, west_ref, east_ref, south_ref, north_ref, out_ref
):
    c, s = c_ref[...], s_ref[...]
    devices = c.shape[0] // 2
    beside = neighbour_values(
        c, col_ref[...], row_ref[...], west_ref[...], east_ref[...], south_ref[...], north_ref[...], rows_x
    )
    c = transport(c, s, [flux_ref[i] for i in range(6)], *beside)
    for k in range(2):
        out_ref[pl.ds(k, devices, stride=2), :] = c[k * devices : (k + 1) * devices]


def second_step(c, s, fluxes, cols, rows, west, east, south, north, rows_x):
    return pl.pallas_call(
        functools.partial(second_kernel, rows_x),
        out_shape=jax.ShapeDtypeStruct(c.shape, F32),
        compiler_params=params(16),
        name="second_step",
    )(c, s, fluxes, cols, rows, west, east, south, north)


def owner_kernel(lines, ids_ref, recv_ref, out_ref):
    devices, owned = ids_ref.shape
    own = ids_ref[pl.ds(place(), 1), :]
    brick = own // lines
    brick_col = column(brick.astype(F32)).astype(jnp.int32)
    square = (owned, owned)
    same = (brick_col == brick) & (iota(square, 1) < iota(square, 0))
    rank = jnp.sum(jnp.where(same, 1.0, 0.0), 1, keepdims=True).astype(jnp.int32)
    mask = brick_col * 2 + rank == iota((owned, 2 * devices), 1)
    out_ref[...] = pick(mask, split(recv_ref[...]))


def to_owner(ids, received, lines):
    return pl.pallas_call(
        functools.partial(owner_kernel, lines),
        out_shape=jax.ShapeDtypeStruct((ids.shape[1], received.shape[1]), F32),
        compiler_params=params(16),
        name="to_owner",
    )(ids, received)


def exchange(low_side, high_side, axis):
    count = lax.axis_size(axis)
    forward = [(i, i + 1) for i in range(count - 1)]
    backward = [(i + 1, i) for i in range(count - 1)]
    return lax.ppermute(high_side, axis, forward), lax.ppermute(low_side, axis, backward)


def body(conductivity, storage, recharge, block_ids, neighbours, concentration, sorption):
    layers, rows_x, width = conductivity.shape
    devices = lax.axis_size(AXES)
    owned = concentration.shape[0]
    ids = block_ids.reshape(devices, owned)
    to_east, to_west, conductivity, storage, recharge, ids, concentration, sorption = load(
        conductivity, storage, recharge, ids, concentration, sorption
    )
    west, east = exchange(to_west, to_east, "gx")
    inner, send, cols, rows = prepare(conductivity, storage, recharge, ids, concentration, sorption)
    strip = pack_strip(inner, west, east)
    south, north = exchange(strip, strip, "gy")
    base, image, gathered, send = flow(
        conductivity, storage, recharge, west, east, strip, south, north, send, rows[:2]
    )
    received = lax.all_to_all(
        send.reshape(devices, 1, ROWS * width), AXES, split_axis=0, concat_axis=0, tiled=True
    ).reshape(devices * ROWS, width)
    c, s, flux, to_east, to_west, misc, scal = first_step(
        received, gathered, cols, rows, layers, rows_x
    )
    west, east = exchange(to_west, to_east, "gx")
    south, north = exchange(misc, misc, "gy")
    head = scal[0, 0] * base + scal[0, 1] * image
    result = second_step(c, s, flux, cols, rows, west, east, south, north, rows_x)
    returned = lax.all_to_all(
        result.reshape(devices, 2, width), AXES, split_axis=0, concat_axis=0, tiled=True
    ).reshape(devices * 2, width)
    return head, to_owner(ids, returned, layers * rows_x)


def solution(mesh):
    return jax.shard_map(
        body,
        mesh=mesh,
        in_specs=(
            P(None, "gx", "gy"),
            P(None, "gx", "gy"),
            P(None, "gx", "gy"),
            P(),
            P(("gx", "gy"), None),
            P(("gx", "gy"), None),
            P(("gx", "gy"), None),
        ),
        out_specs=(P(None, "gx", "gy"), P(("gx", "gy"), None)),
        check_vma=False,
    )
```

```python
import functools

import jax
import jax.numpy as jnp
from jax import lax
from jax.experimental import pallas as pl
from jax.experimental.pallas import tpu as pltpu
from jax.sharding import PartitionSpec as P

PICARD = 3
POROSITY = 0.35
BULK_DENSITY = 1.6
EXPONENT = 0.7
SOFTEN = 0.05
DISPERSION = 0.5
TIME_STEP = 0.1
ADVECT = 1.0
VERTICAL = 2.0
COUPLING = TIME_STEP * DISPERSION

AXES = ("gx", "gy")
ROWS = 9
NONE = -5000
F32 = jnp.float32
BF16 = jnp.bfloat16


def params(mib):
    return pltpu.CompilerParams(vmem_limit_bytes=int(mib * 1024 * 1024))


def iota(shape, dim):
    return lax.broadcasted_iota(jnp.int32, shape, dim)


def roll(x, shift, axis):
    return pltpu.roll(x, shift % x.shape[axis] if isinstance(shift, int) else shift, axis)


def split(x):
    high = x.astype(BF16)
    rest = x - high.astype(F32)
    middle = rest.astype(BF16)
    low = (rest - middle.astype(F32)).astype(BF16)
    return high, middle, low


def pick(mask, parts):
    chosen = jnp.where(mask, 1.0, 0.0).astype(BF16)
    high, middle, low = (jnp.dot(chosen, part, preferred_element_type=F32) for part in parts)
    return (low + middle) + high


def rows_of(parts, start, stop):
    return tuple(part[start:stop] for part in parts)


def place():
    across = lax.axis_size("gy")
    return lax.axis_index("gx") * across + lax.axis_index("gy")


def by_turns(axis, low, high):
    odd = jnp.full(low.shape, lax.axis_index(axis) % 2) == 1
    return jnp.where(odd, low, high), jnp.where(odd, high, low)


def from_turns(axis, first, second):
    at = jnp.full(first.shape, lax.axis_index(axis))
    odd = at % 2 == 1
    low = jnp.where(at == 0, 0.0, jnp.where(odd, first, second))
    high = jnp.where(at == lax.axis_size(axis) - 1, 0.0, jnp.where(odd, second, first))
    return low, high


def swap(axis, first, second):
    count = lax.axis_size(axis)
    one = [(i, i ^ 1) for i in range(count)]
    other = [(i, (i + 1 if i % 2 else i - 1) % count) for i in range(count)]
    return lax.ppermute(first, axis, one), lax.ppermute(second, axis, other)


HBM = pl.BlockSpec(memory_space=pltpu.HBM)
SMEM = pl.BlockSpec(memory_space=pltpu.SMEM)
VMEM = pl.BlockSpec(memory_space=pltpu.VMEM)


def fetch(pairs, sems):
    copies = [pltpu.make_async_copy(src, dst, sems.at[i]) for i, (src, dst) in enumerate(pairs)]
    for copy in copies:
        copy.start()
    return copies


def load_kernel(
    k_hbm, s_hbm, r_hbm, ids_hbm, conc_hbm, sorp_hbm,
    first_ref, second_ref, k_ref, s_ref, r_ref, ids_ref, conc_ref, sorp_ref, sems,
):
    copies = fetch(
        [
            (k_hbm, k_ref),
            (s_hbm, s_ref),
            (r_hbm, r_ref),
            (ids_hbm, ids_ref),
            (conc_hbm, conc_ref),
            (sorp_hbm, sorp_ref),
        ],
        sems,
    )
    for copy in copies:
        copy.wait()
    high = k_ref.shape[1] - 8
    sub = iota(first_ref.shape[1:], 0)
    for z in range(first_ref.shape[0]):
        east = jnp.where(
            sub >= 5,
            k_ref[z, high:],
            jnp.where(sub >= 3, roll(s_ref[z, high:], -3, 0), roll(r_ref[z, high:], -5, 0)),
        )
        west = jnp.where(
            sub < 3,
            k_ref[z, :8],
            jnp.where(sub < 5, roll(s_ref[z, :8], 3, 0), roll(r_ref[z, :8], 5, 0)),
        )
        first_ref[z], second_ref[z] = by_turns("gx", west, east)


def load(*arrays):
    layers, rows, width = arrays[0].shape
    tile = jax.ShapeDtypeStruct((layers, 8, width), F32)
    return pl.pallas_call(
        load_kernel,
        in_specs=[HBM] * 6,
        out_specs=[VMEM] * 8,
        out_shape=[tile, tile] + [jax.ShapeDtypeStruct(x.shape, x.dtype) for x in arrays],
        scratch_shapes=[pltpu.SemaphoreType.DMA((6,))],
        compiler_params=params(8),
        name="load",
    )(*(pltpu.with_memory_space_constraint(x, pltpu.HBM) for x in arrays))


def beside(index, z, west_ref, east_ref):
    shift = (0, 3, 5)[index]
    top, bottom = west_ref[z], east_ref[z]
    if shift:
        top, bottom = roll(top, shift, 0), roll(bottom, -shift, 0)
    return top, bottom


def widened(index, z, own_ref, west_ref, east_ref):
    top, bottom = beside(index, z, west_ref, east_ref)
    return jnp.concatenate([top, own_ref[z], bottom], 0)


def strip_of(layers, layer):
    strip = None
    for z in range(layers):
        turned = roll(layer(z), z * 8 + 4, 1)
        strip = turned if strip is None else jnp.where(iota(turned.shape, 1) >= z * 8, turned, strip)
    return strip


def strip_kernel(inner_ref, first_ref, second_ref, out_ref, west_ref, east_ref):
    layers = west_ref.shape[0]
    west_ref[...], east_ref[...] = from_turns("gx", first_ref[...], second_ref[...])
    rows = inner_ref.shape[1]
    for index in range(3):
        out_ref[index, 8 : 8 + rows] = inner_ref[index]
        out_ref[index, 0:8] = strip_of(layers, lambda z: beside(index, z, west_ref, east_ref)[0])
        out_ref[index, 8 + rows :] = strip_of(layers, lambda z: beside(index, z, west_ref, east_ref)[1])


def pack_strip(inner, first, second):
    rows, width = inner.shape[1:]
    tile = jax.ShapeDtypeStruct(first.shape, F32)
    return pl.pallas_call(
        strip_kernel,
        out_shape=[jax.ShapeDtypeStruct((3, rows + 16, width), F32), tile, tile],
        compiler_params=params(4),
        name="pack_strip",
    )(inner, first, second)


def column(row):
    n = row.shape[1]
    return jnp.sum(jnp.where(iota((n, n), 0) == iota((n, n), 1), row, 0.0), 1, keepdims=True)


def as_row(col):
    n = col.shape[0]
    return jnp.sum(jnp.where(iota((n, n), 0) == iota((n, n), 1), col, 0.0), 0, keepdims=True)


def prepare_kernel(
    down, across, k_ref, s_ref, r_ref, ids_ref, conc_ref, sorp_ref, inner_ref, out_ref, col_ref, row_ref
):
    layers, rows_x = k_ref.shape[:2]
    devices, owned = ids_ref.shape
    lines = layers * rows_x
    me = place()
    ids = ids_ref[...]
    brick = ids // lines
    key = iota(ids.shape, 1) * lines + ids % lines
    gx, gy = me // across, me % across
    cols, rows = [], []
    for target, ok, edge in (
        (me, None, None),
        (me - across, gx > 0, rows_x - 1),
        (me + across, gx < down - 1, 0),
        (me - 1, gy > 0, None),
        (me + 1, gy < across - 1, None),
    ):
        if ok is not None:
            target = jnp.where(ok, target, -1)
        mine = brick == target
        first = jnp.min(jnp.where(mine, key, owned * lines).astype(F32), 1, keepdims=True)
        second = jnp.max(jnp.where(mine, key, -1).astype(F32), 1, keepdims=True)
        for code in (first, second):
            line = code.astype(jnp.int32) % lines
            keep = second >= 0.0
            if edge is not None:
                keep = keep & (line % rows_x == edge)
                line = line // rows_x
            value = jnp.where(keep, line, NONE).astype(F32)
            cols.append(value)
            rows.append(as_row(value))
    lane = iota((devices, 128), 1)
    packed = jnp.zeros((devices, 128), F32)
    for at, value in enumerate(cols):
        packed = jnp.where(lane == at, value, packed)
    col_ref[...] = packed.astype(jnp.int32)
    row_ref[...] = jnp.concatenate(
        rows + [jnp.zeros((16 - len(rows), devices), F32)], 0
    ).astype(jnp.int32)
    own = ids_ref[pl.ds(me, 1), :]
    own_brick = own // lines
    own_row = own % lines % rows_x
    brick_col = column(own_brick.astype(F32)).astype(jnp.int32)
    square = (owned, owned)
    same = (brick_col == own_brick) & (iota(square, 0) < iota(square, 1))
    rank = jnp.sum(jnp.where(same, 1.0, 0.0), 0, keepdims=True).astype(jnp.int32)
    dest = iota((devices, owned), 0)
    conc = conc_ref[...]
    conc_parts = split(conc)
    sorp_parts = split(sorp_ref[...])
    lane = iota((owned, conc.shape[1]), 1)
    misc = jnp.zeros((devices, conc.shape[1]), F32)
    for k in range(2):
        ranked = rank == k
        home = (dest == own_brick) & ranked
        out_ref[pl.ds(k, devices, stride=ROWS), :] = pick(home, conc_parts)
        out_ref[pl.ds(2 + k, devices, stride=ROWS), :] = pick(home, sorp_parts)
        after = (dest == own_brick + across) & ranked & (own_row == rows_x - 1)
        out_ref[pl.ds(4 + k, devices, stride=ROWS), :] = pick(after, conc_parts)
        before = (dest == own_brick - across) & ranked & (own_row == 0)
        out_ref[pl.ds(6 + k, devices, stride=ROWS), :] = pick(before, conc_parts)
        tails = jnp.where(lane // 2 == k, roll(conc, 2 + 2 * k, 1), 0.0)
        heads = jnp.where(lane // 2 == 2 + k, roll(conc, 4 + 2 * k, 1), 0.0)
        north = (dest == own_brick + 1) & ranked & (own_brick % across < across - 1)
        south = (dest == own_brick - 1) & ranked & (own_brick % across > 0)
        misc = misc + pick(north, split(tails)) + pick(south, split(heads))
    out_ref[pl.ds(8, devices, stride=ROWS), :] = misc
    for index, ref in enumerate((k_ref, s_ref, r_ref)):
        inner_ref[index] = strip_of(layers, lambda z: ref[z])


def prepare(conductivity, storage, recharge, ids, concentration, sorption):
    devices, owned = ids.shape
    layers, rows_x, width = conductivity.shape
    kernel = functools.partial(prepare_kernel, lax.axis_size("gx"), lax.axis_size("gy"))
    return pl.pallas_call(
        kernel,
        out_shape=[
            jax.ShapeDtypeStruct((3, rows_x, width), F32),
            jax.ShapeDtypeStruct((devices * ROWS, width), F32),
            jax.ShapeDtypeStruct((devices, 128), jnp.int32),
            jax.ShapeDtypeStruct((16, devices), jnp.int32),
        ],
        compiler_params=params(8),
        name="prepare",
    )(conductivity, storage, recharge, ids, concentration, sorption)


def harmonic(a, c):
    return jnp.where(jnp.minimum(a, c) > 0.0, 2.0 * a * c / (a + c), jnp.maximum(a, c))


def flow_kernel(
    k_ref, s_ref, r_ref, west_ref, east_ref, strip_ref, first_ref, second_ref, send_ref, slots_ref,
    d_out, w_out, gath_out, send_out,
    kx, sx, fw, fs, fb, rd, dd, ww, lines_ref,
):
    layers, rows, width = k_ref.shape
    tall = rows + 16
    shape = (tall, width)
    lane = iota(shape, 1)
    slot = lane % 8
    devices = send_ref.shape[0] // ROWS

    send_out[...] = send_ref[...]

    def side(low):
        def joined(index):
            south, north = from_turns("gy", first_ref[index], second_ref[index])
            if low:
                return jnp.where(slot < 4, south, strip_ref[index])
            return jnp.where(slot < 4, strip_ref[index], north)

        k, s, r = joined(0), joined(1), joined(2)
        face_w = harmonic(k, roll(k, 1, 0))
        face_s = harmonic(k, roll(k, 1, 1))
        face_b = jnp.where(lane >= 8, VERTICAL * harmonic(k, roll(k, 8, 1)), 0.0)
        diagonal = (
            s + face_w + roll(face_w, -1, 0) + face_s + roll(face_s, -1, 1) + face_b + roll(face_b, -8, 1)
        )
        inverse = jnp.where(k > 0.0, 1.0 / diagonal, 0.0)
        d = r * inverse
        flux_w = face_w * (roll(d, 1, 0) - d)
        flux_s = face_s * (roll(d, 1, 1) - d)
        flux_b = face_b * (roll(d, 8, 1) - d)
        image = (
            s * d
            + (roll(flux_w, -1, 0) - flux_w)
            + (roll(flux_s, -1, 1) - flux_s)
            + (roll(flux_b, -8, 1) - flux_b)
        )
        w = image * inverse
        return face_s, flux_s, face_s * (roll(w, 1, 1) - w)

    low_face, low_d, low_w = side(True)
    high_face, high_d, high_w = side(False)

    def with_low(z, field, strip):
        return jnp.where(lane == 0, roll(strip, width - 4 - z * 8, 1), field)

    def north_of(z, field, strip):
        shift = lax.rem(width - 5 + width - z * 8, width)
        return jnp.where(lane == width - 1, roll(strip, shift, 1), roll(field, -1, 1))

    def widen(z, carry):
        kx[z] = widened(0, z, k_ref, west_ref, east_ref)
        return carry

    lax.fori_loop(0, layers, widen, 0, unroll=4)
    fb[0] = jnp.zeros(shape, F32)

    def faces(z, carry):
        k = kx[z]
        face_w = harmonic(k, roll(k, 1, 0))
        face_s = with_low(z, harmonic(k, roll(k, 1, 1)), low_face)
        face_n = north_of(z, face_s, high_face)
        upper = kx[jnp.minimum(z + 1, layers - 1)]
        face_a = jnp.where(z < layers - 1, VERTICAL * harmonic(k, upper), 0.0)
        s = widened(1, z, s_ref, west_ref, east_ref)
        r = widened(2, z, r_ref, west_ref, east_ref)
        diagonal = s + face_w + roll(face_w, -1, 0) + face_s + face_n + fb[z] + face_a
        inverse = jnp.where(k > 0.0, 1.0 / diagonal, 0.0)
        fw[z] = face_w
        fs[z] = face_s
        fb[z + 1] = face_a
        rd[z] = inverse
        dd[z] = r * inverse
        sx[z] = s
        return carry

    lax.fori_loop(0, layers, faces, 0, unroll=2)

    def total(x):
        return jnp.sum(x[8 : 8 + rows].reshape(rows // 8, 8, width), 0)

    def apply(z, field, low, high, block):
        h = field[z]
        below = field[jnp.maximum(z - 1, 0)]
        above = field[jnp.minimum(z + 1, layers - 1)]
        flux_w = fw[z] * (roll(h, 1, 0) - h)
        flux_e = roll(flux_w, -1, 0)
        flux_b = fb[z] * (below - h)
        flux_a = fb[z + 1] * (h - above)
        flux_s = with_low(z, fs[z] * (roll(h, 1, 1) - h), low)
        flux_n = north_of(z, flux_s, high)
        for at, flux in enumerate((flux_w, flux_e, flux_b, flux_a, flux_s, flux_n)):
            start = z * (rows * 16) + (block + at)
            lines_ref[pl.ds(start, rows, stride=16), :] = flux[8 : 8 + rows]
        return h, sx[z] * h + (flux_e - flux_w) + (flux_a - flux_b) + (flux_n - flux_s)

    zero = jnp.zeros((8, width), F32)

    def first(z, sums):
        d, image = apply(z, dd, low_d, high_d, 0)
        w = image * rd[z]
        ww[z] = w
        d_out[z] = d[8 : 8 + rows]
        w_out[z] = w[8 : 8 + rows]
        r = r_ref[z]
        gamma = jnp.sum((r * d[8 : 8 + rows]).reshape(rows // 8, 8, width), 0)
        return sums[0] + gamma, sums[1] + total(d * image), sums[2] + total(image * w)

    gamma, bend, curve = lax.fori_loop(0, layers, first, (zero, zero, zero), unroll=2)

    def second(z, acc):
        w, image = apply(z, ww, low_w, high_w, 6)
        return acc + total(w * image)

    twist = lax.fori_loop(0, layers, second, zero, unroll=2)
    lane_row = iota((devices, width), 1)
    misc = send_ref[pl.ds(8, devices, stride=ROWS), :]
    for at, part in enumerate((gamma, bend, curve, twist)):
        value = jnp.sum(jnp.sum(part, 0, keepdims=True), 1, keepdims=True)
        misc = jnp.where(lane_row == 8 + at, value, misc)
    send_out[pl.ds(8, devices, stride=ROWS), :] = misc
    for k in range(2):

        def gather(i, carry):
            line = pl.multiple_of(jnp.maximum(slots_ref[k, i], 0) * 16, 16)
            slot = pl.multiple_of((k * devices + i) * 16, 16)
            gath_out[pl.ds(slot, 16), :] = lines_ref[pl.ds(line, 16), :]
            return carry

        lax.fori_loop(0, devices, gather, 0, unroll=8)


def flow(conductivity, storage, recharge, west, east, strip, first, second, send, slots):
    layers, rows, width = conductivity.shape
    tall = pltpu.VMEM((layers, rows + 16, width), F32)
    return pl.pallas_call(
        flow_kernel,
        out_shape=[
            jax.ShapeDtypeStruct(conductivity.shape, F32),
            jax.ShapeDtypeStruct(conductivity.shape, F32),
            jax.ShapeDtypeStruct((2 * slots.shape[1] * 16, width), F32),
            jax.ShapeDtypeStruct(send.shape, F32),
        ],
        in_specs=[VMEM] * 9 + [SMEM],
        out_specs=[VMEM] * 4,
        scratch_shapes=[tall] * 4
        + [pltpu.VMEM((layers + 1, rows + 16, width), F32)]
        + [tall] * 3
        + [pltpu.VMEM((layers * rows * 16, width), F32)],
        compiler_params=params(30),
        name="flow",
    )(conductivity, storage, recharge, west, east, strip, first, second, send, slots)


def minmod(a, d):
    return jnp.maximum(jnp.minimum(a, d), 0.0) + jnp.minimum(jnp.maximum(a, d), 0.0)


def tridiagonal(diagonal, right):
    width = diagonal.shape[1]
    side = jnp.where(iota(diagonal.shape, 1) == 0, 0.0, -COUPLING)
    step = 1
    while step < width:
        inverse = 1.0 / diagonal
        scaled = side * inverse
        value = right * inverse
        before = roll(inverse, step, 1)
        right = right - side * roll(value, step, 1) - roll(side * value, -step, 1)
        diagonal = diagonal - side * (side * before) - roll(side * scaled, -step, 1)
        side = -side * roll(scaled, step, 1)
        step *= 2
    return right / diagonal


def transport(c, sorption, fluxes, west, east, lower, upper, ends):
    lane = iota(c.shape, 1)
    width = c.shape[1]
    last = lane == width - 1
    south_one = roll(ends, -1, 1)
    north_one = roll(ends, width - 5, 1)
    back = jnp.where(lane == 0, south_one, roll(c, 1, 1))
    back2 = jnp.where(lane < 2, ends, roll(c, 2, 1))
    ahead = jnp.where(last, north_one, roll(c, -1, 1))
    ahead2 = jnp.where(lane >= width - 2, roll(ends, width - 6, 1), roll(c, -2, 1))
    q_w, q_e, q_b, q_a, q_s, q_n = fluxes

    def face(q, far_left, left, right, far_right):
        rise = right - left
        positive = left + 0.5 * minmod(rise, left - far_left)
        negative = right + 0.5 * minmod(-rise, right - far_right)
        return jnp.maximum(q, 0.0) * positive + jnp.minimum(q, 0.0) * negative

    along = face(q_s, back2, back, c, ahead)
    beyond = face(q_n, back, c, ahead, ahead2)
    advect = along - jnp.where(last, beyond, roll(along, -1, 1))
    advect = advect + jnp.maximum(q_w, 0.0) * west + jnp.minimum(q_w, 0.0) * c
    advect = advect - jnp.maximum(q_e, 0.0) * c - jnp.minimum(q_e, 0.0) * east
    advect = advect + jnp.maximum(q_b, 0.0) * lower + jnp.minimum(q_b, 0.0) * c
    advect = advect - jnp.maximum(q_a, 0.0) * c - jnp.minimum(q_a, 0.0) * upper
    advect = ADVECT * advect
    advect = advect + COUPLING * (
        jnp.where(lane == 0, south_one, 0.0) + jnp.where(last, north_one, 0.0)
    )
    weight = BULK_DENSITY * sorption
    v = c
    source = None
    for sweep in range(PICARD):
        square = v * v + SOFTEN * SOFTEN
        power = weight * jnp.exp((0.5 * (EXPONENT - 1.0)) * jnp.log(square))
        retard = POROSITY + power
        root = jnp.sqrt(square)
        if sweep == 0:
            source = POROSITY * c + power * root + advect
            target = retard * c + advect
        else:
            target = power * (v - root) + source
        v = tridiagonal(retard + 2.0 * COUPLING, target)
    return v


def neighbour_values(c, cols, rows, west_edge, east_edge, south_misc, north_misc, rows_x):
    own_c = jnp.concatenate([cols[:, 0:1], cols[:, 1:2]], 0)
    own_r = jnp.concatenate([rows[0:1], rows[1:2]], 1)
    layers = west_edge.shape[0]
    active = own_c >= 0
    row_c = own_c % rows_x
    layer_c = own_c // rows_x
    first = active & (row_c == 0)
    final = active & (row_c == rows_x - 1)
    at_layer = iota((own_c.shape[0], layers), 1) == layer_c
    parts = split(c)
    west = pick((own_r == own_c - 1) & (row_c != 0), parts) + pick(
        at_layer & first, split(west_edge)
    )
    east = pick((own_r == own_c + 1) & (row_c != rows_x - 1), parts) + pick(
        at_layer & final, split(east_edge)
    )
    lower = pick(own_r == own_c - rows_x, parts)
    upper = pick(own_r == own_c + rows_x, parts)
    lane = iota(south_misc.shape, 1)
    ends = None
    for k in range(2):
        tails = split(jnp.where(lane // 2 == k, south_misc, 0.0))
        heads = split(jnp.where(lane // 2 == 2 + k, north_misc, 0.0))
        part = pick((rows[6 + k : 7 + k] == own_c) & active, tails)
        part = part + pick((rows[8 + k : 9 + k] == own_c) & active, heads)
        ends = part if ends is None else ends + part
    return west, east, lower, upper, ends + roll(ends, -2, 1)


def first_kernel(
    rows_x, recv_ref, gath_ref, col_ref, row_ref, c_out, s_out, flux_out, first_out, second_out, misc_out, scal_out
):
    devices = recv_ref.shape[0] // ROWS
    width = recv_ref.shape[1]

    def received(at):
        return recv_ref[pl.ds(at, devices, stride=ROWS), :]

    cols, rows = col_ref[...], row_ref[...]
    layers = first_out.shape[0]
    misc = received(8)
    sums = jnp.sum(misc, 0, keepdims=True)
    at = iota(sums.shape, 1)
    gamma, bend, curve, twist = (
        jnp.sum(jnp.where(at == 8 + i, sums, 0.0), 1, keepdims=True) for i in range(4)
    )
    alpha = gamma / bend
    gamma_next = alpha * alpha * curve - gamma
    beta = gamma_next / gamma
    cross = bend - alpha * curve
    bend_next = bend - 2.0 * alpha * curve + alpha * alpha * twist + 2.0 * beta * cross + beta * beta * bend
    alpha_next = gamma_next / bend_next
    on_d = alpha + alpha_next * (1.0 + beta)
    on_w = -alpha * alpha_next
    lane8 = iota((8, width), 1)
    scal_out[...] = jnp.where(lane8 == 0, on_d, on_w)

    c = jnp.concatenate([received(0), received(1)], 0)
    s = jnp.concatenate([received(2), received(3)], 0)
    layer = iota((layers, 2 * devices), 0)
    west_codes = jnp.concatenate([rows[2:3], rows[3:4]], 1)
    east_codes = jnp.concatenate([rows[4:5], rows[5:6]], 1)
    west_edge = pick(layer == west_codes, split(jnp.concatenate([received(4), received(5)], 0)))
    east_edge = pick(layer == east_codes, split(jnp.concatenate([received(6), received(7)], 0)))
    fluxes = []
    for i in range(6):
        slots = 2 * devices
        flux = on_d * gath_ref[pl.ds(i, slots, stride=16), :]
        flux = flux + on_w * gath_ref[pl.ds(6 + i, slots, stride=16), :]
        flux_out[i] = flux
        fluxes.append(flux)
    beside = neighbour_values(c, cols, rows, west_edge, east_edge, misc, misc, rows_x)
    c = transport(c, s, fluxes, *beside)
    c_out[...] = c
    s_out[...] = s
    own_r = jnp.concatenate([rows[0:1], rows[1:2]], 1)
    here = (own_r // rows_x == layer) & (own_r >= 0)
    parts = split(c)
    first_out[...], second_out[...] = by_turns(
        "gx",
        pick(here & (own_r % rows_x == 0), parts),
        pick(here & (own_r % rows_x == rows_x - 1), parts),
    )
    lane = iota((devices, width), 1)
    c0, c1 = c[:devices], c[devices:]
    misc_out[...] = jnp.where(
        lane < 2,
        roll(c0, 2, 1),
        jnp.where(lane < 4, roll(c1, 4, 1), jnp.where(lane < 6, roll(c0, 4, 1), roll(c1, 6, 1))),
    )


def first_step(received, gathered, cols, rows, layers, rows_x):
    width = received.shape[1]
    devices = cols.shape[0]
    lines = jax.ShapeDtypeStruct((2 * devices, width), F32)
    edge = jax.ShapeDtypeStruct((layers, width), F32)
    return pl.pallas_call(
        functools.partial(first_kernel, rows_x),
        out_shape=[
            lines,
            lines,
            jax.ShapeDtypeStruct((6, 2 * devices, width), F32),
            edge,
            edge,
            jax.ShapeDtypeStruct((devices, width), F32),
            jax.ShapeDtypeStruct((8, width), F32),
        ],
        compiler_params=params(16),
        name="first_step",
    )(received, gathered, cols, rows)


def second_kernel(
    rows_x, c_ref, s_ref, flux_ref, col_ref, row_ref, edge1_ref, edge2_ref, misc1_ref, misc2_ref, out_ref
):
    c, s = c_ref[...], s_ref[...]
    devices = c.shape[0] // 2
    west, east = from_turns("gx", edge1_ref[...], edge2_ref[...])
    south, north = from_turns("gy", misc1_ref[...], misc2_ref[...])
    beside = neighbour_values(c, col_ref[...], row_ref[...], west, east, south, north, rows_x)
    c = transport(c, s, [flux_ref[i] for i in range(6)], *beside)
    for k in range(2):
        out_ref[pl.ds(k, devices, stride=2), :] = c[k * devices : (k + 1) * devices]


def second_step(c, s, fluxes, cols, rows, edges, miscs, rows_x):
    return pl.pallas_call(
        functools.partial(second_kernel, rows_x),
        out_shape=jax.ShapeDtypeStruct(c.shape, F32),
        compiler_params=params(16),
        name="second_step",
    )(c, s, fluxes, cols, rows, *edges, *miscs)


def owner_kernel(lines, ids_ref, recv_ref, out_ref):
    devices, owned = ids_ref.shape
    own = ids_ref[pl.ds(place(), 1), :]
    brick = own // lines
    brick_col = column(brick.astype(F32)).astype(jnp.int32)
    square = (owned, owned)
    same = (brick_col == brick) & (iota(square, 1) < iota(square, 0))
    rank = jnp.sum(jnp.where(same, 1.0, 0.0), 1, keepdims=True).astype(jnp.int32)
    mask = brick_col * 2 + rank == iota((owned, 2 * devices), 1)
    out_ref[...] = pick(mask, split(recv_ref[...]))


def to_owner(ids, received, lines):
    return pl.pallas_call(
        functools.partial(owner_kernel, lines),
        out_shape=jax.ShapeDtypeStruct((ids.shape[1], received.shape[1]), F32),
        compiler_params=params(16),
        name="to_owner",
    )(ids, received)


def body(conductivity, storage, recharge, block_ids, neighbours, concentration, sorption):
    layers, rows_x, width = conductivity.shape
    devices = lax.axis_size(AXES)
    owned = concentration.shape[0]
    ids = block_ids.reshape(devices, owned)
    first, second, conductivity, storage, recharge, ids, concentration, sorption = load(
        conductivity, storage, recharge, ids, concentration, sorption
    )
    first, second = swap("gx", first, second)
    inner, send, cols, rows = prepare(conductivity, storage, recharge, ids, concentration, sorption)
    strip, west, east = pack_strip(inner, first, second)
    first, second = swap("gy", strip, strip)
    base, image, gathered, send = flow(
        conductivity, storage, recharge, west, east, strip, first, second, send, rows[:2]
    )
    received = lax.all_to_all(
        send.reshape(devices, 1, ROWS * width), AXES, split_axis=0, concat_axis=0, tiled=True
    ).reshape(devices * ROWS, width)
    c, s, flux, first, second, misc, scal = first_step(received, gathered, cols, rows, layers, rows_x)
    edges = swap("gx", first, second)
    miscs = swap("gy", misc, misc)
    head = scal[0, 0] * base + scal[0, 1] * image
    result = second_step(c, s, flux, cols, rows, edges, miscs, rows_x)
    returned = lax.all_to_all(
        result.reshape(devices, 2, width), AXES, split_axis=0, concat_axis=0, tiled=True
    ).reshape(devices * 2, width)
    return head, to_owner(ids, returned, layers * rows_x)


def solution(mesh):
    return jax.shard_map(
        body,
        mesh=mesh,
        in_specs=(
            P(None, "gx", "gy"),
            P(None, "gx", "gy"),
            P(None, "gx", "gy"),
            P(),
            P(("gx", "gy"), None),
            P(("gx", "gy"), None),
            P(("gx", "gy"), None),
        ),
        out_specs=(P(None, "gx", "gy"), P(("gx", "gy"), None)),
        check_vma=False,
    )
```

```python
import functools

import jax
import jax.numpy as jnp
from jax import lax
from jax.experimental import pallas as pl
from jax.experimental.pallas import tpu as pltpu
from jax.sharding import PartitionSpec as P

PICARD = 3
POROSITY = 0.35
BULK_DENSITY = 1.6
EXPONENT = 0.7
SOFTEN = 0.05
DISPERSION = 0.5
TIME_STEP = 0.1
ADVECT = 1.0
VERTICAL = 2.0
COUPLING = TIME_STEP * DISPERSION

AXES = ("gx", "gy")
ROWS = 9
NONE = -5000
F32 = jnp.float32
BF16 = jnp.bfloat16


def params(mib):
    return pltpu.CompilerParams(vmem_limit_bytes=int(mib * 1024 * 1024))


def iota(shape, dim):
    return lax.broadcasted_iota(jnp.int32, shape, dim)


def roll(x, shift, axis):
    return pltpu.roll(x, shift % x.shape[axis] if isinstance(shift, int) else shift, axis)


def split(x):
    high = x.astype(BF16)
    rest = x - high.astype(F32)
    middle = rest.astype(BF16)
    low = (rest - middle.astype(F32)).astype(BF16)
    return high, middle, low


def pick(mask, parts):
    chosen = jnp.where(mask, 1.0, 0.0).astype(BF16)
    high, middle, low = (jnp.dot(chosen, part, preferred_element_type=F32) for part in parts)
    return (low + middle) + high


def rows_of(parts, start, stop):
    return tuple(part[start:stop] for part in parts)


def place():
    across = lax.axis_size("gy")
    return lax.axis_index("gx") * across + lax.axis_index("gy")


def by_turns(axis, low, high):
    odd = jnp.full(low.shape, lax.axis_index(axis) % 2) == 1
    return jnp.where(odd, low, high), jnp.where(odd, high, low)


def from_turns(axis, first, second):
    at = jnp.full(first.shape, lax.axis_index(axis))
    odd = at % 2 == 1
    low = jnp.where(at == 0, 0.0, jnp.where(odd, first, second))
    high = jnp.where(at == lax.axis_size(axis) - 1, 0.0, jnp.where(odd, second, first))
    return low, high


def swap(axis, first, second):
    count = lax.axis_size(axis)
    one = [(i, i ^ 1) for i in range(count)]
    other = [(i, (i + 1 if i % 2 else i - 1) % count) for i in range(count)]
    return lax.ppermute(first, axis, one), lax.ppermute(second, axis, other)


HBM = pl.BlockSpec(memory_space=pltpu.HBM)
SMEM = pl.BlockSpec(memory_space=pltpu.SMEM)
VMEM = pl.BlockSpec(memory_space=pltpu.VMEM)


def fetch(pairs, sems):
    copies = [pltpu.make_async_copy(src, dst, sems.at[i]) for i, (src, dst) in enumerate(pairs)]
    for copy in copies:
        copy.start()
    return copies


def load_kernel(
    k_hbm, s_hbm, r_hbm, ids_hbm, conc_hbm, sorp_hbm,
    first_ref, second_ref, k_ref, s_ref, r_ref, ids_ref, conc_ref, sorp_ref, sems,
):
    copies = fetch(
        [
            (k_hbm, k_ref),
            (s_hbm, s_ref),
            (r_hbm, r_ref),
            (ids_hbm, ids_ref),
            (conc_hbm, conc_ref),
            (sorp_hbm, sorp_ref),
        ],
        sems,
    )
    for copy in copies:
        copy.wait()
    high = k_ref.shape[1] - 8
    sub = iota(first_ref.shape[1:], 0)
    for z in range(first_ref.shape[0]):
        east = jnp.where(
            sub >= 5,
            k_ref[z, high:],
            jnp.where(sub >= 3, roll(s_ref[z, high:], -3, 0), roll(r_ref[z, high:], -5, 0)),
        )
        west = jnp.where(
            sub < 3,
            k_ref[z, :8],
            jnp.where(sub < 5, roll(s_ref[z, :8], 3, 0), roll(r_ref[z, :8], 5, 0)),
        )
        first_ref[z], second_ref[z] = by_turns("gx", west, east)


def load(*arrays):
    layers, rows, width = arrays[0].shape
    tile = jax.ShapeDtypeStruct((layers, 8, width), F32)
    return pl.pallas_call(
        load_kernel,
        in_specs=[HBM] * 6,
        out_specs=[VMEM] * 8,
        out_shape=[tile, tile] + [jax.ShapeDtypeStruct(x.shape, x.dtype) for x in arrays],
        scratch_shapes=[pltpu.SemaphoreType.DMA((6,))],
        compiler_params=params(8),
        name="load",
    )(*(pltpu.with_memory_space_constraint(x, pltpu.HBM) for x in arrays))


def beside(index, z, west_ref, east_ref):
    shift = (0, 3, 5)[index]
    top, bottom = west_ref[z], east_ref[z]
    if shift:
        top, bottom = roll(top, shift, 0), roll(bottom, -shift, 0)
    return top, bottom


def widened(index, z, own_ref, west_ref, east_ref):
    top, bottom = beside(index, z, west_ref, east_ref)
    return jnp.concatenate([top, own_ref[z], bottom], 0)


def strip_of(layers, layer):
    strip = None
    for z in range(layers):
        turned = roll(layer(z), z * 8 + 4, 1)
        strip = turned if strip is None else jnp.where(iota(turned.shape, 1) >= z * 8, turned, strip)
    return strip


def strip_kernel(inner_ref, first_ref, second_ref, out_ref, west_ref, east_ref):
    layers = west_ref.shape[0]
    west_ref[...], east_ref[...] = from_turns("gx", first_ref[...], second_ref[...])
    rows = inner_ref.shape[1]
    for index in range(3):
        out_ref[index, 8 : 8 + rows] = inner_ref[index]
        out_ref[index, 0:8] = strip_of(layers, lambda z: beside(index, z, west_ref, east_ref)[0])
        out_ref[index, 8 + rows :] = strip_of(layers, lambda z: beside(index, z, west_ref, east_ref)[1])


def pack_strip(inner, first, second):
    rows, width = inner.shape[1:]
    tile = jax.ShapeDtypeStruct(first.shape, F32)
    return pl.pallas_call(
        strip_kernel,
        out_shape=[jax.ShapeDtypeStruct((3, rows + 16, width), F32), tile, tile],
        compiler_params=params(4),
        name="pack_strip",
    )(inner, first, second)


def column(row):
    n = row.shape[1]
    return jnp.sum(jnp.where(iota((n, n), 0) == iota((n, n), 1), row, 0.0), 1, keepdims=True)


def as_row(col):
    n = col.shape[0]
    return jnp.sum(jnp.where(iota((n, n), 0) == iota((n, n), 1), col, 0.0), 0, keepdims=True)


def prepare_kernel(
    down, across, k_ref, s_ref, r_ref, ids_ref, conc_ref, sorp_ref, inner_ref, out_ref, col_ref, row_ref
):
    layers, rows_x = k_ref.shape[:2]
    devices, owned = ids_ref.shape
    lines = layers * rows_x
    me = place()
    ids = ids_ref[...]
    brick = ids // lines
    key = iota(ids.shape, 1) * lines + ids % lines
    gx, gy = me // across, me % across
    cols, rows = [], []
    for target, ok, edge in (
        (me, None, None),
        (me - across, gx > 0, rows_x - 1),
        (me + across, gx < down - 1, 0),
        (me - 1, gy > 0, None),
        (me + 1, gy < across - 1, None),
    ):
        if ok is not None:
            target = jnp.where(ok, target, -1)
        mine = brick == target
        first = jnp.min(jnp.where(mine, key, owned * lines).astype(F32), 1, keepdims=True)
        second = jnp.max(jnp.where(mine, key, -1).astype(F32), 1, keepdims=True)
        for code in (first, second):
            line = code.astype(jnp.int32) % lines
            keep = second >= 0.0
            if edge is not None:
                keep = keep & (line % rows_x == edge)
                line = line // rows_x
            value = jnp.where(keep, line, NONE).astype(F32)
            cols.append(value)
            rows.append(as_row(value))
    lane = iota((devices, 128), 1)
    packed = jnp.zeros((devices, 128), F32)
    for at, value in enumerate(cols):
        packed = jnp.where(lane == at, value, packed)
    col_ref[...] = packed.astype(jnp.int32)
    row_ref[...] = jnp.concatenate(
        rows + [jnp.zeros((16 - len(rows), devices), F32)], 0
    ).astype(jnp.int32)
    own = ids_ref[pl.ds(me, 1), :]
    own_brick = own // lines
    own_row = own % lines % rows_x
    brick_col = column(own_brick.astype(F32)).astype(jnp.int32)
    square = (owned, owned)
    same = (brick_col == own_brick) & (iota(square, 0) < iota(square, 1))
    rank = jnp.sum(jnp.where(same, 1.0, 0.0), 0, keepdims=True).astype(jnp.int32)
    dest = iota((devices, owned), 0)
    conc = conc_ref[...]
    conc_parts = split(conc)
    sorp_parts = split(sorp_ref[...])
    lane = iota((owned, conc.shape[1]), 1)
    misc = jnp.zeros((devices, conc.shape[1]), F32)
    for k in range(2):
        ranked = rank == k
        home = (dest == own_brick) & ranked
        out_ref[pl.ds(k, devices, stride=ROWS), :] = pick(home, conc_parts)
        out_ref[pl.ds(2 + k, devices, stride=ROWS), :] = pick(home, sorp_parts)
        after = (dest == own_brick + across) & ranked & (own_row == rows_x - 1)
        out_ref[pl.ds(4 + k, devices, stride=ROWS), :] = pick(after, conc_parts)
        before = (dest == own_brick - across) & ranked & (own_row == 0)
        out_ref[pl.ds(6 + k, devices, stride=ROWS), :] = pick(before, conc_parts)
        tails = jnp.where(lane // 2 == k, roll(conc, 2 + 2 * k, 1), 0.0)
        heads = jnp.where(lane // 2 == 2 + k, roll(conc, 4 + 2 * k, 1), 0.0)
        north = (dest == own_brick + 1) & ranked & (own_brick % across < across - 1)
        south = (dest == own_brick - 1) & ranked & (own_brick % across > 0)
        misc = misc + pick(north, split(tails)) + pick(south, split(heads))
    out_ref[pl.ds(8, devices, stride=ROWS), :] = misc
    for index, ref in enumerate((k_ref, s_ref, r_ref)):
        inner_ref[index] = strip_of(layers, lambda z: ref[z])


def prepare(conductivity, storage, recharge, ids, concentration, sorption):
    devices, owned = ids.shape
    layers, rows_x, width = conductivity.shape
    kernel = functools.partial(prepare_kernel, lax.axis_size("gx"), lax.axis_size("gy"))
    return pl.pallas_call(
        kernel,
        out_shape=[
            jax.ShapeDtypeStruct((3, rows_x, width), F32),
            jax.ShapeDtypeStruct((devices * ROWS, width), F32),
            jax.ShapeDtypeStruct((devices, 128), jnp.int32),
            jax.ShapeDtypeStruct((16, devices), jnp.int32),
        ],
        compiler_params=params(8),
        name="prepare",
    )(conductivity, storage, recharge, ids, concentration, sorption)


def harmonic(a, c):
    return jnp.where(jnp.minimum(a, c) > 0.0, 2.0 * a * c / (a + c), jnp.maximum(a, c))


def flow_kernel(
    k_ref, s_ref, r_ref, west_ref, east_ref, strip_ref, first_ref, second_ref, send_ref, slots_ref,
    d_out, w_out, gath_out, send_out,
    kx, sx, fw, fs, fb, rd, dd, ww, lines_ref,
):
    layers, rows, width = k_ref.shape
    tall = rows + 16
    shape = (tall, width)
    lane = iota(shape, 1)
    slot = lane % 8
    devices = send_ref.shape[0] // ROWS

    send_out[...] = send_ref[...]

    def side(low):
        def joined(index):
            south, north = from_turns("gy", first_ref[index], second_ref[index])
            if low:
                return jnp.where(slot < 4, south, strip_ref[index])
            return jnp.where(slot < 4, strip_ref[index], north)

        k, s, r = joined(0), joined(1), joined(2)
        face_w = harmonic(k, roll(k, 1, 0))
        face_s = harmonic(k, roll(k, 1, 1))
        face_b = jnp.where(lane >= 8, VERTICAL * harmonic(k, roll(k, 8, 1)), 0.0)
        diagonal = (
            s + face_w + roll(face_w, -1, 0) + face_s + roll(face_s, -1, 1) + face_b + roll(face_b, -8, 1)
        )
        inverse = jnp.where(k > 0.0, 1.0 / diagonal, 0.0)
        d = r * inverse
        flux_w = face_w * (roll(d, 1, 0) - d)
        flux_s = face_s * (roll(d, 1, 1) - d)
        flux_b = face_b * (roll(d, 8, 1) - d)
        image = (
            s * d
            + (roll(flux_w, -1, 0) - flux_w)
            + (roll(flux_s, -1, 1) - flux_s)
            + (roll(flux_b, -8, 1) - flux_b)
        )
        w = image * inverse
        return face_s, flux_s, face_s * (roll(w, 1, 1) - w)

    low_face, low_d, low_w = side(True)
    high_face, high_d, high_w = side(False)

    def with_low(z, field, strip):
        return jnp.where(lane == 0, roll(strip, width - 4 - z * 8, 1), field)

    def north_of(z, field, strip):
        shift = lax.rem(width - 5 + width - z * 8, width)
        return jnp.where(lane == width - 1, roll(strip, shift, 1), roll(field, -1, 1))

    def widen(z, carry):
        kx[z] = widened(0, z, k_ref, west_ref, east_ref)
        return carry

    lax.fori_loop(0, layers, widen, 0, unroll=4)
    fb[0] = jnp.zeros(shape, F32)

    def faces(z, carry):
        k = kx[z]
        face_w = harmonic(k, roll(k, 1, 0))
        face_s = with_low(z, harmonic(k, roll(k, 1, 1)), low_face)
        face_n = north_of(z, face_s, high_face)
        upper = kx[jnp.minimum(z + 1, layers - 1)]
        face_a = jnp.where(z < layers - 1, VERTICAL * harmonic(k, upper), 0.0)
        s = widened(1, z, s_ref, west_ref, east_ref)
        r = widened(2, z, r_ref, west_ref, east_ref)
        diagonal = s + face_w + roll(face_w, -1, 0) + face_s + face_n + fb[z] + face_a
        inverse = jnp.where(k > 0.0, 1.0 / diagonal, 0.0)
        fw[z] = face_w
        fs[z] = face_s
        fb[z + 1] = face_a
        rd[z] = inverse
        dd[z] = r * inverse
        sx[z] = s
        return carry

    lax.fori_loop(0, layers, faces, 0, unroll=2)

    def total(x):
        return jnp.sum(x[8 : 8 + rows].reshape(rows // 8, 8, width), 0)

    def apply(z, field, low, high, block):
        h = field[z]
        below = field[jnp.maximum(z - 1, 0)]
        above = field[jnp.minimum(z + 1, layers - 1)]
        flux_w = fw[z] * (roll(h, 1, 0) - h)
        flux_e = roll(flux_w, -1, 0)
        flux_b = fb[z] * (below - h)
        flux_a = fb[z + 1] * (h - above)
        flux_s = with_low(z, fs[z] * (roll(h, 1, 1) - h), low)
        flux_n = north_of(z, flux_s, high)
        for at, flux in enumerate((flux_w, flux_e, flux_b, flux_a, flux_s, flux_n)):
            start = z * (rows * 16) + (block + at)
            lines_ref[pl.ds(start, rows, stride=16), :] = flux[8 : 8 + rows]
        return h, sx[z] * h + (flux_e - flux_w) + (flux_a - flux_b) + (flux_n - flux_s)

    zero = jnp.zeros((8, width), F32)

    def first(z, sums):
        d, image = apply(z, dd, low_d, high_d, 0)
        w = image * rd[z]
        ww[z] = w
        d_out[z] = d[8 : 8 + rows]
        w_out[z] = w[8 : 8 + rows]
        r = r_ref[z]
        gamma = jnp.sum((r * d[8 : 8 + rows]).reshape(rows // 8, 8, width), 0)
        return sums[0] + gamma, sums[1] + total(d * image), sums[2] + total(image * w)

    gamma, bend, curve = lax.fori_loop(0, layers, first, (zero, zero, zero), unroll=2)

    def second(z, acc):
        w, image = apply(z, ww, low_w, high_w, 6)
        return acc + total(w * image)

    twist = lax.fori_loop(0, layers, second, zero, unroll=2)
    lane_row = iota((devices, width), 1)
    misc = send_ref[pl.ds(8, devices, stride=ROWS), :]
    for at, part in enumerate((gamma, bend, curve, twist)):
        value = jnp.sum(jnp.sum(part, 0, keepdims=True), 1, keepdims=True)
        misc = jnp.where(lane_row == 8 + at, value, misc)
    send_out[pl.ds(8, devices, stride=ROWS), :] = misc
    for k in range(2):

        def gather(i, carry):
            line = pl.multiple_of(jnp.maximum(slots_ref[k, i], 0) * 16, 16)
            slot = pl.multiple_of((k * devices + i) * 16, 16)
            gath_out[pl.ds(slot, 16), :] = lines_ref[pl.ds(line, 16), :]
            return carry

        lax.fori_loop(0, devices, gather, 0, unroll=8)


def flow(conductivity, storage, recharge, west, east, strip, first, second, send, slots):
    layers, rows, width = conductivity.shape
    tall = pltpu.VMEM((layers, rows + 16, width), F32)
    return pl.pallas_call(
        flow_kernel,
        out_shape=[
            jax.ShapeDtypeStruct(conductivity.shape, F32),
            jax.ShapeDtypeStruct(conductivity.shape, F32),
            jax.ShapeDtypeStruct((2 * slots.shape[1] * 16, width), F32),
            jax.ShapeDtypeStruct(send.shape, F32),
        ],
        in_specs=[VMEM] * 9 + [SMEM],
        out_specs=[VMEM] * 4,
        scratch_shapes=[tall] * 4
        + [pltpu.VMEM((layers + 1, rows + 16, width), F32)]
        + [tall] * 3
        + [pltpu.VMEM((layers * rows * 16, width), F32)],
        compiler_params=params(30),
        name="flow",
    )(conductivity, storage, recharge, west, east, strip, first, second, send, slots)


CHUNK = 16


def minmod(a, d):
    return jnp.maximum(jnp.minimum(a, d), 0.0) + jnp.minimum(jnp.maximum(a, d), 0.0)


def to_cells(lines, scratch):
    half = lines.shape[0] // 2
    count = lines.shape[1] // CHUNK
    for k in range(2):
        scratch[k] = lines[k * half : (k + 1) * half].T
    tiles = [
        jnp.concatenate([scratch[k, pl.ds(j, count, stride=CHUNK), :] for k in range(2)], 1)
        for j in range(CHUNK)
    ]
    return jnp.concatenate(tiles, 0)


def to_lines(tiles, scratch):
    half = tiles[0].shape[1] // 2
    count = tiles[0].shape[0]
    for k in range(2):
        for j, tile in enumerate(tiles):
            scratch[k, pl.ds(j, count, stride=CHUNK), :] = tile[:, k * half : (k + 1) * half]
    return [scratch[k].T for k in range(2)]


def stacked(x):
    return jnp.concatenate(split(x), 0)


def take(parts, mask):
    chosen = jnp.where(mask, 1.0, 0.0).astype(BF16)
    out = jnp.dot(parts, chosen, preferred_element_type=F32)
    count = parts.shape[0] // 3
    return (out[2 * count :] + out[count : 2 * count]) + out[:count]


def reduction(side, diagonal, right):
    count = diagonal.shape[0]
    step = 1
    while step < count:
        inverse = 1.0 / diagonal
        scaled = side * inverse
        value = right * inverse
        right = right - side * roll(value, step, 0) - roll(side * value, -step, 0)
        diagonal = diagonal - side * (side * roll(inverse, step, 0)) - roll(side * scaled, -step, 0)
        side = -side * roll(scaled, step, 0)
        step *= 2
    return right / diagonal


def tridiagonal(diagonal, right):
    off = -COUPLING
    last = CHUNK - 1
    one = jnp.ones_like(diagonal[0])
    zero = jnp.zeros_like(one)
    lead, lead_right = [one, diagonal[0]], [right[0]]
    for j in range(1, last):
        lead_right.append(right[j] * lead[j] - off * lead_right[j - 1])
        lead.append(diagonal[j] * lead[j] - (off * off) * lead[j - 1])
    trail, trail_right = {last: one, last + 1: zero}, {last: zero}
    for j in range(last - 1, -1, -1):
        trail_right[j] = right[j] * trail[j + 1] - off * trail_right[j + 1]
        trail[j] = diagonal[j] * trail[j + 1] - (off * off) * trail[j + 2]
    inverse = 1.0 / lead[last]
    sub = iota(one.shape, 0)
    top = sub == one.shape[0] - 1
    far = off * (-off) ** (last - 1)
    side = jnp.where(sub == 0, 0.0, (-off * far) * inverse)
    above = jnp.where(top, 0.0, roll(trail[1] * inverse, -1, 0))
    above_right = jnp.where(top, 0.0, roll(trail_right[0] * inverse, -1, 0))
    z = reduction(
        side,
        diagonal[last] - (off * off) * (lead[last - 1] * inverse + above),
        right[last] - off * (lead_right[last - 1] * inverse + above_right),
    )
    before = jnp.where(sub == 0, 0.0, roll(z, 1, 0))
    out = []
    for j in range(last):
        low = lead_right[j] - (off * (-off) ** j) * before
        high = off * trail_right[j + 1] + (off * (-off) ** (last - 1 - j)) * z
        out.append(inverse * (trail[j + 1] * low - lead[j] * high))
    return out + [z]


def transport(c, sorption, fluxes, west, east, lower, upper, ends):
    q_w, q_e, q_b, q_a, q_s, q_n = fluxes
    south_two, south_one, north_one, north_two = ends
    sub = iota(c[0].shape, 0)
    bottom, top = sub == 0, sub == c[0].shape[0] - 1
    before = [
        jnp.where(bottom, south_two, roll(c[-2], 1, 0)),
        jnp.where(bottom, south_one, roll(c[-1], 1, 0)),
    ]
    after = [
        jnp.where(top, north_one, roll(c[0], -1, 0)),
        jnp.where(top, north_two, roll(c[1], -1, 0)),
    ]
    line = before + c + after

    def face(q, far_left, left, right, far_right):
        rise = right - left
        positive = left + 0.5 * minmod(rise, left - far_left)
        negative = right + 0.5 * minmod(-rise, right - far_right)
        return jnp.maximum(q, 0.0) * positive + jnp.minimum(q, 0.0) * negative

    along = [face(q_s[j], *line[j : j + 4]) for j in range(CHUNK)]
    beyond = face(q_n, *line[CHUNK : CHUNK + 4])
    along.append(jnp.where(top, beyond, roll(along[0], -1, 0)))
    v = list(c)
    source = [None] * CHUNK
    diagonal, right = [None] * CHUNK, [None] * CHUNK
    for sweep in range(PICARD):
        for j in range(CHUNK):
            square = v[j] * v[j] + SOFTEN * SOFTEN
            power = (BULK_DENSITY * sorption[j]) * jnp.exp(
                (0.5 * (EXPONENT - 1.0)) * jnp.log(square)
            )
            retard = POROSITY + power
            root = jnp.sqrt(square)
            if sweep == 0:
                value = c[j]
                advect = along[j] - along[j + 1]
                advect = advect + jnp.maximum(q_w[j], 0.0) * west[j] + jnp.minimum(q_w[j], 0.0) * value
                advect = advect - jnp.maximum(q_e[j], 0.0) * value - jnp.minimum(q_e[j], 0.0) * east[j]
                advect = advect + jnp.maximum(q_b[j], 0.0) * lower[j] + jnp.minimum(q_b[j], 0.0) * value
                advect = advect - jnp.maximum(q_a[j], 0.0) * value - jnp.minimum(q_a[j], 0.0) * upper[j]
                advect = ADVECT * advect
                if j == 0:
                    advect = advect + jnp.where(bottom, COUPLING * south_one, 0.0)
                if j == CHUNK - 1:
                    advect = advect + jnp.where(top, COUPLING * north_one, 0.0)
                source[j] = POROSITY * value + power * root + advect
                right[j] = retard * value + advect
            else:
                right[j] = power * (v[j] - root) + source[j]
            diagonal[j] = retard + 2.0 * COUPLING
        v = tridiagonal(diagonal, right)
    return v


def tiles_of(x):
    count = x.shape[0] // CHUNK
    return [x[j * count : (j + 1) * count] for j in range(CHUNK)]


def both(x, at, axis):
    if axis:
        return jnp.concatenate([x[at : at + 1], x[at + 1 : at + 2]], 1)
    return jnp.concatenate([x[:, at : at + 1], x[:, at + 1 : at + 2]], 0)


def inner_neighbours(c, cols, rows, rows_x):
    own_c, own_r = both(cols, 0, 0), both(rows, 0, 1)
    at = own_r % rows_x
    parts = stacked(c)
    west = take(parts, (own_c == own_r - 1) & (at != 0))
    east = take(parts, (own_c == own_r + 1) & (at != rows_x - 1))
    lower = take(parts, own_c == own_r - rows_x)
    upper = take(parts, own_c == own_r + rows_x)
    return west, east, lower, upper


def end_values(south, north, cols, rows):
    own_r = both(rows, 0, 1)
    active = own_r >= 0
    tails = take(stacked(south), (both(cols, 6, 0) == own_r) & active)
    heads = take(stacked(north), (both(cols, 8, 0) == own_r) & active)
    return tails[0:1], tails[1:2], heads[2:3], heads[3:4]


def first_kernel(
    rows_x, layers, recv_ref, gath_ref, col_ref, row_ref,
    c_out, s_out, flux_out, edge_out, end_out, scal_out, scratch,
):
    devices = recv_ref.shape[0] // ROWS
    slots = 2 * devices
    width = recv_ref.shape[1]

    def received(at):
        return recv_ref[pl.ds(at, devices, stride=ROWS), :]

    def pair(at):
        return jnp.concatenate([received(at), received(at + 1)], 0)

    cols, rows = col_ref[...], row_ref[...]
    misc = received(8)
    sums = jnp.sum(misc, 0, keepdims=True)
    at = iota(sums.shape, 1)
    gamma, bend, curve, twist = (
        jnp.sum(jnp.where(at == 8 + i, sums, 0.0), 1, keepdims=True) for i in range(4)
    )
    alpha = gamma / bend
    gamma_next = alpha * alpha * curve - gamma
    beta = gamma_next / gamma
    cross = bend - alpha * curve
    bend_next = bend - 2.0 * alpha * curve + alpha * alpha * twist + 2.0 * beta * cross + beta * beta * bend
    alpha_next = gamma_next / bend_next
    on_d = alpha + alpha_next * (1.0 + beta)
    on_w = -alpha * alpha_next
    scal_out[...] = jnp.where(iota((8, width), 1) == 0, on_d, on_w)

    c = to_cells(pair(0), scratch.at[0])
    s = to_cells(pair(2), scratch.at[1])
    s_out[...] = s
    beside_w = to_cells(pair(4), scratch.at[2])
    beside_e = to_cells(pair(6), scratch.at[3])
    fluxes = []
    for i in range(6):
        flux = on_d * gath_ref[pl.ds(i, slots, stride=16), :]
        flux = flux + on_w * gath_ref[pl.ds(6 + i, slots, stride=16), :]
        flux = to_cells(flux, scratch.at[4 + i])
        if i == 5:
            flux = flux[width - width // CHUNK :]
            flux_out[5, : flux.shape[0]] = flux
            fluxes.append(flux)
        else:
            flux_out[i] = flux
            fluxes.append(tiles_of(flux))
    west, east, lower, upper = inner_neighbours(c, cols, rows, rows_x)
    own_c, own_r = both(cols, 0, 0), both(rows, 0, 1)
    layer, row = own_r // rows_x, own_r % rows_x
    active = own_r >= 0
    west = west + take(stacked(beside_w), (both(cols, 2, 0) == layer) & active & (row == 0))
    east = east + take(stacked(beside_e), (both(cols, 4, 0) == layer) & active & (row == rows_x - 1))
    turned = misc.T
    ends = [
        jnp.concatenate([turned[a : a + 1], turned[a + 2 : a + 3]], 1) for a in (0, 1, 4, 5)
    ] + [jnp.zeros((4, slots), F32)]
    ends = jnp.concatenate(ends, 0)
    ends = end_values(ends, ends, cols, rows)
    tiles = transport(
        tiles_of(c), tiles_of(s), fluxes, tiles_of(west), tiles_of(east), tiles_of(lower), tiles_of(upper), ends
    )
    c = jnp.concatenate(tiles, 0)
    c_out[...] = c
    count = tiles[0].shape[0]
    end_out[...] = jnp.concatenate(
        [
            tiles[-2][count - 1 :],
            tiles[-1][count - 1 :],
            tiles[0][:1],
            tiles[1][:1],
            jnp.zeros((4, slots), F32),
        ],
        0,
    )
    lane = iota((slots, width), 1)
    high = (own_c % rows_x == rows_x - 1) & (own_c // rows_x == lane)
    low = (own_c % rows_x == 0) & (own_c // rows_x + layers == lane)
    edge = take(stacked(c), (high | low) & (own_c >= 0))
    edge_out[...] = edge.T[: 2 * layers]


def first_step(received, gathered, cols, rows, layers, rows_x):
    width = received.shape[1]
    devices = cols.shape[0]
    cells = jax.ShapeDtypeStruct((width, 2 * devices), F32)
    return pl.pallas_call(
        functools.partial(first_kernel, rows_x, layers),
        out_shape=[
            cells,
            cells,
            jax.ShapeDtypeStruct((6, width, 2 * devices), F32),
            jax.ShapeDtypeStruct((2 * layers, width), F32),
            jax.ShapeDtypeStruct((8, 2 * devices), F32),
            jax.ShapeDtypeStruct((8, width), F32),
        ],
        scratch_shapes=[pltpu.VMEM((10, 2, width, devices), F32)],
        compiler_params=params(16),
        name="first_step",
    )(received, gathered, cols, rows)


def second_kernel(
    rows_x, c_ref, s_ref, flux_ref, col_ref, row_ref, edge1_ref, edge2_ref, end1_ref, end2_ref, out_ref, scratch
):
    c, s = c_ref[...], s_ref[...]
    width = c.shape[0]
    devices = c.shape[1] // 2
    cols, rows = col_ref[...], row_ref[...]
    west, east, lower, upper = inner_neighbours(c, cols, rows, rows_x)
    west_edge, east_edge = from_turns("gx", edge1_ref[...], edge2_ref[...])
    layers = west_edge.shape[0] // 2
    own_r = both(rows, 0, 1)
    layer, row = own_r // rows_x, own_r % rows_x
    active = own_r >= 0
    code = iota((width, 2 * devices), 0)
    rest = jnp.zeros((width - 2 * layers, width), F32)
    west_edge = jnp.concatenate([west_edge, rest], 0).T
    east_edge = jnp.concatenate([east_edge, rest], 0).T
    west = west + take(stacked(west_edge), (code == layer) & active & (row == 0))
    east = east + take(stacked(east_edge), (code == layer + layers) & active & (row == rows_x - 1))
    south, north = from_turns("gy", end1_ref[...], end2_ref[...])
    ends = end_values(south, north, cols, rows)
    fluxes = [tiles_of(flux_ref[i]) for i in range(5)] + [flux_ref[5, : width // CHUNK]]
    tiles = transport(
        tiles_of(c), tiles_of(s), fluxes, tiles_of(west), tiles_of(east), tiles_of(lower), tiles_of(upper), ends
    )
    for k, lines in enumerate(to_lines(tiles, scratch)):
        out_ref[pl.ds(k, devices, stride=2), :] = lines


def second_step(c, s, fluxes, cols, rows, edges, ends, rows_x):
    width, slots = c.shape
    return pl.pallas_call(
        functools.partial(second_kernel, rows_x),
        out_shape=jax.ShapeDtypeStruct((slots, width), F32),
        scratch_shapes=[pltpu.VMEM((2, width, slots // 2), F32)],
        compiler_params=params(16),
        name="second_step",
    )(c, s, fluxes, cols, rows, *edges, *ends)


def owner_kernel(lines, ids_ref, recv_ref, out_ref):
    devices, owned = ids_ref.shape
    own = ids_ref[pl.ds(place(), 1), :]
    brick = own // lines
    brick_col = column(brick.astype(F32)).astype(jnp.int32)
    square = (owned, owned)
    same = (brick_col == brick) & (iota(square, 1) < iota(square, 0))
    rank = jnp.sum(jnp.where(same, 1.0, 0.0), 1, keepdims=True).astype(jnp.int32)
    mask = brick_col * 2 + rank == iota((owned, 2 * devices), 1)
    out_ref[...] = pick(mask, split(recv_ref[...]))


def to_owner(ids, received, lines):
    return pl.pallas_call(
        functools.partial(owner_kernel, lines),
        out_shape=jax.ShapeDtypeStruct((ids.shape[1], received.shape[1]), F32),
        compiler_params=params(16),
        name="to_owner",
    )(ids, received)


def body(conductivity, storage, recharge, block_ids, neighbours, concentration, sorption):
    layers, rows_x, width = conductivity.shape
    devices = lax.axis_size(AXES)
    owned = concentration.shape[0]
    ids = block_ids.reshape(devices, owned)
    first, second, conductivity, storage, recharge, ids, concentration, sorption = load(
        conductivity, storage, recharge, ids, concentration, sorption
    )
    first, second = swap("gx", first, second)
    inner, send, cols, rows = prepare(conductivity, storage, recharge, ids, concentration, sorption)
    strip, west, east = pack_strip(inner, first, second)
    first, second = swap("gy", strip, strip)
    base, image, gathered, send = flow(
        conductivity, storage, recharge, west, east, strip, first, second, send, rows[:2]
    )
    received = lax.all_to_all(
        send.reshape(devices, 1, ROWS * width), AXES, split_axis=0, concat_axis=0, tiled=True
    ).reshape(devices * ROWS, width)
    c, s, flux, edge, end, scal = first_step(received, gathered, cols, rows, layers, rows_x)
    edges = swap("gx", edge, edge)
    ends = swap("gy", end, end)
    head = scal[0, 0] * base + scal[0, 1] * image
    result = second_step(c, s, flux, cols, rows, edges, ends, rows_x)
    returned = lax.all_to_all(
        result.reshape(devices, 2, width), AXES, split_axis=0, concat_axis=0, tiled=True
    ).reshape(devices * 2, width)
    return head, to_owner(ids, returned, layers * rows_x)


def solution(mesh):
    return jax.shard_map(
        body,
        mesh=mesh,
        in_specs=(
            P(None, "gx", "gy"),
            P(None, "gx", "gy"),
            P(None, "gx", "gy"),
            P(),
            P(("gx", "gy"), None),
            P(("gx", "gy"), None),
            P(("gx", "gy"), None),
        ),
        out_specs=(P(None, "gx", "gy"), P(("gx", "gy"), None)),
        check_vma=False,
    )
```

```python
import functools

import jax
import jax.numpy as jnp
from jax import lax
from jax.experimental import pallas as pl
from jax.experimental.pallas import tpu as pltpu
from jax.sharding import PartitionSpec as P

PICARD = 3
POROSITY = 0.35
BULK_DENSITY = 1.6
EXPONENT = 0.7
SOFTEN = 0.05
DISPERSION = 0.5
TIME_STEP = 0.1
ADVECT = 1.0
VERTICAL = 2.0
COUPLING = TIME_STEP * DISPERSION

AXES = ("gx", "gy")
ROWS = 9
NONE = -5000
F32 = jnp.float32
BF16 = jnp.bfloat16


def params(mib):
    return pltpu.CompilerParams(vmem_limit_bytes=int(mib * 1024 * 1024))


def iota(shape, dim):
    return lax.broadcasted_iota(jnp.int32, shape, dim)


def roll(x, shift, axis):
    return pltpu.roll(x, shift % x.shape[axis] if isinstance(shift, int) else shift, axis)


def split(x):
    high = x.astype(BF16)
    rest = x - high.astype(F32)
    middle = rest.astype(BF16)
    low = (rest - middle.astype(F32)).astype(BF16)
    return high, middle, low


def pick(mask, parts):
    chosen = jnp.where(mask, 1.0, 0.0).astype(BF16)
    high, middle, low = (jnp.dot(chosen, part, preferred_element_type=F32) for part in parts)
    return (low + middle) + high


def rows_of(parts, start, stop):
    return tuple(part[start:stop] for part in parts)


def place():
    across = lax.axis_size("gy")
    return lax.axis_index("gx") * across + lax.axis_index("gy")


def by_turns(axis, low, high):
    odd = jnp.full(low.shape, lax.axis_index(axis) % 2) == 1
    return jnp.where(odd, low, high), jnp.where(odd, high, low)


def from_turns(axis, first, second):
    at = jnp.full(first.shape, lax.axis_index(axis))
    odd = at % 2 == 1
    low = jnp.where(at == 0, 0.0, jnp.where(odd, first, second))
    high = jnp.where(at == lax.axis_size(axis) - 1, 0.0, jnp.where(odd, second, first))
    return low, high


def swap(axis, first, second):
    count = lax.axis_size(axis)
    one = [(i, i ^ 1) for i in range(count)]
    other = [(i, (i + 1 if i % 2 else i - 1) % count) for i in range(count)]
    return lax.ppermute(first, axis, one), lax.ppermute(second, axis, other)


HBM = pl.BlockSpec(memory_space=pltpu.HBM)
SMEM = pl.BlockSpec(memory_space=pltpu.SMEM)
VMEM = pl.BlockSpec(memory_space=pltpu.VMEM)


def fetch(pairs, sems):
    copies = [pltpu.make_async_copy(src, dst, sems.at[i]) for i, (src, dst) in enumerate(pairs)]
    for copy in copies:
        copy.start()
    return copies


def pinned(arrays):
    return tuple(pltpu.with_memory_space_constraint(x, pltpu.HBM) for x in arrays)


def edges_kernel(k_hbm, s_hbm, r_hbm, first_ref, second_ref, tiles, sems):
    rows = k_hbm.shape[1]
    pairs = []
    for i, ref in enumerate((k_hbm, s_hbm, r_hbm)):
        pairs.append((ref.at[:, pl.ds(rows - 8, 8), :], tiles.at[2 * i]))
        pairs.append((ref.at[:, pl.ds(0, 8), :], tiles.at[2 * i + 1]))
    for copy in fetch(pairs, sems):
        copy.wait()
    sub = iota(first_ref.shape[1:], 0)
    for z in range(first_ref.shape[0]):
        east = jnp.where(
            sub >= 5,
            tiles[0, z],
            jnp.where(sub >= 3, roll(tiles[2, z], -3, 0), roll(tiles[4, z], -5, 0)),
        )
        west = jnp.where(
            sub < 3,
            tiles[1, z],
            jnp.where(sub < 5, roll(tiles[3, z], 3, 0), roll(tiles[5, z], 5, 0)),
        )
        first_ref[z], second_ref[z] = by_turns("gx", west, east)


def pack_edges(*arrays):
    layers, rows, width = arrays[0].shape
    tile = jax.ShapeDtypeStruct((layers, 8, width), F32)
    return pl.pallas_call(
        edges_kernel,
        in_specs=[HBM] * 3,
        out_specs=[VMEM] * 2,
        out_shape=[tile, tile],
        scratch_shapes=[pltpu.VMEM((6, layers, 8, width), F32), pltpu.SemaphoreType.DMA((6,))],
        compiler_params=params(8),
        name="pack_edges",
    )(*pinned(arrays))


def beside(index, z, west_ref, east_ref):
    shift = (0, 3, 5)[index]
    top, bottom = west_ref[z], east_ref[z]
    if shift:
        top, bottom = roll(top, shift, 0), roll(bottom, -shift, 0)
    return top, bottom


def widened(index, z, own_ref, west_ref, east_ref):
    top, bottom = beside(index, z, west_ref, east_ref)
    return jnp.concatenate([top, own_ref[z], bottom], 0)


def strip_of(layers, layer):
    strip = None
    for z in range(layers):
        turned = roll(layer(z), z * 8 + 4, 1)
        strip = turned if strip is None else jnp.where(iota(turned.shape, 1) >= z * 8, turned, strip)
    return strip


def strip_kernel(inner_ref, first_ref, second_ref, out_ref, west_ref, east_ref, one_ref, other_ref):
    layers = west_ref.shape[0]
    west_ref[...], east_ref[...] = from_turns("gx", first_ref[...], second_ref[...])
    rows = inner_ref.shape[1]
    for index in range(3):
        out_ref[index, 8 : 8 + rows] = inner_ref[index]
        out_ref[index, 0:8] = strip_of(layers, lambda z: beside(index, z, west_ref, east_ref)[0])
        out_ref[index, 8 + rows :] = strip_of(layers, lambda z: beside(index, z, west_ref, east_ref)[1])
    k, s, r = out_ref[0], out_ref[1], out_ref[2]
    slot = iota(k.shape, 1) % 8
    south = jnp.where(slot >= 4, k, jnp.where(slot >= 2, roll(s, -2, 1), roll(r, -4, 1)))
    north = jnp.where(slot < 4, k, jnp.where(slot < 6, roll(s, 2, 1), roll(r, 4, 1)))
    one_ref[...], other_ref[...] = by_turns("gy", south, north)


def pack_strip(inner, first, second):
    rows, width = inner.shape[1:]
    tile = jax.ShapeDtypeStruct(first.shape, F32)
    return pl.pallas_call(
        strip_kernel,
        out_shape=[jax.ShapeDtypeStruct((3, rows + 16, width), F32), tile, tile]
        + [jax.ShapeDtypeStruct((rows + 16, width), F32)] * 2,
        compiler_params=params(4),
        name="pack_strip",
    )(inner, first, second)


def column(row):
    n = row.shape[1]
    return jnp.sum(jnp.where(iota((n, n), 0) == iota((n, n), 1), row, 0.0), 1, keepdims=True)


def as_row(col):
    n = col.shape[0]
    return jnp.sum(jnp.where(iota((n, n), 0) == iota((n, n), 1), col, 0.0), 0, keepdims=True)


def slot_codes(ids, target, lines):
    brick = ids // lines
    key = iota(ids.shape, 1) * lines + ids % lines
    mine = brick == target
    first = jnp.min(jnp.where(mine, key, ids.shape[1] * lines).astype(F32), 1, keepdims=True)
    second = jnp.max(jnp.where(mine, key, -1).astype(F32), 1, keepdims=True)
    cols = [
        jnp.where(second >= 0.0, code.astype(jnp.int32) % lines, NONE).astype(F32)
        for code in (first, second)
    ]
    rows = [as_row(col) for col in cols]
    return jnp.concatenate(cols, 0).astype(jnp.int32), jnp.concatenate(rows, 1).astype(jnp.int32)


def load_kernel(
    down, across,
    k_hbm, s_hbm, r_hbm, ids_hbm, conc_hbm, sorp_hbm,
    k_ref, s_ref, r_ref, ids_ref, conc_ref, sorp_ref, own_ref,
    inner_ref, ends_ref, sides_ref, edges_ref, pick_ref, slots_ref,
    sems,
):
    refs = (k_ref, s_ref, r_ref)
    copies = fetch(
        [
            (ids_hbm, ids_ref),
            (k_hbm, k_ref),
            (s_hbm, s_ref),
            (r_hbm, r_ref),
            (conc_hbm, conc_ref),
            (sorp_hbm, sorp_ref),
        ],
        sems,
    )
    layers, rows_x = k_ref.shape[:2]
    slots = slots_ref.shape[1]
    lines = layers * rows_x
    me = place()
    gx, gy = me // across, me % across
    copies[0].wait()
    ids = ids_ref[...]
    code, slot = slot_codes(ids, me, lines)
    west, _ = slot_codes(ids, jnp.where(gx > 0, me - across, -1), lines)
    east, _ = slot_codes(ids, jnp.where(gx < down - 1, me + across, -1), lines)
    south, _ = slot_codes(ids, jnp.where(gy > 0, me - 1, -1), lines)
    north, _ = slot_codes(ids, jnp.where(gy < across - 1, me + 1, -1), lines)
    slots_ref[...] = slot
    active = slot >= 0
    layer, row = slot // rows_x, slot % rows_x
    low, high = active & (row == 0), active & (row == rows_x - 1)

    def ones(mask):
        return jnp.where(mask, 1.0, 0.0).astype(BF16)

    inner_ref[:, :slots] = ones((code == slot - 1) & (row != 0))
    inner_ref[:, slots : 2 * slots] = ones((code == slot + 1) & (row != rows_x - 1))
    inner_ref[:, 2 * slots : 3 * slots] = ones(code == slot - rows_x)
    inner_ref[:, 3 * slots :] = ones(code == slot + rows_x)
    ends_ref[:, :slots] = ones((south == slot) & active)
    ends_ref[:, slots:] = ones((north == slot) & active)
    sides_ref[:, :slots] = ones((west == slot + rows_x - 1) & low)
    sides_ref[:, slots:] = ones((east == slot - rows_x + 1) & high)
    at = iota((edges_ref.shape[0], slots), 0)
    edges_ref[:, :slots] = ones((at == layer) & low)
    edges_ref[:, slots:] = ones((at == layer + layers) & high)
    at = iota((slots, pick_ref.shape[1]), 1)
    pick_ref[...] = ones(
        (code >= 0)
        & (
            ((code % rows_x == rows_x - 1) & (code // rows_x == at))
            | ((code % rows_x == 0) & (code // rows_x + layers == at))
        )
    )
    for index, ref in enumerate(refs):
        copies[1 + index].wait()
        own_ref[index] = strip_of(layers, lambda z: ref[z])
    copies[4].wait()
    copies[5].wait()


def load(*arrays):
    rows, width = arrays[0].shape[1:]
    layers = arrays[0].shape[0]
    slots = 2 * arrays[3].shape[0]
    kernel = functools.partial(load_kernel, lax.axis_size("gx"), lax.axis_size("gy"))
    return pl.pallas_call(
        kernel,
        in_specs=[HBM] * 6,
        out_specs=[VMEM] * 13,
        out_shape=[jax.ShapeDtypeStruct(x.shape, x.dtype) for x in arrays]
        + [
            jax.ShapeDtypeStruct((3, rows, width), F32),
            jax.ShapeDtypeStruct((slots, 4 * slots), BF16),
            jax.ShapeDtypeStruct((slots, 2 * slots), BF16),
            jax.ShapeDtypeStruct((slots, 2 * slots), BF16),
            jax.ShapeDtypeStruct((2 * layers, 2 * slots), BF16),
            jax.ShapeDtypeStruct((slots, width), BF16),
            jax.ShapeDtypeStruct((1, slots), jnp.int32),
        ],
        scratch_shapes=[pltpu.SemaphoreType.DMA((6,))],
        compiler_params=params(8),
        name="load",
    )(*pinned(arrays))


def send_kernel(
    across, rows_x, layers, ids_ref, conc_ref, sorp_ref, out_ref, mask_ref
):
    devices, owned = ids_ref.shape
    lines = layers * rows_x
    me = place()
    own = ids_ref[pl.ds(me, 1), :]
    own_brick = own // lines
    own_row = own % lines % rows_x
    brick_col = column(own_brick.astype(F32)).astype(jnp.int32)
    square = (owned, owned)
    same = (brick_col == own_brick) & (iota(square, 0) < iota(square, 1))
    rank = jnp.sum(jnp.where(same, 1.0, 0.0), 0, keepdims=True).astype(jnp.int32)
    back = jnp.where(iota((2 * devices, owned), 0) == own_brick * 2 + rank, 1.0, 0.0)
    mask_ref[...] = back.T.astype(BF16)
    dest = iota((devices, owned), 0)
    conc = conc_ref[...]
    conc_parts = split(conc)
    sorp_parts = split(sorp_ref[...])
    lane = iota((owned, conc.shape[1]), 1)
    misc = jnp.zeros((devices, conc.shape[1]), F32)
    for k in range(2):
        ranked = rank == k
        home = (dest == own_brick) & ranked
        out_ref[pl.ds(k, devices, stride=ROWS), :] = pick(home, conc_parts)
        out_ref[pl.ds(2 + k, devices, stride=ROWS), :] = pick(home, sorp_parts)
        after = (dest == own_brick + across) & ranked & (own_row == rows_x - 1)
        out_ref[pl.ds(4 + k, devices, stride=ROWS), :] = pick(after, conc_parts)
        before = (dest == own_brick - across) & ranked & (own_row == 0)
        out_ref[pl.ds(6 + k, devices, stride=ROWS), :] = pick(before, conc_parts)
        tails = jnp.where(lane // 2 == k, roll(conc, 2 + 2 * k, 1), 0.0)
        heads = jnp.where(lane // 2 == 2 + k, roll(conc, 4 + 2 * k, 1), 0.0)
        north = (dest == own_brick + 1) & ranked & (own_brick % across < across - 1)
        south = (dest == own_brick - 1) & ranked & (own_brick % across > 0)
        misc = misc + pick(north, split(tails)) + pick(south, split(heads))
    out_ref[pl.ds(8, devices, stride=ROWS), :] = misc


def pack_send(ids, concentration, sorption, layers, rows_x):
    devices, owned = ids.shape
    width = concentration.shape[1]
    slots = 2 * devices
    kernel = functools.partial(send_kernel, lax.axis_size("gy"), rows_x, layers)
    return pl.pallas_call(
        kernel,
        out_shape=[
            jax.ShapeDtypeStruct((devices * ROWS, width), F32),
            jax.ShapeDtypeStruct((owned, slots), BF16),
        ],
        compiler_params=params(8),
        name="pack_send",
    )(ids, concentration, sorption)


def harmonic(a, c):
    return jnp.where(jnp.minimum(a, c) > 0.0, 2.0 * a * c / (a + c), jnp.maximum(a, c))


def faces_kernel(k_ref, s_ref, west_ref, east_ref, fw, fs, fb, part):
    layers, rows, width = k_ref.shape
    shape = (rows + 16, width)
    lane = iota(shape, 1)
    fb[0] = jnp.zeros(shape, F32)

    def step(z, carry):
        k = widened(0, z, k_ref, west_ref, east_ref)
        face_w = harmonic(k, roll(k, 1, 0))
        face_s = jnp.where(lane == 0, 0.0, harmonic(k, roll(k, 1, 1)))
        upper = widened(0, jnp.minimum(z + 1, layers - 1), k_ref, west_ref, east_ref)
        face_a = jnp.where(z < layers - 1, VERTICAL * harmonic(k, upper), 0.0)
        s = widened(1, z, s_ref, west_ref, east_ref)
        fw[z] = face_w
        fs[z] = face_s
        part[z] = s + face_w + roll(face_w, -1, 0) + face_s + roll(face_s, -1, 1) + fb[z] + face_a
        fb[z + 1] = face_a
        return carry

    lax.fori_loop(0, layers, step, 0, unroll=2)


def faces_of(conductivity, storage, west, east):
    layers, rows, width = conductivity.shape
    tall = jax.ShapeDtypeStruct((layers, rows + 16, width), F32)
    return pl.pallas_call(
        faces_kernel,
        out_shape=[tall, tall, jax.ShapeDtypeStruct((layers + 1, rows + 16, width), F32), tall],
        compiler_params=params(8),
        name="faces",
    )(conductivity, storage, west, east)


def flow_kernel(
    k_ref, s_ref, r_ref, west_ref, east_ref, strip_ref, first_ref, second_ref, send_ref, slots_ref,
    fw, fs, fb, part,
    d_out, w_out, gath_out, send_out,
    rd, dd, ww, lines_ref,
):
    layers, rows, width = k_ref.shape
    tall = rows + 16
    shape = (tall, width)
    lane = iota(shape, 1)
    slot = lane % 8
    devices = send_ref.shape[0] // ROWS

    send_out[...] = send_ref[...]

    def side(low):
        def joined(index):
            south, north = from_turns("gy", first_ref[...], second_ref[...])
            shift = 2 * index
            if low:
                return jnp.where(slot < 4, roll(south, -shift, 1), strip_ref[index])
            return jnp.where(slot < 4, strip_ref[index], roll(north, shift, 1))

        k, s, r = joined(0), joined(1), joined(2)
        face_w = harmonic(k, roll(k, 1, 0))
        face_s = harmonic(k, roll(k, 1, 1))
        face_b = jnp.where(lane >= 8, VERTICAL * harmonic(k, roll(k, 8, 1)), 0.0)
        diagonal = (
            s + face_w + roll(face_w, -1, 0) + face_s + roll(face_s, -1, 1) + face_b + roll(face_b, -8, 1)
        )
        inverse = jnp.where(k > 0.0, 1.0 / diagonal, 0.0)
        d = r * inverse
        flux_w = face_w * (roll(d, 1, 0) - d)
        flux_s = face_s * (roll(d, 1, 1) - d)
        flux_b = face_b * (roll(d, 8, 1) - d)
        image = (
            s * d
            + (roll(flux_w, -1, 0) - flux_w)
            + (roll(flux_s, -1, 1) - flux_s)
            + (roll(flux_b, -8, 1) - flux_b)
        )
        w = image * inverse
        return face_s, flux_s, face_s * (roll(w, 1, 1) - w)

    low_face, low_d, low_w = side(True)
    high_face, high_d, high_w = side(False)

    def with_low(z, field, strip):
        return jnp.where(lane == 0, roll(strip, width - 4 - z * 8, 1), field)

    def north_of(z, field, strip):
        shift = lax.rem(width - 5 + width - z * 8, width)
        return jnp.where(lane == width - 1, roll(strip, shift, 1), roll(field, -1, 1))

    def scale(z, carry):
        k = widened(0, z, k_ref, west_ref, east_ref)
        r = widened(2, z, r_ref, west_ref, east_ref)
        low = jnp.where(lane == 0, roll(low_face, width - 4 - z * 8, 1), 0.0)
        shift = lax.rem(width - 5 + width - z * 8, width)
        high = jnp.where(lane == width - 1, roll(high_face, shift, 1), 0.0)
        diagonal = part[z] + low + high
        inverse = jnp.where(k > 0.0, 1.0 / diagonal, 0.0)
        rd[z] = inverse
        dd[z] = r * inverse
        return carry

    lax.fori_loop(0, layers, scale, 0, unroll=8)

    def total(x):
        return jnp.sum(x[8 : 8 + rows].reshape(rows // 8, 8, width), 0)

    def apply(z, field, low, high, block):
        h = field[z]
        below = field[jnp.maximum(z - 1, 0)]
        above = field[jnp.minimum(z + 1, layers - 1)]
        flux_w = fw[z] * (roll(h, 1, 0) - h)
        flux_e = roll(flux_w, -1, 0)
        flux_b = fb[z] * (below - h)
        flux_a = fb[z + 1] * (h - above)
        flux_s = with_low(z, fs[z] * (roll(h, 1, 1) - h), low)
        flux_n = north_of(z, flux_s, high)
        for at, flux in enumerate((flux_w, flux_e, flux_b, flux_a, flux_s, flux_n)):
            start = z * (rows * 16) + (block + at)
            lines_ref[pl.ds(start, rows, stride=16), :] = flux[8 : 8 + rows]
        s = widened(1, z, s_ref, west_ref, east_ref)
        return h, s * h + (flux_e - flux_w) + (flux_a - flux_b) + (flux_n - flux_s)

    zero = jnp.zeros((8, width), F32)

    def first(z, sums):
        d, image = apply(z, dd, low_d, high_d, 0)
        w = image * rd[z]
        ww[z] = w
        d_out[z] = d[8 : 8 + rows]
        w_out[z] = w[8 : 8 + rows]
        r = r_ref[z]
        gamma = jnp.sum((r * d[8 : 8 + rows]).reshape(rows // 8, 8, width), 0)
        return sums[0] + gamma, sums[1] + total(d * image), sums[2] + total(image * w)

    gamma, bend, curve = lax.fori_loop(0, layers, first, (zero, zero, zero), unroll=8)

    def second(z, acc):
        w, image = apply(z, ww, low_w, high_w, 6)
        return acc + total(w * image)

    twist = lax.fori_loop(0, layers, second, zero, unroll=8)
    lane_row = iota((devices, width), 1)
    misc = send_ref[pl.ds(8, devices, stride=ROWS), :]
    for at, part in enumerate((gamma, bend, curve, twist)):
        value = jnp.sum(jnp.sum(part, 0, keepdims=True), 1, keepdims=True)
        misc = jnp.where(lane_row == 8 + at, value, misc)
    send_out[pl.ds(8, devices, stride=ROWS), :] = misc
    for k in range(2):

        def gather(i, carry):
            line = pl.multiple_of(jnp.maximum(slots_ref[0, k * devices + i], 0) * 16, 16)
            slot = pl.multiple_of((k * devices + i) * 16, 16)
            gath_out[pl.ds(slot, 16), :] = lines_ref[pl.ds(line, 16), :]
            return carry

        lax.fori_loop(0, devices, gather, 0, unroll=8)


def flow(conductivity, storage, recharge, west, east, strip, first, second, send, slots, faces):
    layers, rows, width = conductivity.shape
    tall = pltpu.VMEM((layers, rows + 16, width), F32)
    return pl.pallas_call(
        flow_kernel,
        out_shape=[
            jax.ShapeDtypeStruct(conductivity.shape, F32),
            jax.ShapeDtypeStruct(conductivity.shape, F32),
            jax.ShapeDtypeStruct((slots.shape[1] * 16, width), F32),
            jax.ShapeDtypeStruct(send.shape, F32),
        ],
        in_specs=[VMEM] * 9 + [SMEM] + [VMEM] * 4,
        out_specs=[VMEM] * 4,
        scratch_shapes=[tall] * 3 + [pltpu.VMEM((layers * rows * 16, width), F32)],
        compiler_params=params(20),
        name="flow",
    )(conductivity, storage, recharge, west, east, strip, first, second, send, slots, *faces)


CHUNK = 16


def minmod(a, d):
    return jnp.maximum(jnp.minimum(a, d), 0.0) + jnp.minimum(jnp.maximum(a, d), 0.0)


def to_cells(lines, scratch):
    half = lines.shape[0] // 2
    count = lines.shape[1] // CHUNK
    for k in range(2):
        scratch[k] = lines[k * half : (k + 1) * half].T
    tiles = [
        jnp.concatenate([scratch[k, pl.ds(j, count, stride=CHUNK), :] for k in range(2)], 1)
        for j in range(CHUNK)
    ]
    return jnp.concatenate(tiles, 0)


def to_lines(tiles, scratch):
    half = tiles[0].shape[1] // 2
    count = tiles[0].shape[0]
    for k in range(2):
        for j, tile in enumerate(tiles):
            scratch[k, pl.ds(j, count, stride=CHUNK), :] = tile[:, k * half : (k + 1) * half]
    return [scratch[k].T for k in range(2)]


def stacked(x):
    return jnp.concatenate(split(x), 0)


def take(parts, chosen):
    out = jnp.dot(parts, chosen, preferred_element_type=F32)
    count = parts.shape[0] // 3
    return (out[2 * count :] + out[count : 2 * count]) + out[:count]


def reduction(side, diagonal, right):
    count = diagonal.shape[0]
    step = 1
    while step < count:
        inverse = 1.0 / diagonal
        scaled = side * inverse
        value = right * inverse
        right = right - side * roll(value, step, 0) - roll(side * value, -step, 0)
        diagonal = diagonal - side * (side * roll(inverse, step, 0)) - roll(side * scaled, -step, 0)
        side = -side * roll(scaled, step, 0)
        step *= 2
    return right / diagonal


def tridiagonal(diagonal, right):
    off = -COUPLING
    last = CHUNK - 1
    one = jnp.ones_like(diagonal[0])
    zero = jnp.zeros_like(one)
    lead, lead_right = [one, diagonal[0]], [right[0]]
    for j in range(1, last):
        lead_right.append(right[j] * lead[j] - off * lead_right[j - 1])
        lead.append(diagonal[j] * lead[j] - (off * off) * lead[j - 1])
    trail, trail_right = {last: one, last + 1: zero}, {last: zero}
    for j in range(last - 1, -1, -1):
        trail_right[j] = right[j] * trail[j + 1] - off * trail_right[j + 1]
        trail[j] = diagonal[j] * trail[j + 1] - (off * off) * trail[j + 2]
    inverse = 1.0 / lead[last]
    sub = iota(one.shape, 0)
    top = sub == one.shape[0] - 1
    far = off * (-off) ** (last - 1)
    side = jnp.where(sub == 0, 0.0, (-off * far) * inverse)
    above = jnp.where(top, 0.0, roll(trail[1] * inverse, -1, 0))
    above_right = jnp.where(top, 0.0, roll(trail_right[0] * inverse, -1, 0))
    z = reduction(
        side,
        diagonal[last] - (off * off) * (lead[last - 1] * inverse + above),
        right[last] - off * (lead_right[last - 1] * inverse + above_right),
    )
    before = jnp.where(sub == 0, 0.0, roll(z, 1, 0))
    out = []
    for j in range(last):
        low = lead_right[j] - (off * (-off) ** j) * before
        high = off * trail_right[j + 1] + (off * (-off) ** (last - 1 - j)) * z
        out.append(inverse * (trail[j + 1] * low - lead[j] * high))
    return out + [z]


def transport(c, sorption, fluxes, west, east, lower, upper, ends):
    q_w, q_e, q_b, q_a, q_s, q_n = fluxes
    south_two, south_one, north_one, north_two = ends
    sub = iota(c[0].shape, 0)
    bottom, top = sub == 0, sub == c[0].shape[0] - 1
    before = [
        jnp.where(bottom, south_two, roll(c[-2], 1, 0)),
        jnp.where(bottom, south_one, roll(c[-1], 1, 0)),
    ]
    after = [
        jnp.where(top, north_one, roll(c[0], -1, 0)),
        jnp.where(top, north_two, roll(c[1], -1, 0)),
    ]
    line = before + c + after

    def face(q, far_left, left, right, far_right):
        rise = right - left
        positive = left + 0.5 * minmod(rise, left - far_left)
        negative = right + 0.5 * minmod(-rise, right - far_right)
        return jnp.maximum(q, 0.0) * positive + jnp.minimum(q, 0.0) * negative

    along = [face(q_s[j], *line[j : j + 4]) for j in range(CHUNK)]
    beyond = face(q_n, *line[CHUNK : CHUNK + 4])
    along.append(jnp.where(top, beyond, roll(along[0], -1, 0)))
    v = list(c)
    source = [None] * CHUNK
    diagonal, right = [None] * CHUNK, [None] * CHUNK
    for sweep in range(PICARD):
        for j in range(CHUNK):
            square = v[j] * v[j] + SOFTEN * SOFTEN
            power = (BULK_DENSITY * sorption[j]) * jnp.exp(
                (0.5 * (EXPONENT - 1.0)) * jnp.log(square)
            )
            retard = POROSITY + power
            root = jnp.sqrt(square)
            if sweep == 0:
                value = c[j]
                advect = along[j] - along[j + 1]
                advect = advect + jnp.maximum(q_w[j], 0.0) * west[j] + jnp.minimum(q_w[j], 0.0) * value
                advect = advect - jnp.maximum(q_e[j], 0.0) * value - jnp.minimum(q_e[j], 0.0) * east[j]
                advect = advect + jnp.maximum(q_b[j], 0.0) * lower[j] + jnp.minimum(q_b[j], 0.0) * value
                advect = advect - jnp.maximum(q_a[j], 0.0) * value - jnp.minimum(q_a[j], 0.0) * upper[j]
                advect = ADVECT * advect
                if j == 0:
                    advect = advect + jnp.where(bottom, COUPLING * south_one, 0.0)
                if j == CHUNK - 1:
                    advect = advect + jnp.where(top, COUPLING * north_one, 0.0)
                source[j] = POROSITY * value + power * root + advect
                right[j] = retard * value + advect
            else:
                right[j] = power * (v[j] - root) + source[j]
            diagonal[j] = retard + 2.0 * COUPLING
        v = tridiagonal(diagonal, right)
    return v


def tiles_of(x):
    count = x.shape[0] // CHUNK
    return [x[j * count : (j + 1) * count] for j in range(CHUNK)]


def inner_neighbours(c, chosen):
    slots = c.shape[1]
    values = take(stacked(c), chosen)
    return [values[:, i * slots : (i + 1) * slots] for i in range(4)]


def end_values(south, north, chosen):
    slots = south.shape[1]
    tails = take(stacked(south), chosen[:, :slots])
    heads = take(stacked(north), chosen[:, slots:])
    return tails[0:1], tails[1:2], heads[2:3], heads[3:4]


def first_kernel(
    recv_ref, gath_ref, inner_ref, ends_ref, sides_ref, pick_ref,
    c_out, s_out, flux_out, edge_out, end_out, scal_out, scratch,
):
    devices = recv_ref.shape[0] // ROWS
    slots = 2 * devices
    width = recv_ref.shape[1]

    def received(at):
        return recv_ref[pl.ds(at, devices, stride=ROWS), :]

    def pair(at):
        return jnp.concatenate([received(at), received(at + 1)], 0)

    misc = received(8)
    sums = jnp.sum(misc, 0, keepdims=True)
    at = iota(sums.shape, 1)
    gamma, bend, curve, twist = (
        jnp.sum(jnp.where(at == 8 + i, sums, 0.0), 1, keepdims=True) for i in range(4)
    )
    alpha = gamma / bend
    gamma_next = alpha * alpha * curve - gamma
    beta = gamma_next / gamma
    cross = bend - alpha * curve
    bend_next = bend - 2.0 * alpha * curve + alpha * alpha * twist + 2.0 * beta * cross + beta * beta * bend
    alpha_next = gamma_next / bend_next
    on_d = alpha + alpha_next * (1.0 + beta)
    on_w = -alpha * alpha_next
    scal_out[...] = jnp.where(iota((8, width), 1) == 0, on_d, on_w)

    c = to_cells(pair(0), scratch.at[0])
    s = to_cells(pair(2), scratch.at[1])
    s_out[...] = s
    beside_w = to_cells(pair(4), scratch.at[2])
    beside_e = to_cells(pair(6), scratch.at[3])
    fluxes = []
    for i in range(6):
        flux = on_d * gath_ref[pl.ds(i, slots, stride=16), :]
        flux = flux + on_w * gath_ref[pl.ds(6 + i, slots, stride=16), :]
        flux = to_cells(flux, scratch.at[4 + i])
        if i == 5:
            flux = flux[width - width // CHUNK :]
            flux_out[5, : flux.shape[0]] = flux
            fluxes.append(flux)
        else:
            flux_out[i] = flux
            fluxes.append(tiles_of(flux))
    west, east, lower, upper = inner_neighbours(c, inner_ref[...])
    west = west + take(stacked(beside_w), sides_ref[:, :slots])
    east = east + take(stacked(beside_e), sides_ref[:, slots:])
    turned = misc.T
    ends = [
        jnp.concatenate([turned[a : a + 1], turned[a + 2 : a + 3]], 1) for a in (0, 1, 4, 5)
    ] + [jnp.zeros((4, slots), F32)]
    ends = jnp.concatenate(ends, 0)
    ends = end_values(ends, ends, ends_ref[...])
    tiles = transport(
        tiles_of(c), tiles_of(s), fluxes, tiles_of(west), tiles_of(east), tiles_of(lower), tiles_of(upper), ends
    )
    c = jnp.concatenate(tiles, 0)
    c_out[...] = c
    count = tiles[0].shape[0]
    end_out[...] = jnp.concatenate(
        [
            tiles[-2][count - 1 :],
            tiles[-1][count - 1 :],
            tiles[0][:1],
            tiles[1][:1],
            jnp.zeros((4, slots), F32),
        ],
        0,
    )
    edge = take(stacked(c), pick_ref[...])
    edge_out[...] = edge.T[: edge_out.shape[0]]


def first_step(received, gathered, inner, ends, sides, picks, layers):
    width = received.shape[1]
    slots = inner.shape[0]
    cells = jax.ShapeDtypeStruct((width, slots), F32)
    return pl.pallas_call(
        first_kernel,
        out_shape=[
            cells,
            cells,
            jax.ShapeDtypeStruct((6, width, slots), F32),
            jax.ShapeDtypeStruct((2 * layers, width), F32),
            jax.ShapeDtypeStruct((8, slots), F32),
            jax.ShapeDtypeStruct((8, width), F32),
        ],
        scratch_shapes=[pltpu.VMEM((10, 2, width, slots // 2), F32)],
        compiler_params=params(16),
        name="first_step",
    )(received, gathered, inner, ends, sides, picks)


def second_kernel(
    c_ref, s_ref, flux_ref, inner_ref, ends_ref, edges_ref, edge1_ref, edge2_ref, end1_ref, end2_ref, out_ref, scratch
):
    c, s = c_ref[...], s_ref[...]
    width, slots = c.shape
    devices = slots // 2
    west, east, lower, upper = inner_neighbours(c, inner_ref[...])
    west_edge, east_edge = from_turns("gx", edge1_ref[...], edge2_ref[...])
    rest = jnp.zeros((width - west_edge.shape[0], width), F32)
    count = west_edge.shape[0]
    west_edge = jnp.concatenate([west_edge, rest], 0).T[:, :count]
    east_edge = jnp.concatenate([east_edge, rest], 0).T[:, :count]
    west = west + take(stacked(west_edge), edges_ref[:, :slots])
    east = east + take(stacked(east_edge), edges_ref[:, slots:])
    south, north = from_turns("gy", end1_ref[...], end2_ref[...])
    ends = end_values(south, north, ends_ref[...])
    fluxes = [tiles_of(flux_ref[i]) for i in range(5)] + [flux_ref[5, : width // CHUNK]]
    tiles = transport(
        tiles_of(c), tiles_of(s), fluxes, tiles_of(west), tiles_of(east), tiles_of(lower), tiles_of(upper), ends
    )
    for k, lines in enumerate(to_lines(tiles, scratch)):
        out_ref[pl.ds(k, devices, stride=2), :] = lines


def second_step(c, s, fluxes, inner, ends, edges, edge, end):
    width, slots = c.shape
    return pl.pallas_call(
        second_kernel,
        out_shape=jax.ShapeDtypeStruct((slots, width), F32),
        scratch_shapes=[pltpu.VMEM((2, width, slots // 2), F32)],
        compiler_params=params(16),
        name="second_step",
    )(c, s, fluxes, inner, ends, edges, *edge, *end)


def owner_kernel(mask_ref, recv_ref, out_ref):
    chosen = mask_ref[...]
    high, middle, low = (
        jnp.dot(chosen, part, preferred_element_type=F32) for part in split(recv_ref[...])
    )
    out_ref[...] = (low + middle) + high


def to_owner(mask, received):
    return pl.pallas_call(
        owner_kernel,
        out_shape=jax.ShapeDtypeStruct((mask.shape[0], received.shape[1]), F32),
        compiler_params=params(4),
        name="to_owner",
    )(mask, received)


def body(conductivity, storage, recharge, block_ids, neighbours, concentration, sorption):
    layers, rows_x, width = conductivity.shape
    devices = lax.axis_size(AXES)
    owned = concentration.shape[0]
    ids = block_ids.reshape(devices, owned)
    first, second = swap("gx", *pack_edges(conductivity, storage, recharge))
    (
        conductivity, storage, recharge, ids, concentration, sorption, own,
        inner, ends, sides, edges, picks, slots,
    ) = load(conductivity, storage, recharge, ids, concentration, sorption)
    strip, west, east, first, second = pack_strip(own, first, second)
    first, second = swap("gy", first, second)
    send, mask = pack_send(ids, concentration, sorption, layers, rows_x)
    faces = faces_of(conductivity, storage, west, east)
    base, image, gathered, send = flow(
        conductivity, storage, recharge, west, east, strip, first, second, send, slots, faces
    )
    received = lax.all_to_all(
        send.reshape(devices, 1, ROWS * width), AXES, split_axis=0, concat_axis=0, tiled=True
    ).reshape(devices * ROWS, width)
    c, s, flux, edge, end, scal = first_step(received, gathered, inner, ends, sides, picks, layers)
    edge = swap("gx", edge, edge)
    end = swap("gy", end, end)
    head = scal[0, 0] * base + scal[0, 1] * image
    result = second_step(c, s, flux, inner, ends, edges, edge, end)
    returned = lax.all_to_all(
        result.reshape(devices, 2, width), AXES, split_axis=0, concat_axis=0, tiled=True
    ).reshape(devices * 2, width)
    return head, to_owner(mask, returned)


def solution(mesh):
    return jax.shard_map(
        body,
        mesh=mesh,
        in_specs=(
            P(None, "gx", "gy"),
            P(None, "gx", "gy"),
            P(None, "gx", "gy"),
            P(),
            P(("gx", "gy"), None),
            P(("gx", "gy"), None),
            P(("gx", "gy"), None),
        ),
        out_specs=(P(None, "gx", "gy"), P(("gx", "gy"), None)),
        check_vma=False,
    )
```

```python
import functools

import jax
import jax.numpy as jnp
from jax import lax
from jax.experimental import pallas as pl
from jax.experimental.pallas import tpu as pltpu
from jax.sharding import PartitionSpec as P

PICARD = 3
POROSITY = 0.35
BULK_DENSITY = 1.6
EXPONENT = 0.7
SOFTEN = 0.05
DISPERSION = 0.5
TIME_STEP = 0.1
ADVECT = 1.0
VERTICAL = 2.0
COUPLING = TIME_STEP * DISPERSION

AXES = ("gx", "gy")
ROWS = 9
NONE = -5000
F32 = jnp.float32
BF16 = jnp.bfloat16


def params(mib):
    return pltpu.CompilerParams(vmem_limit_bytes=int(mib * 1024 * 1024))


def iota(shape, dim):
    return lax.broadcasted_iota(jnp.int32, shape, dim)


def roll(x, shift, axis):
    return pltpu.roll(x, shift % x.shape[axis] if isinstance(shift, int) else shift, axis)


def split(x):
    high = x.astype(BF16)
    rest = x - high.astype(F32)
    middle = rest.astype(BF16)
    low = (rest - middle.astype(F32)).astype(BF16)
    return high, middle, low


def pick(mask, parts):
    chosen = jnp.where(mask, 1.0, 0.0).astype(BF16)
    high, middle, low = (jnp.dot(chosen, part, preferred_element_type=F32) for part in parts)
    return (low + middle) + high


def rows_of(parts, start, stop):
    return tuple(part[start:stop] for part in parts)


def place():
    across = lax.axis_size("gy")
    return lax.axis_index("gx") * across + lax.axis_index("gy")


def by_turns(axis, low, high):
    odd = jnp.full(low.shape, lax.axis_index(axis) % 2) == 1
    return jnp.where(odd, low, high), jnp.where(odd, high, low)


def from_turns(axis, first, second):
    at = jnp.full(first.shape, lax.axis_index(axis))
    odd = at % 2 == 1
    low = jnp.where(at == 0, 0.0, jnp.where(odd, first, second))
    high = jnp.where(at == lax.axis_size(axis) - 1, 0.0, jnp.where(odd, second, first))
    return low, high


def swap(axis, first, second):
    count = lax.axis_size(axis)
    one = [(i, i ^ 1) for i in range(count)]
    if axis == "gx":
        other = [(i, (i + 1 if i % 2 else i - 1) % count) for i in range(count)]
        return lax.ppermute(first, axis, one), lax.ppermute(second, axis, other)
    pairs = []
    for row in range(lax.axis_size("gx")):
        for i in range(count):
            partner = i + 1 if i % 2 else i - 1
            if 0 <= partner < count:
                pairs.append((row * count + i, row * count + partner))
            else:
                pairs.append((row * count + i, (row ^ 1) * count + i))
    return lax.ppermute(first, axis, one), lax.ppermute(second, AXES, pairs)


HBM = pl.BlockSpec(memory_space=pltpu.HBM)
SMEM = pl.BlockSpec(memory_space=pltpu.SMEM)
VMEM = pl.BlockSpec(memory_space=pltpu.VMEM)


def fetch(pairs, sems):
    copies = [pltpu.make_async_copy(src, dst, sems.at[i]) for i, (src, dst) in enumerate(pairs)]
    for copy in copies:
        copy.start()
    return copies


def pinned(arrays):
    return tuple(pltpu.with_memory_space_constraint(x, pltpu.HBM) for x in arrays)


def edges_kernel(k_hbm, s_hbm, r_hbm, first_ref, second_ref, tiles, sems):
    rows = k_hbm.shape[1]
    pairs = []
    for i, ref in enumerate((k_hbm, s_hbm, r_hbm)):
        pairs.append((ref.at[:, pl.ds(rows - 8, 8), :], tiles.at[2 * i]))
        pairs.append((ref.at[:, pl.ds(0, 8), :], tiles.at[2 * i + 1]))
    for copy in fetch(pairs, sems):
        copy.wait()
    sub = iota(first_ref.shape[1:], 0)
    for z in range(first_ref.shape[0]):
        east = jnp.where(
            sub >= 5,
            tiles[0, z],
            jnp.where(sub >= 3, roll(tiles[2, z], -3, 0), roll(tiles[4, z], -5, 0)),
        )
        west = jnp.where(
            sub < 3,
            tiles[1, z],
            jnp.where(sub < 5, roll(tiles[3, z], 3, 0), roll(tiles[5, z], 5, 0)),
        )
        first_ref[z], second_ref[z] = by_turns("gx", west, east)


def pack_edges(*arrays):
    layers, rows, width = arrays[0].shape
    tile = jax.ShapeDtypeStruct((layers, 8, width), F32)
    return pl.pallas_call(
        edges_kernel,
        in_specs=[HBM] * 3,
        out_specs=[VMEM] * 2,
        out_shape=[tile, tile],
        scratch_shapes=[pltpu.VMEM((6, layers, 8, width), F32), pltpu.SemaphoreType.DMA((6,))],
        compiler_params=params(8),
        name="pack_edges",
    )(*pinned(arrays))


def beside(index, z, west_ref, east_ref):
    shift = (0, 3, 5)[index]
    top, bottom = west_ref[z], east_ref[z]
    if shift:
        top, bottom = roll(top, shift, 0), roll(bottom, -shift, 0)
    return top, bottom


def widened(index, z, own_ref, west_ref, east_ref):
    top, bottom = beside(index, z, west_ref, east_ref)
    return jnp.concatenate([top, own_ref[z], bottom], 0)


def strip_of(layers, layer):
    strip = None
    for z in range(layers):
        turned = roll(layer(z), z * 8 + 4, 1)
        strip = turned if strip is None else jnp.where(iota(turned.shape, 1) >= z * 8, turned, strip)
    return strip


def strip_kernel(inner_ref, first_ref, second_ref, out_ref, west_ref, east_ref, one_ref, other_ref):
    layers = west_ref.shape[0]
    west_ref[...], east_ref[...] = from_turns("gx", first_ref[...], second_ref[...])
    rows = inner_ref.shape[1]
    for index in range(3):
        out_ref[index, 8 : 8 + rows] = inner_ref[index]
        out_ref[index, 0:8] = strip_of(layers, lambda z: beside(index, z, west_ref, east_ref)[0])
        out_ref[index, 8 + rows :] = strip_of(layers, lambda z: beside(index, z, west_ref, east_ref)[1])
    k, s, r = out_ref[0], out_ref[1], out_ref[2]
    slot = iota(k.shape, 1) % 8
    south = jnp.where(slot >= 4, k, jnp.where(slot >= 2, roll(s, -2, 1), roll(r, -4, 1)))
    north = jnp.where(slot < 4, k, jnp.where(slot < 6, roll(s, 2, 1), roll(r, 4, 1)))
    one_ref[...], other_ref[...] = by_turns("gy", south, north)


def pack_strip(inner, first, second):
    rows, width = inner.shape[1:]
    tile = jax.ShapeDtypeStruct(first.shape, F32)
    return pl.pallas_call(
        strip_kernel,
        out_shape=[jax.ShapeDtypeStruct((3, rows + 16, width), F32), tile, tile]
        + [jax.ShapeDtypeStruct((rows + 16, width), F32)] * 2,
        compiler_params=params(4),
        name="pack_strip",
    )(inner, first, second)


def column(row):
    n = row.shape[1]
    return jnp.sum(jnp.where(iota((n, n), 0) == iota((n, n), 1), row, 0.0), 1, keepdims=True)


def as_row(col):
    n = col.shape[0]
    return jnp.sum(jnp.where(iota((n, n), 0) == iota((n, n), 1), col, 0.0), 0, keepdims=True)


def slot_codes(ids, target, lines):
    brick = ids // lines
    key = iota(ids.shape, 1) * lines + ids % lines
    mine = brick == target
    first = jnp.min(jnp.where(mine, key, ids.shape[1] * lines).astype(F32), 1, keepdims=True)
    second = jnp.max(jnp.where(mine, key, -1).astype(F32), 1, keepdims=True)
    cols = [
        jnp.where(second >= 0.0, code.astype(jnp.int32) % lines, NONE).astype(F32)
        for code in (first, second)
    ]
    rows = [as_row(col) for col in cols]
    return jnp.concatenate(cols, 0).astype(jnp.int32), jnp.concatenate(rows, 1).astype(jnp.int32)


def load_kernel(
    down, across,
    k_hbm, s_hbm, r_hbm, ids_hbm, conc_hbm, sorp_hbm,
    k_ref, s_ref, r_ref, ids_ref, conc_ref, sorp_ref, own_ref,
    inner_ref, ends_ref, sides_ref, edges_ref, pick_ref, slots_ref,
    sems,
):
    refs = (k_ref, s_ref, r_ref)
    copies = fetch(
        [
            (ids_hbm, ids_ref),
            (k_hbm, k_ref),
            (s_hbm, s_ref),
            (r_hbm, r_ref),
            (conc_hbm, conc_ref),
            (sorp_hbm, sorp_ref),
        ],
        sems,
    )
    layers, rows_x = k_ref.shape[:2]
    slots = slots_ref.shape[1]
    lines = layers * rows_x
    me = place()
    gx, gy = me // across, me % across
    copies[0].wait()
    ids = ids_ref[...]
    code, slot = slot_codes(ids, me, lines)
    west, _ = slot_codes(ids, jnp.where(gx > 0, me - across, -1), lines)
    east, _ = slot_codes(ids, jnp.where(gx < down - 1, me + across, -1), lines)
    south, _ = slot_codes(ids, jnp.where(gy > 0, me - 1, -1), lines)
    north, _ = slot_codes(ids, jnp.where(gy < across - 1, me + 1, -1), lines)
    slots_ref[...] = slot
    active = slot >= 0
    layer, row = slot // rows_x, slot % rows_x
    low, high = active & (row == 0), active & (row == rows_x - 1)

    def ones(mask):
        return jnp.where(mask, 1.0, 0.0).astype(BF16)

    inner_ref[:, :slots] = ones((code == slot - 1) & (row != 0))
    inner_ref[:, slots : 2 * slots] = ones((code == slot + 1) & (row != rows_x - 1))
    inner_ref[:, 2 * slots : 3 * slots] = ones(code == slot - rows_x)
    inner_ref[:, 3 * slots :] = ones(code == slot + rows_x)
    ends_ref[:, :slots] = ones((south == slot) & active)
    ends_ref[:, slots:] = ones((north == slot) & active)
    sides_ref[:, :slots] = ones((west == slot + rows_x - 1) & low)
    sides_ref[:, slots:] = ones((east == slot - rows_x + 1) & high)
    at = iota((edges_ref.shape[0], slots), 0)
    edges_ref[:, :slots] = ones((at == layer) & low)
    edges_ref[:, slots:] = ones((at == layer + layers) & high)
    at = iota((slots, pick_ref.shape[1]), 1)
    pick_ref[...] = ones(
        (code >= 0)
        & (
            ((code % rows_x == rows_x - 1) & (code // rows_x == at))
            | ((code % rows_x == 0) & (code // rows_x + layers == at))
        )
    )
    for index, ref in enumerate(refs):
        copies[1 + index].wait()
        own_ref[index] = strip_of(layers, lambda z: ref[z])
    copies[4].wait()
    copies[5].wait()


def load(*arrays):
    rows, width = arrays[0].shape[1:]
    layers = arrays[0].shape[0]
    slots = 2 * arrays[3].shape[0]
    kernel = functools.partial(load_kernel, lax.axis_size("gx"), lax.axis_size("gy"))
    return pl.pallas_call(
        kernel,
        in_specs=[HBM] * 6,
        out_specs=[VMEM] * 13,
        out_shape=[jax.ShapeDtypeStruct(x.shape, x.dtype) for x in arrays]
        + [
            jax.ShapeDtypeStruct((3, rows, width), F32),
            jax.ShapeDtypeStruct((slots, 4 * slots), BF16),
            jax.ShapeDtypeStruct((slots, 2 * slots), BF16),
            jax.ShapeDtypeStruct((slots, 2 * slots), BF16),
            jax.ShapeDtypeStruct((2 * layers, 2 * slots), BF16),
            jax.ShapeDtypeStruct((slots, width), BF16),
            jax.ShapeDtypeStruct((1, slots), jnp.int32),
        ],
        scratch_shapes=[pltpu.SemaphoreType.DMA((6,))],
        compiler_params=params(8),
        name="load",
    )(*pinned(arrays))


def send_kernel(
    across, rows_x, layers, ids_ref, conc_ref, sorp_ref, out_ref, mask_ref
):
    devices, owned = ids_ref.shape
    lines = layers * rows_x
    me = place()
    own = ids_ref[pl.ds(me, 1), :]
    own_brick = own // lines
    own_row = own % lines % rows_x
    brick_col = column(own_brick.astype(F32)).astype(jnp.int32)
    square = (owned, owned)
    same = (brick_col == own_brick) & (iota(square, 0) < iota(square, 1))
    rank = jnp.sum(jnp.where(same, 1.0, 0.0), 0, keepdims=True).astype(jnp.int32)
    back = jnp.where(iota((2 * devices, owned), 0) == own_brick * 2 + rank, 1.0, 0.0)
    mask_ref[...] = back.T.astype(BF16)
    dest = iota((devices, owned), 0)
    conc = conc_ref[...]
    conc_parts = split(conc)
    sorp_parts = split(sorp_ref[...])
    lane = iota((owned, conc.shape[1]), 1)
    misc = jnp.zeros((devices, conc.shape[1]), F32)
    for k in range(2):
        ranked = rank == k
        home = (dest == own_brick) & ranked
        out_ref[pl.ds(k, devices, stride=ROWS), :] = pick(home, conc_parts)
        out_ref[pl.ds(2 + k, devices, stride=ROWS), :] = pick(home, sorp_parts)
        after = (dest == own_brick + across) & ranked & (own_row == rows_x - 1)
        out_ref[pl.ds(4 + k, devices, stride=ROWS), :] = pick(after, conc_parts)
        before = (dest == own_brick - across) & ranked & (own_row == 0)
        out_ref[pl.ds(6 + k, devices, stride=ROWS), :] = pick(before, conc_parts)
        tails = jnp.where(lane // 2 == k, roll(conc, 2 + 2 * k, 1), 0.0)
        heads = jnp.where(lane // 2 == 2 + k, roll(conc, 4 + 2 * k, 1), 0.0)
        north = (dest == own_brick + 1) & ranked & (own_brick % across < across - 1)
        south = (dest == own_brick - 1) & ranked & (own_brick % across > 0)
        misc = misc + pick(north, split(tails)) + pick(south, split(heads))
    out_ref[pl.ds(8, devices, stride=ROWS), :] = misc


def pack_send(ids, concentration, sorption, layers, rows_x):
    devices, owned = ids.shape
    width = concentration.shape[1]
    slots = 2 * devices
    kernel = functools.partial(send_kernel, lax.axis_size("gy"), rows_x, layers)
    return pl.pallas_call(
        kernel,
        out_shape=[
            jax.ShapeDtypeStruct((devices * ROWS, width), F32),
            jax.ShapeDtypeStruct((owned, slots), BF16),
        ],
        compiler_params=params(8),
        name="pack_send",
    )(ids, concentration, sorption)


def harmonic(a, c):
    return jnp.where(jnp.minimum(a, c) > 0.0, 2.0 * a * c / (a + c), jnp.maximum(a, c))


def faces_kernel(k_ref, s_ref, west_ref, east_ref, fw, fs, fb, part):
    layers, rows, width = k_ref.shape
    shape = (rows + 16, width)
    lane = iota(shape, 1)
    fb[0] = jnp.zeros(shape, F32)

    def step(z, carry):
        k = widened(0, z, k_ref, west_ref, east_ref)
        face_w = harmonic(k, roll(k, 1, 0))
        face_s = jnp.where(lane == 0, 0.0, harmonic(k, roll(k, 1, 1)))
        upper = widened(0, jnp.minimum(z + 1, layers - 1), k_ref, west_ref, east_ref)
        face_a = jnp.where(z < layers - 1, VERTICAL * harmonic(k, upper), 0.0)
        s = widened(1, z, s_ref, west_ref, east_ref)
        fw[z] = face_w
        fs[z] = face_s
        part[z] = s + face_w + roll(face_w, -1, 0) + face_s + roll(face_s, -1, 1) + fb[z] + face_a
        fb[z + 1] = face_a
        return carry

    lax.fori_loop(0, layers, step, 0, unroll=2)


def faces_of(conductivity, storage, west, east):
    layers, rows, width = conductivity.shape
    tall = jax.ShapeDtypeStruct((layers, rows + 16, width), F32)
    return pl.pallas_call(
        faces_kernel,
        out_shape=[tall, tall, jax.ShapeDtypeStruct((layers + 1, rows + 16, width), F32), tall],
        compiler_params=params(8),
        name="faces",
    )(conductivity, storage, west, east)


def flow_kernel(
    k_ref, s_ref, r_ref, west_ref, east_ref, strip_ref, first_ref, second_ref, send_ref, slots_ref,
    fw, fs, fb, part,
    d_out, w_out, gath_out, send_out,
    rd, dd, ww, lines_ref,
):
    layers, rows, width = k_ref.shape
    tall = rows + 16
    shape = (tall, width)
    lane = iota(shape, 1)
    slot = lane % 8
    devices = send_ref.shape[0] // ROWS

    send_out[...] = send_ref[...]

    def side(low):
        def joined(index):
            south, north = from_turns("gy", first_ref[...], second_ref[...])
            shift = 2 * index
            if low:
                return jnp.where(slot < 4, roll(south, -shift, 1), strip_ref[index])
            return jnp.where(slot < 4, strip_ref[index], roll(north, shift, 1))

        k, s, r = joined(0), joined(1), joined(2)
        face_w = harmonic(k, roll(k, 1, 0))
        face_s = harmonic(k, roll(k, 1, 1))
        face_b = jnp.where(lane >= 8, VERTICAL * harmonic(k, roll(k, 8, 1)), 0.0)
        diagonal = (
            s + face_w + roll(face_w, -1, 0) + face_s + roll(face_s, -1, 1) + face_b + roll(face_b, -8, 1)
        )
        inverse = jnp.where(k > 0.0, 1.0 / diagonal, 0.0)
        d = r * inverse
        flux_w = face_w * (roll(d, 1, 0) - d)
        flux_s = face_s * (roll(d, 1, 1) - d)
        flux_b = face_b * (roll(d, 8, 1) - d)
        image = (
            s * d
            + (roll(flux_w, -1, 0) - flux_w)
            + (roll(flux_s, -1, 1) - flux_s)
            + (roll(flux_b, -8, 1) - flux_b)
        )
        w = image * inverse
        return face_s, flux_s, face_s * (roll(w, 1, 1) - w)

    low_face, low_d, low_w = side(True)
    high_face, high_d, high_w = side(False)

    def with_low(z, field, strip):
        return jnp.where(lane == 0, roll(strip, width - 4 - z * 8, 1), field)

    def north_of(z, field, strip):
        shift = lax.rem(width - 5 + width - z * 8, width)
        return jnp.where(lane == width - 1, roll(strip, shift, 1), roll(field, -1, 1))

    def scale(z, carry):
        k = widened(0, z, k_ref, west_ref, east_ref)
        r = widened(2, z, r_ref, west_ref, east_ref)
        low = jnp.where(lane == 0, roll(low_face, width - 4 - z * 8, 1), 0.0)
        shift = lax.rem(width - 5 + width - z * 8, width)
        high = jnp.where(lane == width - 1, roll(high_face, shift, 1), 0.0)
        diagonal = part[z] + low + high
        inverse = jnp.where(k > 0.0, 1.0 / diagonal, 0.0)
        rd[z] = inverse
        dd[z] = r * inverse
        return carry

    lax.fori_loop(0, layers, scale, 0, unroll=8)

    def total(x):
        return jnp.sum(x[8 : 8 + rows].reshape(rows // 8, 8, width), 0)

    def apply(z, field, low, high, block):
        h = field[z]
        below = field[jnp.maximum(z - 1, 0)]
        above = field[jnp.minimum(z + 1, layers - 1)]
        flux_w = fw[z] * (roll(h, 1, 0) - h)
        flux_e = roll(flux_w, -1, 0)
        flux_b = fb[z] * (below - h)
        flux_a = fb[z + 1] * (h - above)
        flux_s = with_low(z, fs[z] * (roll(h, 1, 1) - h), low)
        flux_n = north_of(z, flux_s, high)
        for at, flux in enumerate((flux_w, flux_e, flux_b, flux_a, flux_s, flux_n)):
            start = z * (rows * 16) + (block + at)
            lines_ref[pl.ds(start, rows, stride=16), :] = flux[8 : 8 + rows]
        s = widened(1, z, s_ref, west_ref, east_ref)
        return h, s * h + (flux_e - flux_w) + (flux_a - flux_b) + (flux_n - flux_s)

    zero = jnp.zeros((8, width), F32)

    def first(z, sums):
        d, image = apply(z, dd, low_d, high_d, 0)
        w = image * rd[z]
        ww[z] = w
        d_out[z] = d[8 : 8 + rows]
        w_out[z] = w[8 : 8 + rows]
        r = r_ref[z]
        gamma = jnp.sum((r * d[8 : 8 + rows]).reshape(rows // 8, 8, width), 0)
        return sums[0] + gamma, sums[1] + total(d * image), sums[2] + total(image * w)

    gamma, bend, curve = lax.fori_loop(0, layers, first, (zero, zero, zero), unroll=8)

    def second(z, acc):
        w, image = apply(z, ww, low_w, high_w, 6)
        return acc + total(w * image)

    twist = lax.fori_loop(0, layers, second, zero, unroll=8)
    lane_row = iota((devices, width), 1)
    misc = send_ref[pl.ds(8, devices, stride=ROWS), :]
    for at, part in enumerate((gamma, bend, curve, twist)):
        value = jnp.sum(jnp.sum(part, 0, keepdims=True), 1, keepdims=True)
        misc = jnp.where(lane_row == 8 + at, value, misc)
    send_out[pl.ds(8, devices, stride=ROWS), :] = misc
    for k in range(2):

        def gather(i, carry):
            line = pl.multiple_of(jnp.maximum(slots_ref[0, k * devices + i], 0) * 16, 16)
            slot = pl.multiple_of((k * devices + i) * 16, 16)
            gath_out[pl.ds(slot, 16), :] = lines_ref[pl.ds(line, 16), :]
            return carry

        lax.fori_loop(0, devices, gather, 0, unroll=8)


def flow(conductivity, storage, recharge, west, east, strip, first, second, send, slots, faces):
    layers, rows, width = conductivity.shape
    tall = pltpu.VMEM((layers, rows + 16, width), F32)
    return pl.pallas_call(
        flow_kernel,
        out_shape=[
            jax.ShapeDtypeStruct(conductivity.shape, F32),
            jax.ShapeDtypeStruct(conductivity.shape, F32),
            jax.ShapeDtypeStruct((slots.shape[1] * 16, width), F32),
            jax.ShapeDtypeStruct(send.shape, F32),
        ],
        in_specs=[VMEM] * 9 + [SMEM] + [VMEM] * 4,
        out_specs=[VMEM] * 4,
        scratch_shapes=[tall] * 3 + [pltpu.VMEM((layers * rows * 16, width), F32)],
        compiler_params=params(20),
        name="flow",
    )(conductivity, storage, recharge, west, east, strip, first, second, send, slots, *faces)


CHUNK = 16


def minmod(a, d):
    return jnp.maximum(jnp.minimum(a, d), 0.0) + jnp.minimum(jnp.maximum(a, d), 0.0)


def to_cells(lines, scratch):
    half = lines.shape[0] // 2
    count = lines.shape[1] // CHUNK
    for k in range(2):
        scratch[k] = lines[k * half : (k + 1) * half].T
    tiles = [
        jnp.concatenate([scratch[k, pl.ds(j, count, stride=CHUNK), :] for k in range(2)], 1)
        for j in range(CHUNK)
    ]
    return jnp.concatenate(tiles, 0)


def to_lines(tiles, scratch):
    half = tiles[0].shape[1] // 2
    count = tiles[0].shape[0]
    for k in range(2):
        for j, tile in enumerate(tiles):
            scratch[k, pl.ds(j, count, stride=CHUNK), :] = tile[:, k * half : (k + 1) * half]
    return [scratch[k].T for k in range(2)]


def stacked(x):
    return jnp.concatenate(split(x), 0)


def take(parts, chosen):
    out = jnp.dot(parts, chosen, preferred_element_type=F32)
    count = parts.shape[0] // 3
    return (out[2 * count :] + out[count : 2 * count]) + out[:count]


def reduction(side, diagonal, right):
    count = diagonal.shape[0]
    step = 1
    while step < count:
        inverse = 1.0 / diagonal
        scaled = side * inverse
        value = right * inverse
        right = right - side * roll(value, step, 0) - roll(side * value, -step, 0)
        diagonal = diagonal - side * (side * roll(inverse, step, 0)) - roll(side * scaled, -step, 0)
        side = -side * roll(scaled, step, 0)
        step *= 2
    return right / diagonal


def tridiagonal(diagonal, right):
    off = -COUPLING
    last = CHUNK - 1
    one = jnp.ones_like(diagonal[0])
    zero = jnp.zeros_like(one)
    lead, lead_right = [one, diagonal[0]], [right[0]]
    for j in range(1, last):
        lead_right.append(right[j] * lead[j] - off * lead_right[j - 1])
        lead.append(diagonal[j] * lead[j] - (off * off) * lead[j - 1])
    trail, trail_right = {last: one, last + 1: zero}, {last: zero}
    for j in range(last - 1, -1, -1):
        trail_right[j] = right[j] * trail[j + 1] - off * trail_right[j + 1]
        trail[j] = diagonal[j] * trail[j + 1] - (off * off) * trail[j + 2]
    inverse = 1.0 / lead[last]
    sub = iota(one.shape, 0)
    top = sub == one.shape[0] - 1
    far = off * (-off) ** (last - 1)
    side = jnp.where(sub == 0, 0.0, (-off * far) * inverse)
    above = jnp.where(top, 0.0, roll(trail[1] * inverse, -1, 0))
    above_right = jnp.where(top, 0.0, roll(trail_right[0] * inverse, -1, 0))
    z = reduction(
        side,
        diagonal[last] - (off * off) * (lead[last - 1] * inverse + above),
        right[last] - off * (lead_right[last - 1] * inverse + above_right),
    )
    before = jnp.where(sub == 0, 0.0, roll(z, 1, 0))
    out = []
    for j in range(last):
        low = lead_right[j] - (off * (-off) ** j) * before
        high = off * trail_right[j + 1] + (off * (-off) ** (last - 1 - j)) * z
        out.append(inverse * (trail[j + 1] * low - lead[j] * high))
    return out + [z]


def transport(c, sorption, fluxes, west, east, lower, upper, ends):
    q_w, q_e, q_b, q_a, q_s, q_n = fluxes
    south_two, south_one, north_one, north_two = ends
    sub = iota(c[0].shape, 0)
    bottom, top = sub == 0, sub == c[0].shape[0] - 1
    before = [
        jnp.where(bottom, south_two, roll(c[-2], 1, 0)),
        jnp.where(bottom, south_one, roll(c[-1], 1, 0)),
    ]
    after = [
        jnp.where(top, north_one, roll(c[0], -1, 0)),
        jnp.where(top, north_two, roll(c[1], -1, 0)),
    ]
    line = before + c + after

    def face(q, far_left, left, right, far_right):
        rise = right - left
        positive = left + 0.5 * minmod(rise, left - far_left)
        negative = right + 0.5 * minmod(-rise, right - far_right)
        return jnp.maximum(q, 0.0) * positive + jnp.minimum(q, 0.0) * negative

    along = [face(q_s[j], *line[j : j + 4]) for j in range(CHUNK)]
    beyond = face(q_n, *line[CHUNK : CHUNK + 4])
    along.append(jnp.where(top, beyond, roll(along[0], -1, 0)))
    v = list(c)
    source = [None] * CHUNK
    diagonal, right = [None] * CHUNK, [None] * CHUNK
    for sweep in range(PICARD):
        for j in range(CHUNK):
            square = v[j] * v[j] + SOFTEN * SOFTEN
            power = (BULK_DENSITY * sorption[j]) * jnp.exp(
                (0.5 * (EXPONENT - 1.0)) * jnp.log(square)
            )
            retard = POROSITY + power
            root = jnp.sqrt(square)
            if sweep == 0:
                value = c[j]
                advect = along[j] - along[j + 1]
                advect = advect + jnp.maximum(q_w[j], 0.0) * west[j] + jnp.minimum(q_w[j], 0.0) * value
                advect = advect - jnp.maximum(q_e[j], 0.0) * value - jnp.minimum(q_e[j], 0.0) * east[j]
                advect = advect + jnp.maximum(q_b[j], 0.0) * lower[j] + jnp.minimum(q_b[j], 0.0) * value
                advect = advect - jnp.maximum(q_a[j], 0.0) * value - jnp.minimum(q_a[j], 0.0) * upper[j]
                advect = ADVECT * advect
                if j == 0:
                    advect = advect + jnp.where(bottom, COUPLING * south_one, 0.0)
                if j == CHUNK - 1:
                    advect = advect + jnp.where(top, COUPLING * north_one, 0.0)
                source[j] = POROSITY * value + power * root + advect
                right[j] = retard * value + advect
            else:
                right[j] = power * (v[j] - root) + source[j]
            diagonal[j] = retard + 2.0 * COUPLING
        v = tridiagonal(diagonal, right)
    return v


def tiles_of(x):
    count = x.shape[0] // CHUNK
    return [x[j * count : (j + 1) * count] for j in range(CHUNK)]


def inner_neighbours(c, chosen):
    slots = c.shape[1]
    values = take(stacked(c), chosen)
    return [values[:, i * slots : (i + 1) * slots] for i in range(4)]


def end_values(south, north, chosen):
    slots = south.shape[1]
    tails = take(stacked(south), chosen[:, :slots])
    heads = take(stacked(north), chosen[:, slots:])
    return tails[0:1], tails[1:2], heads[2:3], heads[3:4]


def first_kernel(
    recv_ref, gath_ref, inner_ref, ends_ref, sides_ref, pick_ref,
    c_out, s_out, flux_out, edge_out, end_out, scal_out, scratch,
):
    devices = recv_ref.shape[0] // ROWS
    slots = 2 * devices
    width = recv_ref.shape[1]

    def received(at):
        return recv_ref[pl.ds(at, devices, stride=ROWS), :]

    def pair(at):
        return jnp.concatenate([received(at), received(at + 1)], 0)

    misc = received(8)
    sums = jnp.sum(misc, 0, keepdims=True)
    at = iota(sums.shape, 1)
    gamma, bend, curve, twist = (
        jnp.sum(jnp.where(at == 8 + i, sums, 0.0), 1, keepdims=True) for i in range(4)
    )
    alpha = gamma / bend
    gamma_next = alpha * alpha * curve - gamma
    beta = gamma_next / gamma
    cross = bend - alpha * curve
    bend_next = bend - 2.0 * alpha * curve + alpha * alpha * twist + 2.0 * beta * cross + beta * beta * bend
    alpha_next = gamma_next / bend_next
    on_d = alpha + alpha_next * (1.0 + beta)
    on_w = -alpha * alpha_next
    scal_out[...] = jnp.where(iota((8, width), 1) == 0, on_d, on_w)

    c = to_cells(pair(0), scratch.at[0])
    s = to_cells(pair(2), scratch.at[1])
    s_out[...] = s
    beside_w = to_cells(pair(4), scratch.at[2])
    beside_e = to_cells(pair(6), scratch.at[3])
    fluxes = []
    for i in range(6):
        flux = on_d * gath_ref[pl.ds(i, slots, stride=16), :]
        flux = flux + on_w * gath_ref[pl.ds(6 + i, slots, stride=16), :]
        flux = to_cells(flux, scratch.at[4 + i])
        if i == 5:
            flux = flux[width - width // CHUNK :]
            flux_out[5, : flux.shape[0]] = flux
            fluxes.append(flux)
        else:
            flux_out[i] = flux
            fluxes.append(tiles_of(flux))
    west, east, lower, upper = inner_neighbours(c, inner_ref[...])
    west = west + take(stacked(beside_w), sides_ref[:, :slots])
    east = east + take(stacked(beside_e), sides_ref[:, slots:])
    turned = misc.T
    ends = [
        jnp.concatenate([turned[a : a + 1], turned[a + 2 : a + 3]], 1) for a in (0, 1, 4, 5)
    ] + [jnp.zeros((4, slots), F32)]
    ends = jnp.concatenate(ends, 0)
    ends = end_values(ends, ends, ends_ref[...])
    tiles = transport(
        tiles_of(c), tiles_of(s), fluxes, tiles_of(west), tiles_of(east), tiles_of(lower), tiles_of(upper), ends
    )
    c = jnp.concatenate(tiles, 0)
    c_out[...] = c
    count = tiles[0].shape[0]
    end_out[...] = jnp.concatenate(
        [
            tiles[-2][count - 1 :],
            tiles[-1][count - 1 :],
            tiles[0][:1],
            tiles[1][:1],
            jnp.zeros((4, slots), F32),
        ],
        0,
    )
    edge = take(stacked(c), pick_ref[...])
    edge_out[...] = edge.T[: edge_out.shape[0]]


def first_step(received, gathered, inner, ends, sides, picks, layers):
    width = received.shape[1]
    slots = inner.shape[0]
    cells = jax.ShapeDtypeStruct((width, slots), F32)
    return pl.pallas_call(
        first_kernel,
        out_shape=[
            cells,
            cells,
            jax.ShapeDtypeStruct((6, width, slots), F32),
            jax.ShapeDtypeStruct((2 * layers, width), F32),
            jax.ShapeDtypeStruct((8, slots), F32),
            jax.ShapeDtypeStruct((8, width), F32),
        ],
        scratch_shapes=[pltpu.VMEM((10, 2, width, slots // 2), F32)],
        compiler_params=params(16),
        name="first_step",
    )(received, gathered, inner, ends, sides, picks)


def second_kernel(
    c_ref, s_ref, flux_ref, inner_ref, ends_ref, edges_ref, edge1_ref, edge2_ref, end1_ref, end2_ref, out_ref, scratch
):
    c, s = c_ref[...], s_ref[...]
    width, slots = c.shape
    devices = slots // 2
    west, east, lower, upper = inner_neighbours(c, inner_ref[...])
    west_edge, east_edge = from_turns("gx", edge1_ref[...], edge2_ref[...])
    rest = jnp.zeros((width - west_edge.shape[0], width), F32)
    count = west_edge.shape[0]
    west_edge = jnp.concatenate([west_edge, rest], 0).T[:, :count]
    east_edge = jnp.concatenate([east_edge, rest], 0).T[:, :count]
    west = west + take(stacked(west_edge), edges_ref[:, :slots])
    east = east + take(stacked(east_edge), edges_ref[:, slots:])
    south, north = from_turns("gy", end1_ref[...], end2_ref[...])
    ends = end_values(south, north, ends_ref[...])
    fluxes = [tiles_of(flux_ref[i]) for i in range(5)] + [flux_ref[5, : width // CHUNK]]
    tiles = transport(
        tiles_of(c), tiles_of(s), fluxes, tiles_of(west), tiles_of(east), tiles_of(lower), tiles_of(upper), ends
    )
    for k, lines in enumerate(to_lines(tiles, scratch)):
        out_ref[pl.ds(k, devices, stride=2), :] = lines


def second_step(c, s, fluxes, inner, ends, edges, edge, end):
    width, slots = c.shape
    return pl.pallas_call(
        second_kernel,
        out_shape=jax.ShapeDtypeStruct((slots, width), F32),
        scratch_shapes=[pltpu.VMEM((2, width, slots // 2), F32)],
        compiler_params=params(16),
        name="second_step",
    )(c, s, fluxes, inner, ends, edges, *edge, *end)


def owner_kernel(mask_ref, recv_ref, out_ref):
    chosen = mask_ref[...]
    high, middle, low = (
        jnp.dot(chosen, part, preferred_element_type=F32) for part in split(recv_ref[...])
    )
    out_ref[...] = (low + middle) + high


def to_owner(mask, received):
    return pl.pallas_call(
        owner_kernel,
        out_shape=jax.ShapeDtypeStruct((mask.shape[0], received.shape[1]), F32),
        compiler_params=params(4),
        name="to_owner",
    )(mask, received)


def body(conductivity, storage, recharge, block_ids, neighbours, concentration, sorption):
    layers, rows_x, width = conductivity.shape
    devices = lax.axis_size(AXES)
    owned = concentration.shape[0]
    ids = block_ids.reshape(devices, owned)
    first, second = swap("gx", *pack_edges(conductivity, storage, recharge))
    (
        conductivity, storage, recharge, ids, concentration, sorption, own,
        inner, ends, sides, edges, picks, slots,
    ) = load(conductivity, storage, recharge, ids, concentration, sorption)
    strip, west, east, first, second = pack_strip(own, first, second)
    first, second = swap("gy", first, second)
    send, mask = pack_send(ids, concentration, sorption, layers, rows_x)
    faces = faces_of(conductivity, storage, west, east)
    base, image, gathered, send = flow(
        conductivity, storage, recharge, west, east, strip, first, second, send, slots, faces
    )
    received = lax.all_to_all(
        send.reshape(devices, 1, ROWS * width), AXES, split_axis=0, concat_axis=0, tiled=True
    ).reshape(devices * ROWS, width)
    c, s, flux, edge, end, scal = first_step(received, gathered, inner, ends, sides, picks, layers)
    edge = swap("gx", edge, edge)
    end = swap("gy", end, end)
    head = scal[0, 0] * base + scal[0, 1] * image
    result = second_step(c, s, flux, inner, ends, edges, edge, end)
    returned = lax.all_to_all(
        result.reshape(devices, 2, width), AXES, split_axis=0, concat_axis=0, tiled=True
    ).reshape(devices * 2, width)
    return head, to_owner(mask, returned)


def solution(mesh):
    return jax.shard_map(
        body,
        mesh=mesh,
        in_specs=(
            P(None, "gx", "gy"),
            P(None, "gx", "gy"),
            P(None, "gx", "gy"),
            P(),
            P(("gx", "gy"), None),
            P(("gx", "gy"), None),
            P(("gx", "gy"), None),
        ),
        out_specs=(P(None, "gx", "gy"), P(("gx", "gy"), None)),
        check_vma=False,
    )
```

```python
import functools

import jax
import jax.numpy as jnp
from jax import lax
from jax.experimental import pallas as pl
from jax.experimental.pallas import tpu as pltpu
from jax.sharding import PartitionSpec as P

PICARD = 3
POROSITY = 0.35
BULK_DENSITY = 1.6
EXPONENT = 0.7
SOFTEN = 0.05
DISPERSION = 0.5
TIME_STEP = 0.1
ADVECT = 1.0
VERTICAL = 2.0
COUPLING = TIME_STEP * DISPERSION

AXES = ("gx", "gy")
ROWS = 9
NONE = -5000
F32 = jnp.float32
BF16 = jnp.bfloat16


def params(mib):
    return pltpu.CompilerParams(vmem_limit_bytes=int(mib * 1024 * 1024))


def iota(shape, dim):
    return lax.broadcasted_iota(jnp.int32, shape, dim)


def roll(x, shift, axis):
    return pltpu.roll(x, shift % x.shape[axis] if isinstance(shift, int) else shift, axis)


def split(x):
    high = x.astype(BF16)
    rest = x - high.astype(F32)
    middle = rest.astype(BF16)
    low = (rest - middle.astype(F32)).astype(BF16)
    return high, middle, low


def pick(mask, parts):
    chosen = jnp.where(mask, 1.0, 0.0).astype(BF16)
    high, middle, low = (jnp.dot(chosen, part, preferred_element_type=F32) for part in parts)
    return (low + middle) + high


def rows_of(parts, start, stop):
    return tuple(part[start:stop] for part in parts)


def place():
    across = lax.axis_size("gy")
    return lax.axis_index("gx") * across + lax.axis_index("gy")


def by_turns(axis, low, high):
    odd = jnp.full(low.shape, lax.axis_index(axis) % 2) == 1
    return jnp.where(odd, low, high), jnp.where(odd, high, low)


def from_turns(axis, first, second):
    at = jnp.full(first.shape, lax.axis_index(axis))
    odd = at % 2 == 1
    low = jnp.where(at == 0, 0.0, jnp.where(odd, first, second))
    high = jnp.where(at == lax.axis_size(axis) - 1, 0.0, jnp.where(odd, second, first))
    return low, high


def swap(axis, first, second):
    count = lax.axis_size(axis)
    one = [(i, i ^ 1) for i in range(count)]
    if axis == "gx":
        other = [(i, (i + 1 if i % 2 else i - 1) % count) for i in range(count)]
        return lax.ppermute(first, axis, one), lax.ppermute(second, axis, other)
    pairs = []
    for row in range(lax.axis_size("gx")):
        for i in range(count):
            partner = i + 1 if i % 2 else i - 1
            if 0 <= partner < count:
                pairs.append((row * count + i, row * count + partner))
            else:
                pairs.append((row * count + i, (row ^ 1) * count + i))
    return lax.ppermute(first, axis, one), lax.ppermute(second, AXES, pairs)


HBM = pl.BlockSpec(memory_space=pltpu.HBM)
SMEM = pl.BlockSpec(memory_space=pltpu.SMEM)
VMEM = pl.BlockSpec(memory_space=pltpu.VMEM)


def fetch(pairs, sems):
    copies = [pltpu.make_async_copy(src, dst, sems.at[i]) for i, (src, dst) in enumerate(pairs)]
    for copy in copies:
        copy.start()
    return copies


def pinned(arrays):
    return tuple(pltpu.with_memory_space_constraint(x, pltpu.HBM) for x in arrays)


def edges_kernel(k_hbm, s_hbm, r_hbm, first_ref, second_ref, tiles, sems):
    rows = k_hbm.shape[1]
    pairs = []
    for i, ref in enumerate((k_hbm, s_hbm, r_hbm)):
        pairs.append((ref.at[:, pl.ds(rows - 8, 8), :], tiles.at[2 * i]))
        pairs.append((ref.at[:, pl.ds(0, 8), :], tiles.at[2 * i + 1]))
    for copy in fetch(pairs, sems):
        copy.wait()
    sub = iota(first_ref.shape[1:], 0)
    for z in range(first_ref.shape[0]):
        east = jnp.where(
            sub >= 5,
            tiles[0, z],
            jnp.where(sub >= 3, roll(tiles[2, z], -3, 0), roll(tiles[4, z], -5, 0)),
        )
        west = jnp.where(
            sub < 3,
            tiles[1, z],
            jnp.where(sub < 5, roll(tiles[3, z], 3, 0), roll(tiles[5, z], 5, 0)),
        )
        first_ref[z], second_ref[z] = by_turns("gx", west, east)


def pack_edges(*arrays):
    layers, rows, width = arrays[0].shape
    tile = jax.ShapeDtypeStruct((layers, 8, width), F32)
    return pl.pallas_call(
        edges_kernel,
        in_specs=[HBM] * 3,
        out_specs=[VMEM] * 2,
        out_shape=[tile, tile],
        scratch_shapes=[pltpu.VMEM((6, layers, 8, width), F32), pltpu.SemaphoreType.DMA((6,))],
        compiler_params=params(8),
        name="pack_edges",
    )(*pinned(arrays))


def beside(index, z, west_ref, east_ref):
    shift = (0, 3, 5)[index]
    top, bottom = west_ref[z], east_ref[z]
    if shift:
        top, bottom = roll(top, shift, 0), roll(bottom, -shift, 0)
    return top, bottom


def widened(index, z, own_ref, west_ref, east_ref):
    top, bottom = beside(index, z, west_ref, east_ref)
    return jnp.concatenate([top, own_ref[z], bottom], 0)


def strip_of(layers, layer):
    strip = None
    for z in range(layers):
        turned = roll(layer(z), z * 8 + 4, 1)
        strip = turned if strip is None else jnp.where(iota(turned.shape, 1) >= z * 8, turned, strip)
    return strip


def strip_kernel(inner_ref, first_ref, second_ref, out_ref, west_ref, east_ref, one_ref, other_ref):
    layers = west_ref.shape[0]
    west_ref[...], east_ref[...] = from_turns("gx", first_ref[...], second_ref[...])
    rows = inner_ref.shape[1]
    for index in range(3):
        out_ref[index, 8 : 8 + rows] = inner_ref[index]
        out_ref[index, 0:8] = strip_of(layers, lambda z: beside(index, z, west_ref, east_ref)[0])
        out_ref[index, 8 + rows :] = strip_of(layers, lambda z: beside(index, z, west_ref, east_ref)[1])
    k, s, r = out_ref[0], out_ref[1], out_ref[2]
    slot = iota(k.shape, 1) % 8
    south = jnp.where(slot >= 4, k, jnp.where(slot >= 2, roll(s, -2, 1), roll(r, -4, 1)))
    north = jnp.where(slot < 4, k, jnp.where(slot < 6, roll(s, 2, 1), roll(r, 4, 1)))
    one_ref[...], other_ref[...] = by_turns("gy", south, north)


def pack_strip(inner, first, second):
    rows, width = inner.shape[1:]
    tile = jax.ShapeDtypeStruct(first.shape, F32)
    return pl.pallas_call(
        strip_kernel,
        out_shape=[jax.ShapeDtypeStruct((3, rows + 16, width), F32), tile, tile]
        + [jax.ShapeDtypeStruct((rows + 16, width), F32)] * 2,
        compiler_params=params(4),
        name="pack_strip",
    )(inner, first, second)


def column(row):
    n = row.shape[1]
    return jnp.sum(jnp.where(iota((n, n), 0) == iota((n, n), 1), row, 0.0), 1, keepdims=True)


def as_row(col):
    n = col.shape[0]
    return jnp.sum(jnp.where(iota((n, n), 0) == iota((n, n), 1), col, 0.0), 0, keepdims=True)


def slot_codes(ids, target, lines):
    brick = ids // lines
    key = iota(ids.shape, 1) * lines + ids % lines
    mine = brick == target
    first = jnp.min(jnp.where(mine, key, ids.shape[1] * lines).astype(F32), 1, keepdims=True)
    second = jnp.max(jnp.where(mine, key, -1).astype(F32), 1, keepdims=True)
    cols = [
        jnp.where(second >= 0.0, code.astype(jnp.int32) % lines, NONE).astype(F32)
        for code in (first, second)
    ]
    rows = [as_row(col) for col in cols]
    return jnp.concatenate(cols, 0).astype(jnp.int32), jnp.concatenate(rows, 1).astype(jnp.int32)


def load_kernel(
    down, across,
    k_hbm, s_hbm, r_hbm, ids_hbm, conc_hbm, sorp_hbm,
    k_ref, s_ref, r_ref, ids_ref, conc_ref, sorp_ref, own_ref,
    inner_ref, ends_ref, sides_ref, edges_ref, pick_ref, slots_ref,
    sems,
):
    refs = (k_ref, s_ref, r_ref)
    copies = fetch(
        [
            (ids_hbm, ids_ref),
            (k_hbm, k_ref),
            (s_hbm, s_ref),
            (r_hbm, r_ref),
            (conc_hbm, conc_ref),
            (sorp_hbm, sorp_ref),
        ],
        sems,
    )
    layers, rows_x = k_ref.shape[:2]
    slots = slots_ref.shape[1]
    lines = layers * rows_x
    me = place()
    gx, gy = me // across, me % across
    copies[0].wait()
    ids = ids_ref[...]
    code, slot = slot_codes(ids, me, lines)
    west, _ = slot_codes(ids, jnp.where(gx > 0, me - across, -1), lines)
    east, _ = slot_codes(ids, jnp.where(gx < down - 1, me + across, -1), lines)
    south, _ = slot_codes(ids, jnp.where(gy > 0, me - 1, -1), lines)
    north, _ = slot_codes(ids, jnp.where(gy < across - 1, me + 1, -1), lines)
    slots_ref[...] = slot
    active = slot >= 0
    layer, row = slot // rows_x, slot % rows_x
    low, high = active & (row == 0), active & (row == rows_x - 1)

    def ones(mask):
        return jnp.where(mask, 1.0, 0.0).astype(BF16)

    inner_ref[:, :slots] = ones((code == slot - 1) & (row != 0))
    inner_ref[:, slots : 2 * slots] = ones((code == slot + 1) & (row != rows_x - 1))
    inner_ref[:, 2 * slots : 3 * slots] = ones(code == slot - rows_x)
    inner_ref[:, 3 * slots :] = ones(code == slot + rows_x)
    ends_ref[:, :slots] = ones((south == slot) & active)
    ends_ref[:, slots:] = ones((north == slot) & active)
    sides_ref[:, :slots] = ones((west == slot + rows_x - 1) & low)
    sides_ref[:, slots:] = ones((east == slot - rows_x + 1) & high)
    at = iota((edges_ref.shape[0], slots), 0)
    edges_ref[:, :slots] = ones((at == layer) & low)
    edges_ref[:, slots:] = ones((at == layer + layers) & high)
    at = iota((slots, pick_ref.shape[1]), 1)
    pick_ref[...] = ones(
        (code >= 0)
        & (
            ((code % rows_x == rows_x - 1) & (code // rows_x == at))
            | ((code % rows_x == 0) & (code // rows_x + layers == at))
        )
    )
    for index, ref in enumerate(refs):
        copies[1 + index].wait()
        own_ref[index] = strip_of(layers, lambda z: ref[z])
    copies[4].wait()
    copies[5].wait()


def load(*arrays):
    rows, width = arrays[0].shape[1:]
    layers = arrays[0].shape[0]
    slots = 2 * arrays[3].shape[0]
    kernel = functools.partial(load_kernel, lax.axis_size("gx"), lax.axis_size("gy"))
    return pl.pallas_call(
        kernel,
        in_specs=[HBM] * 6,
        out_specs=[VMEM] * 13,
        out_shape=[jax.ShapeDtypeStruct(x.shape, x.dtype) for x in arrays]
        + [
            jax.ShapeDtypeStruct((3, rows, width), F32),
            jax.ShapeDtypeStruct((slots, 4 * slots), BF16),
            jax.ShapeDtypeStruct((slots, 2 * slots), BF16),
            jax.ShapeDtypeStruct((slots, 2 * slots), BF16),
            jax.ShapeDtypeStruct((2 * layers, 2 * slots), BF16),
            jax.ShapeDtypeStruct((slots, width), BF16),
            jax.ShapeDtypeStruct((1, slots), jnp.int32),
        ],
        scratch_shapes=[pltpu.SemaphoreType.DMA((6,))],
        compiler_params=params(8),
        name="load",
    )(*pinned(arrays))


def send_kernel(
    across, rows_x, layers, ids_ref, conc_ref, sorp_ref, out_ref, mask_ref
):
    devices, owned = ids_ref.shape
    lines = layers * rows_x
    me = place()
    own = ids_ref[pl.ds(me, 1), :]
    own_brick = own // lines
    own_row = own % lines % rows_x
    brick_col = column(own_brick.astype(F32)).astype(jnp.int32)
    square = (owned, owned)
    same = (brick_col == own_brick) & (iota(square, 0) < iota(square, 1))
    rank = jnp.sum(jnp.where(same, 1.0, 0.0), 0, keepdims=True).astype(jnp.int32)
    back = jnp.where(iota((2 * devices, owned), 0) == own_brick * 2 + rank, 1.0, 0.0)
    mask_ref[...] = back.T.astype(BF16)
    dest = iota((devices, owned), 0)
    conc = conc_ref[...]
    conc_parts = split(conc)
    sorp_parts = split(sorp_ref[...])
    lane = iota((owned, conc.shape[1]), 1)
    misc = jnp.zeros((devices, conc.shape[1]), F32)
    for k in range(2):
        ranked = rank == k
        home = (dest == own_brick) & ranked
        out_ref[pl.ds(k, devices, stride=ROWS), :] = pick(home, conc_parts)
        out_ref[pl.ds(2 + k, devices, stride=ROWS), :] = pick(home, sorp_parts)
        after = (dest == own_brick + across) & ranked & (own_row == rows_x - 1)
        out_ref[pl.ds(4 + k, devices, stride=ROWS), :] = pick(after, conc_parts)
        before = (dest == own_brick - across) & ranked & (own_row == 0)
        out_ref[pl.ds(6 + k, devices, stride=ROWS), :] = pick(before, conc_parts)
        tails = jnp.where(lane // 2 == k, roll(conc, 2 + 2 * k, 1), 0.0)
        heads = jnp.where(lane // 2 == 2 + k, roll(conc, 4 + 2 * k, 1), 0.0)
        north = (dest == own_brick + 1) & ranked & (own_brick % across < across - 1)
        south = (dest == own_brick - 1) & ranked & (own_brick % across > 0)
        misc = misc + pick(north, split(tails)) + pick(south, split(heads))
    out_ref[pl.ds(8, devices, stride=ROWS), :] = misc


def pack_send(ids, concentration, sorption, layers, rows_x):
    devices, owned = ids.shape
    width = concentration.shape[1]
    slots = 2 * devices
    kernel = functools.partial(send_kernel, lax.axis_size("gy"), rows_x, layers)
    return pl.pallas_call(
        kernel,
        out_shape=[
            jax.ShapeDtypeStruct((devices * ROWS, width), F32),
            jax.ShapeDtypeStruct((owned, slots), BF16),
        ],
        compiler_params=params(8),
        name="pack_send",
    )(ids, concentration, sorption)


def harmonic(a, c):
    return jnp.where(jnp.minimum(a, c) > 0.0, 2.0 * a * c / (a + c), jnp.maximum(a, c))


def faces_kernel(k_ref, s_ref, west_ref, east_ref, fw, fs, fb, part):
    layers, rows, width = k_ref.shape
    shape = (rows + 16, width)
    lane = iota(shape, 1)
    fb[0] = jnp.zeros(shape, F32)

    def step(z, carry):
        k = widened(0, z, k_ref, west_ref, east_ref)
        face_w = harmonic(k, roll(k, 1, 0))
        face_s = jnp.where(lane == 0, 0.0, harmonic(k, roll(k, 1, 1)))
        upper = widened(0, jnp.minimum(z + 1, layers - 1), k_ref, west_ref, east_ref)
        face_a = jnp.where(z < layers - 1, VERTICAL * harmonic(k, upper), 0.0)
        s = widened(1, z, s_ref, west_ref, east_ref)
        fw[z] = face_w
        fs[z] = face_s
        part[z] = s + face_w + roll(face_w, -1, 0) + face_s + roll(face_s, -1, 1) + fb[z] + face_a
        fb[z + 1] = face_a
        return carry

    lax.fori_loop(0, layers, step, 0, unroll=8)


def faces_of(conductivity, storage, west, east):
    layers, rows, width = conductivity.shape
    tall = jax.ShapeDtypeStruct((layers, rows + 16, width), F32)
    return pl.pallas_call(
        faces_kernel,
        out_shape=[tall, tall, jax.ShapeDtypeStruct((layers + 1, rows + 16, width), F32), tall],
        compiler_params=params(8),
        name="faces",
    )(conductivity, storage, west, east)


def flow_kernel(
    k_ref, s_ref, r_ref, west_ref, east_ref, strip_ref, first_ref, second_ref, send_ref, slots_ref,
    fw, fs, fb, part,
    d_out, w_out, gath_out, send_out,
    rd, dd, ww, lines_ref,
):
    layers, rows, width = k_ref.shape
    tall = rows + 16
    shape = (tall, width)
    lane = iota(shape, 1)
    slot = lane % 8
    devices = send_ref.shape[0] // ROWS

    send_out[...] = send_ref[...]

    def side(low):
        def joined(index):
            south, north = from_turns("gy", first_ref[...], second_ref[...])
            shift = 2 * index
            if low:
                return jnp.where(slot < 4, roll(south, -shift, 1), strip_ref[index])
            return jnp.where(slot < 4, strip_ref[index], roll(north, shift, 1))

        k, s, r = joined(0), joined(1), joined(2)
        face_w = harmonic(k, roll(k, 1, 0))
        face_s = harmonic(k, roll(k, 1, 1))
        face_b = jnp.where(lane >= 8, VERTICAL * harmonic(k, roll(k, 8, 1)), 0.0)
        diagonal = (
            s + face_w + roll(face_w, -1, 0) + face_s + roll(face_s, -1, 1) + face_b + roll(face_b, -8, 1)
        )
        inverse = jnp.where(k > 0.0, 1.0 / diagonal, 0.0)
        d = r * inverse
        flux_w = face_w * (roll(d, 1, 0) - d)
        flux_s = face_s * (roll(d, 1, 1) - d)
        flux_b = face_b * (roll(d, 8, 1) - d)
        image = (
            s * d
            + (roll(flux_w, -1, 0) - flux_w)
            + (roll(flux_s, -1, 1) - flux_s)
            + (roll(flux_b, -8, 1) - flux_b)
        )
        w = image * inverse
        return face_s, flux_s, face_s * (roll(w, 1, 1) - w)

    low_face, low_d, low_w = side(True)
    high_face, high_d, high_w = side(False)

    def with_low(z, field, strip):
        return jnp.where(lane == 0, roll(strip, width - 4 - z * 8, 1), field)

    def north_of(z, field, strip):
        shift = lax.rem(width - 5 + width - z * 8, width)
        return jnp.where(lane == width - 1, roll(strip, shift, 1), roll(field, -1, 1))

    def scale(z, carry):
        k = widened(0, z, k_ref, west_ref, east_ref)
        r = widened(2, z, r_ref, west_ref, east_ref)
        low = jnp.where(lane == 0, roll(low_face, width - 4 - z * 8, 1), 0.0)
        shift = lax.rem(width - 5 + width - z * 8, width)
        high = jnp.where(lane == width - 1, roll(high_face, shift, 1), 0.0)
        diagonal = part[z] + low + high
        inverse = jnp.where(k > 0.0, 1.0 / diagonal, 0.0)
        rd[z] = inverse
        dd[z] = r * inverse
        return carry

    lax.fori_loop(0, layers, scale, 0, unroll=8)

    def total(x):
        return jnp.sum(x[8 : 8 + rows].reshape(rows // 8, 8, width), 0)

    def apply(z, field, low, high, block):
        h = field[z]
        below = field[jnp.maximum(z - 1, 0)]
        above = field[jnp.minimum(z + 1, layers - 1)]
        flux_w = fw[z] * (roll(h, 1, 0) - h)
        flux_e = roll(flux_w, -1, 0)
        flux_b = fb[z] * (below - h)
        flux_a = fb[z + 1] * (h - above)
        flux_s = with_low(z, fs[z] * (roll(h, 1, 1) - h), low)
        flux_n = north_of(z, flux_s, high)
        for at, flux in enumerate((flux_w, flux_e, flux_b, flux_a, flux_s, flux_n)):
            start = z * (rows * 16) + (block + at)
            lines_ref[pl.ds(start, rows, stride=16), :] = flux[8 : 8 + rows]
        s = widened(1, z, s_ref, west_ref, east_ref)
        return h, s * h + (flux_e - flux_w) + (flux_a - flux_b) + (flux_n - flux_s)

    zero = jnp.zeros((8, width), F32)

    def first(z, sums):
        d, image = apply(z, dd, low_d, high_d, 0)
        w = image * rd[z]
        ww[z] = w
        d_out[z] = d[8 : 8 + rows]
        w_out[z] = w[8 : 8 + rows]
        r = r_ref[z]
        gamma = jnp.sum((r * d[8 : 8 + rows]).reshape(rows // 8, 8, width), 0)
        return sums[0] + gamma, sums[1] + total(d * image), sums[2] + total(image * w)

    gamma, bend, curve = lax.fori_loop(0, layers, first, (zero, zero, zero), unroll=8)

    def second(z, acc):
        w, image = apply(z, ww, low_w, high_w, 6)
        return acc + total(w * image)

    twist = lax.fori_loop(0, layers, second, zero, unroll=8)
    lane_row = iota((devices, width), 1)
    misc = send_ref[pl.ds(8, devices, stride=ROWS), :]
    for at, part in enumerate((gamma, bend, curve, twist)):
        value = jnp.sum(jnp.sum(part, 0, keepdims=True), 1, keepdims=True)
        misc = jnp.where(lane_row == 8 + at, value, misc)
    send_out[pl.ds(8, devices, stride=ROWS), :] = misc
    for k in range(2):

        def gather(i, carry):
            line = pl.multiple_of(jnp.maximum(slots_ref[0, k * devices + i], 0) * 16, 16)
            slot = pl.multiple_of((k * devices + i) * 16, 16)
            gath_out[pl.ds(slot, 16), :] = lines_ref[pl.ds(line, 16), :]
            return carry

        lax.fori_loop(0, devices, gather, 0, unroll=8)


def flow(conductivity, storage, recharge, west, east, strip, first, second, send, slots, faces):
    layers, rows, width = conductivity.shape
    tall = pltpu.VMEM((layers, rows + 16, width), F32)
    return pl.pallas_call(
        flow_kernel,
        out_shape=[
            jax.ShapeDtypeStruct(conductivity.shape, F32),
            jax.ShapeDtypeStruct(conductivity.shape, F32),
            jax.ShapeDtypeStruct((slots.shape[1] * 16, width), F32),
            jax.ShapeDtypeStruct(send.shape, F32),
        ],
        in_specs=[VMEM] * 9 + [SMEM] + [VMEM] * 4,
        out_specs=[VMEM] * 4,
        scratch_shapes=[tall] * 3 + [pltpu.VMEM((layers * rows * 16, width), F32)],
        compiler_params=params(20),
        name="flow",
    )(conductivity, storage, recharge, west, east, strip, first, second, send, slots, *faces)


CHUNK = 16


def minmod(a, d):
    return jnp.maximum(jnp.minimum(a, d), 0.0) + jnp.minimum(jnp.maximum(a, d), 0.0)


def to_cells(lines, scratch):
    half = lines.shape[0] // 2
    count = lines.shape[1] // CHUNK
    for k in range(2):
        scratch[k] = lines[k * half : (k + 1) * half].T
    tiles = [
        jnp.concatenate([scratch[k, pl.ds(j, count, stride=CHUNK), :] for k in range(2)], 1)
        for j in range(CHUNK)
    ]
    return jnp.concatenate(tiles, 0)


def to_lines(tiles, scratch):
    half = tiles[0].shape[1] // 2
    count = tiles[0].shape[0]
    for k in range(2):
        for j, tile in enumerate(tiles):
            scratch[k, pl.ds(j, count, stride=CHUNK), :] = tile[:, k * half : (k + 1) * half]
    return [scratch[k].T for k in range(2)]


def stacked(x):
    return jnp.concatenate(split(x), 0)


def take(parts, chosen):
    out = jnp.dot(parts, chosen, preferred_element_type=F32)
    count = parts.shape[0] // 3
    return (out[2 * count :] + out[count : 2 * count]) + out[:count]


def reduction(side, diagonal, right):
    count = diagonal.shape[0]
    step = 1
    while step < count:
        inverse = 1.0 / diagonal
        scaled = side * inverse
        value = right * inverse
        right = right - side * roll(value, step, 0) - roll(side * value, -step, 0)
        diagonal = diagonal - side * (side * roll(inverse, step, 0)) - roll(side * scaled, -step, 0)
        side = -side * roll(scaled, step, 0)
        step *= 2
    return right / diagonal


def tridiagonal(diagonal, right):
    off = -COUPLING
    last = CHUNK - 1
    one = jnp.ones_like(diagonal[0])
    zero = jnp.zeros_like(one)
    lead, lead_right = [one, diagonal[0]], [right[0]]
    for j in range(1, last):
        lead_right.append(right[j] * lead[j] - off * lead_right[j - 1])
        lead.append(diagonal[j] * lead[j] - (off * off) * lead[j - 1])
    trail, trail_right = {last: one, last + 1: zero}, {last: zero}
    for j in range(last - 1, -1, -1):
        trail_right[j] = right[j] * trail[j + 1] - off * trail_right[j + 1]
        trail[j] = diagonal[j] * trail[j + 1] - (off * off) * trail[j + 2]
    inverse = 1.0 / lead[last]
    sub = iota(one.shape, 0)
    top = sub == one.shape[0] - 1
    far = off * (-off) ** (last - 1)
    side = jnp.where(sub == 0, 0.0, (-off * far) * inverse)
    above = jnp.where(top, 0.0, roll(trail[1] * inverse, -1, 0))
    above_right = jnp.where(top, 0.0, roll(trail_right[0] * inverse, -1, 0))
    z = reduction(
        side,
        diagonal[last] - (off * off) * (lead[last - 1] * inverse + above),
        right[last] - off * (lead_right[last - 1] * inverse + above_right),
    )
    before = jnp.where(sub == 0, 0.0, roll(z, 1, 0))
    out = []
    for j in range(last):
        low = lead_right[j] - (off * (-off) ** j) * before
        high = off * trail_right[j + 1] + (off * (-off) ** (last - 1 - j)) * z
        out.append(inverse * (trail[j + 1] * low - lead[j] * high))
    return out + [z]


def transport(c, sorption, fluxes, west, east, lower, upper, ends):
    q_w, q_e, q_b, q_a, q_s, q_n = fluxes
    south_two, south_one, north_one, north_two = ends
    sub = iota(c[0].shape, 0)
    bottom, top = sub == 0, sub == c[0].shape[0] - 1
    before = [
        jnp.where(bottom, south_two, roll(c[-2], 1, 0)),
        jnp.where(bottom, south_one, roll(c[-1], 1, 0)),
    ]
    after = [
        jnp.where(top, north_one, roll(c[0], -1, 0)),
        jnp.where(top, north_two, roll(c[1], -1, 0)),
    ]
    line = before + c + after

    def face(q, far_left, left, right, far_right):
        rise = right - left
        positive = left + 0.5 * minmod(rise, left - far_left)
        negative = right + 0.5 * minmod(-rise, right - far_right)
        return jnp.maximum(q, 0.0) * positive + jnp.minimum(q, 0.0) * negative

    along = [face(q_s[j], *line[j : j + 4]) for j in range(CHUNK)]
    beyond = face(q_n, *line[CHUNK : CHUNK + 4])
    along.append(jnp.where(top, beyond, roll(along[0], -1, 0)))
    v = list(c)
    source = [None] * CHUNK
    diagonal, right = [None] * CHUNK, [None] * CHUNK
    for sweep in range(PICARD):
        for j in range(CHUNK):
            square = v[j] * v[j] + SOFTEN * SOFTEN
            power = (BULK_DENSITY * sorption[j]) * jnp.exp(
                (0.5 * (EXPONENT - 1.0)) * jnp.log(square)
            )
            retard = POROSITY + power
            root = jnp.sqrt(square)
            if sweep == 0:
                value = c[j]
                advect = along[j] - along[j + 1]
                advect = advect + jnp.maximum(q_w[j], 0.0) * west[j] + jnp.minimum(q_w[j], 0.0) * value
                advect = advect - jnp.maximum(q_e[j], 0.0) * value - jnp.minimum(q_e[j], 0.0) * east[j]
                advect = advect + jnp.maximum(q_b[j], 0.0) * lower[j] + jnp.minimum(q_b[j], 0.0) * value
                advect = advect - jnp.maximum(q_a[j], 0.0) * value - jnp.minimum(q_a[j], 0.0) * upper[j]
                advect = ADVECT * advect
                if j == 0:
                    advect = advect + jnp.where(bottom, COUPLING * south_one, 0.0)
                if j == CHUNK - 1:
                    advect = advect + jnp.where(top, COUPLING * north_one, 0.0)
                source[j] = POROSITY * value + power * root + advect
                right[j] = retard * value + advect
            else:
                right[j] = power * (v[j] - root) + source[j]
            diagonal[j] = retard + 2.0 * COUPLING
        v = tridiagonal(diagonal, right)
    return v


def tiles_of(x):
    count = x.shape[0] // CHUNK
    return [x[j * count : (j + 1) * count] for j in range(CHUNK)]


def inner_neighbours(c, chosen):
    slots = c.shape[1]
    values = take(stacked(c), chosen)
    return [values[:, i * slots : (i + 1) * slots] for i in range(4)]


def end_values(south, north, chosen):
    slots = south.shape[1]
    tails = take(stacked(south), chosen[:, :slots])
    heads = take(stacked(north), chosen[:, slots:])
    return tails[0:1], tails[1:2], heads[2:3], heads[3:4]


def first_kernel(
    recv_ref, gath_ref, inner_ref, ends_ref, sides_ref, pick_ref,
    c_out, s_out, flux_out, edge_out, end_out, on_d_out, on_w_out, scratch,
):
    devices = recv_ref.shape[0] // ROWS
    slots = 2 * devices
    width = recv_ref.shape[1]

    def received(at):
        return recv_ref[pl.ds(at, devices, stride=ROWS), :]

    def pair(at):
        return jnp.concatenate([received(at), received(at + 1)], 0)

    misc = received(8)
    sums = jnp.sum(misc, 0, keepdims=True)
    at = iota(sums.shape, 1)
    gamma, bend, curve, twist = (
        jnp.sum(jnp.where(at == 8 + i, sums, 0.0), 1, keepdims=True) for i in range(4)
    )
    alpha = gamma / bend
    gamma_next = alpha * alpha * curve - gamma
    beta = gamma_next / gamma
    cross = bend - alpha * curve
    bend_next = bend - 2.0 * alpha * curve + alpha * alpha * twist + 2.0 * beta * cross + beta * beta * bend
    alpha_next = gamma_next / bend_next
    on_d = alpha + alpha_next * (1.0 + beta)
    on_w = -alpha * alpha_next
    on_d_out[...] = jnp.broadcast_to(on_d, (1, width))
    on_w_out[...] = jnp.broadcast_to(on_w, (1, width))

    c = to_cells(pair(0), scratch.at[0])
    s = to_cells(pair(2), scratch.at[1])
    s_out[...] = s
    beside_w = to_cells(pair(4), scratch.at[2])
    beside_e = to_cells(pair(6), scratch.at[3])
    fluxes = []
    for i in range(6):
        flux = on_d * gath_ref[pl.ds(i, slots, stride=16), :]
        flux = flux + on_w * gath_ref[pl.ds(6 + i, slots, stride=16), :]
        flux = to_cells(flux, scratch.at[4 + i])
        if i == 5:
            flux = flux[width - width // CHUNK :]
            flux_out[5, : flux.shape[0]] = flux
            fluxes.append(flux)
        else:
            flux_out[i] = flux
            fluxes.append(tiles_of(flux))
    west, east, lower, upper = inner_neighbours(c, inner_ref[...])
    west = west + take(stacked(beside_w), sides_ref[:, :slots])
    east = east + take(stacked(beside_e), sides_ref[:, slots:])
    turned = misc.T
    ends = [
        jnp.concatenate([turned[a : a + 1], turned[a + 2 : a + 3]], 1) for a in (0, 1, 4, 5)
    ] + [jnp.zeros((4, slots), F32)]
    ends = jnp.concatenate(ends, 0)
    ends = end_values(ends, ends, ends_ref[...])
    tiles = transport(
        tiles_of(c), tiles_of(s), fluxes, tiles_of(west), tiles_of(east), tiles_of(lower), tiles_of(upper), ends
    )
    c = jnp.concatenate(tiles, 0)
    c_out[...] = c
    count = tiles[0].shape[0]
    end_out[...] = jnp.concatenate(
        [
            tiles[-2][count - 1 :],
            tiles[-1][count - 1 :],
            tiles[0][:1],
            tiles[1][:1],
            jnp.zeros((4, slots), F32),
        ],
        0,
    )
    edge = take(stacked(c), pick_ref[...])
    edge_out[...] = edge.T[: edge_out.shape[0]]


def first_step(received, gathered, inner, ends, sides, picks, layers):
    width = received.shape[1]
    slots = inner.shape[0]
    cells = jax.ShapeDtypeStruct((width, slots), F32)
    return pl.pallas_call(
        first_kernel,
        out_shape=[
            cells,
            cells,
            jax.ShapeDtypeStruct((6, width, slots), F32),
            jax.ShapeDtypeStruct((2 * layers, width), F32),
            jax.ShapeDtypeStruct((8, slots), F32),
            jax.ShapeDtypeStruct((1, width), F32),
            jax.ShapeDtypeStruct((1, width), F32),
        ],
        scratch_shapes=[pltpu.VMEM((10, 2, width, slots // 2), F32)],
        compiler_params=params(16),
        name="first_step",
    )(received, gathered, inner, ends, sides, picks)


def second_kernel(
    c_ref, s_ref, flux_ref, inner_ref, ends_ref, edges_ref, edge1_ref, edge2_ref, end1_ref, end2_ref, out_ref, scratch
):
    c, s = c_ref[...], s_ref[...]
    width, slots = c.shape
    devices = slots // 2
    west, east, lower, upper = inner_neighbours(c, inner_ref[...])
    west_edge, east_edge = from_turns("gx", edge1_ref[...], edge2_ref[...])
    rest = jnp.zeros((width - west_edge.shape[0], width), F32)
    count = west_edge.shape[0]
    west_edge = jnp.concatenate([west_edge, rest], 0).T[:, :count]
    east_edge = jnp.concatenate([east_edge, rest], 0).T[:, :count]
    west = west + take(stacked(west_edge), edges_ref[:, :slots])
    east = east + take(stacked(east_edge), edges_ref[:, slots:])
    south, north = from_turns("gy", end1_ref[...], end2_ref[...])
    ends = end_values(south, north, ends_ref[...])
    fluxes = [tiles_of(flux_ref[i]) for i in range(5)] + [flux_ref[5, : width // CHUNK]]
    tiles = transport(
        tiles_of(c), tiles_of(s), fluxes, tiles_of(west), tiles_of(east), tiles_of(lower), tiles_of(upper), ends
    )
    for k, lines in enumerate(to_lines(tiles, scratch)):
        out_ref[pl.ds(k, devices, stride=2), :] = lines


def second_step(c, s, fluxes, inner, ends, edges, edge, end):
    width, slots = c.shape
    return pl.pallas_call(
        second_kernel,
        out_shape=jax.ShapeDtypeStruct((slots, width), F32),
        scratch_shapes=[pltpu.VMEM((2, width, slots // 2), F32)],
        compiler_params=params(16),
        name="second_step",
    )(c, s, fluxes, inner, ends, edges, *edge, *end)


def owner_kernel(mask_ref, recv_ref, out_ref):
    chosen = mask_ref[...]
    high, middle, low = (
        jnp.dot(chosen, part, preferred_element_type=F32) for part in split(recv_ref[...])
    )
    out_ref[...] = (low + middle) + high


def to_owner(mask, received):
    return pl.pallas_call(
        owner_kernel,
        out_shape=jax.ShapeDtypeStruct((mask.shape[0], received.shape[1]), F32),
        compiler_params=params(4),
        name="to_owner",
    )(mask, received)


def body(conductivity, storage, recharge, block_ids, neighbours, concentration, sorption):
    layers, rows_x, width = conductivity.shape
    devices = lax.axis_size(AXES)
    owned = concentration.shape[0]
    ids = block_ids.reshape(devices, owned)
    first, second = swap("gx", *pack_edges(conductivity, storage, recharge))
    (
        conductivity, storage, recharge, ids, concentration, sorption, own,
        inner, ends, sides, edges, picks, slots,
    ) = load(conductivity, storage, recharge, ids, concentration, sorption)
    strip, west, east, first, second = pack_strip(own, first, second)
    first, second = swap("gy", first, second)
    send, mask = pack_send(ids, concentration, sorption, layers, rows_x)
    faces = faces_of(conductivity, storage, west, east)
    base, image, gathered, send = flow(
        conductivity, storage, recharge, west, east, strip, first, second, send, slots, faces
    )
    received = lax.all_to_all(
        send.reshape(devices, 1, ROWS * width), AXES, split_axis=0, concat_axis=0, tiled=True
    ).reshape(devices * ROWS, width)
    c, s, flux, edge, end, on_base, on_image = first_step(received, gathered, inner, ends, sides, picks, layers)
    edge = swap("gx", edge, edge)
    end = swap("gy", end, end)
    head = on_base[None] * base + on_image[None] * image
    result = second_step(c, s, flux, inner, ends, edges, edge, end)
    returned = lax.all_to_all(
        result.reshape(devices, 2, width), AXES, split_axis=0, concat_axis=0, tiled=True
    ).reshape(devices * 2, width)
    return head, to_owner(mask, returned)


def solution(mesh):
    return jax.shard_map(
        body,
        mesh=mesh,
        in_specs=(
            P(None, "gx", "gy"),
            P(None, "gx", "gy"),
            P(None, "gx", "gy"),
            P(),
            P(("gx", "gy"), None),
            P(("gx", "gy"), None),
            P(("gx", "gy"), None),
        ),
        out_specs=(P(None, "gx", "gy"), P(("gx", "gy"), None)),
        check_vma=False,
    )
```

```python
import functools

import jax
import jax.numpy as jnp
from jax import lax
from jax.experimental import pallas as pl
from jax.experimental.pallas import tpu as pltpu
from jax.sharding import PartitionSpec as P

PICARD = 3
POROSITY = 0.35
BULK_DENSITY = 1.6
EXPONENT = 0.7
SOFTEN = 0.05
DISPERSION = 0.5
TIME_STEP = 0.1
ADVECT = 1.0
VERTICAL = 2.0
COUPLING = TIME_STEP * DISPERSION

AXES = ("gx", "gy")
ROWS = 9
NONE = -5000
F32 = jnp.float32
BF16 = jnp.bfloat16


def params(mib):
    return pltpu.CompilerParams(vmem_limit_bytes=int(mib * 1024 * 1024))


def iota(shape, dim):
    return lax.broadcasted_iota(jnp.int32, shape, dim)


def roll(x, shift, axis):
    return pltpu.roll(x, shift % x.shape[axis] if isinstance(shift, int) else shift, axis)


def split(x):
    high = x.astype(BF16)
    rest = x - high.astype(F32)
    middle = rest.astype(BF16)
    low = (rest - middle.astype(F32)).astype(BF16)
    return high, middle, low


def pick(mask, parts):
    chosen = jnp.where(mask, 1.0, 0.0).astype(BF16)
    high, middle, low = (jnp.dot(chosen, part, preferred_element_type=F32) for part in parts)
    return (low + middle) + high


def rows_of(parts, start, stop):
    return tuple(part[start:stop] for part in parts)


def place():
    across = lax.axis_size("gy")
    return lax.axis_index("gx") * across + lax.axis_index("gy")


def by_turns(axis, low, high):
    odd = jnp.full(low.shape, lax.axis_index(axis) % 2) == 1
    return jnp.where(odd, low, high), jnp.where(odd, high, low)


def from_turns(axis, first, second):
    at = jnp.full(first.shape, lax.axis_index(axis))
    odd = at % 2 == 1
    low = jnp.where(at == 0, 0.0, jnp.where(odd, first, second))
    high = jnp.where(at == lax.axis_size(axis) - 1, 0.0, jnp.where(odd, second, first))
    return low, high


def swap(axis, first, second):
    count = lax.axis_size(axis)
    one = [(i, i ^ 1) for i in range(count)]
    if axis == "gx":
        other = [(i, (i + 1 if i % 2 else i - 1) % count) for i in range(count)]
        return lax.ppermute(first, axis, one), lax.ppermute(second, axis, other)
    pairs = []
    for row in range(lax.axis_size("gx")):
        for i in range(count):
            partner = i + 1 if i % 2 else i - 1
            if 0 <= partner < count:
                pairs.append((row * count + i, row * count + partner))
            else:
                pairs.append((row * count + i, (row ^ 1) * count + i))
    return lax.ppermute(first, axis, one), lax.ppermute(second, AXES, pairs)


HBM = pl.BlockSpec(memory_space=pltpu.HBM)
SMEM = pl.BlockSpec(memory_space=pltpu.SMEM)
VMEM = pl.BlockSpec(memory_space=pltpu.VMEM)


def fetch(pairs, sems):
    copies = [pltpu.make_async_copy(src, dst, sems.at[i]) for i, (src, dst) in enumerate(pairs)]
    for copy in copies:
        copy.start()
    return copies


def pinned(arrays):
    return tuple(pltpu.with_memory_space_constraint(x, pltpu.HBM) for x in arrays)


def edges_kernel(k_hbm, s_hbm, r_hbm, first_ref, second_ref, tiles, sems):
    rows = k_hbm.shape[1]
    pairs = []
    for i, ref in enumerate((k_hbm, s_hbm, r_hbm)):
        pairs.append((ref.at[:, pl.ds(rows - 8, 8), :], tiles.at[2 * i]))
        pairs.append((ref.at[:, pl.ds(0, 8), :], tiles.at[2 * i + 1]))
    for copy in fetch(pairs, sems):
        copy.wait()
    sub = iota(first_ref.shape[1:], 0)
    for z in range(first_ref.shape[0]):
        east = jnp.where(
            sub >= 5,
            tiles[0, z],
            jnp.where(sub >= 3, roll(tiles[2, z], -3, 0), roll(tiles[4, z], -5, 0)),
        )
        west = jnp.where(
            sub < 3,
            tiles[1, z],
            jnp.where(sub < 5, roll(tiles[3, z], 3, 0), roll(tiles[5, z], 5, 0)),
        )
        first_ref[z], second_ref[z] = by_turns("gx", west, east)


def pack_edges(*arrays):
    layers, rows, width = arrays[0].shape
    tile = jax.ShapeDtypeStruct((layers, 8, width), F32)
    return pl.pallas_call(
        edges_kernel,
        in_specs=[HBM] * 3,
        out_specs=[VMEM] * 2,
        out_shape=[tile, tile],
        scratch_shapes=[pltpu.VMEM((6, layers, 8, width), F32), pltpu.SemaphoreType.DMA((6,))],
        compiler_params=params(8),
        name="pack_edges",
    )(*pinned(arrays))


def beside(index, z, west_ref, east_ref):
    shift = (0, 3, 5)[index]
    top, bottom = west_ref[z], east_ref[z]
    if shift:
        top, bottom = roll(top, shift, 0), roll(bottom, -shift, 0)
    return top, bottom


def widened(index, z, own_ref, west_ref, east_ref):
    top, bottom = beside(index, z, west_ref, east_ref)
    return jnp.concatenate([top, own_ref[z], bottom], 0)


def strip_of(layers, layer):
    strip = None
    for z in range(layers):
        turned = roll(layer(z), z * 8 + 4, 1)
        strip = turned if strip is None else jnp.where(iota(turned.shape, 1) >= z * 8, turned, strip)
    return strip


def strip_kernel(inner_ref, first_ref, second_ref, out_ref, west_ref, east_ref, one_ref, other_ref):
    layers = west_ref.shape[0]
    west_ref[...], east_ref[...] = from_turns("gx", first_ref[...], second_ref[...])
    rows = inner_ref.shape[1]
    for index in range(3):
        out_ref[index, 8 : 8 + rows] = inner_ref[index]
        out_ref[index, 0:8] = strip_of(layers, lambda z: beside(index, z, west_ref, east_ref)[0])
        out_ref[index, 8 + rows :] = strip_of(layers, lambda z: beside(index, z, west_ref, east_ref)[1])
    k, s, r = out_ref[0], out_ref[1], out_ref[2]
    slot = iota(k.shape, 1) % 8
    south = jnp.where(slot >= 4, k, jnp.where(slot >= 2, roll(s, -2, 1), roll(r, -4, 1)))
    north = jnp.where(slot < 4, k, jnp.where(slot < 6, roll(s, 2, 1), roll(r, 4, 1)))
    one_ref[...], other_ref[...] = by_turns("gy", south, north)


def pack_strip(inner, first, second):
    rows, width = inner.shape[1:]
    tile = jax.ShapeDtypeStruct(first.shape, F32)
    return pl.pallas_call(
        strip_kernel,
        out_shape=[jax.ShapeDtypeStruct((3, rows + 16, width), F32), tile, tile]
        + [jax.ShapeDtypeStruct((rows + 16, width), F32)] * 2,
        compiler_params=params(4),
        name="pack_strip",
    )(inner, first, second)


def column(row):
    n = row.shape[1]
    return jnp.sum(jnp.where(iota((n, n), 0) == iota((n, n), 1), row, 0.0), 1, keepdims=True)


def as_row(col):
    n = col.shape[0]
    return jnp.sum(jnp.where(iota((n, n), 0) == iota((n, n), 1), col, 0.0), 0, keepdims=True)


def slot_codes(ids, target, lines):
    brick = ids // lines
    key = iota(ids.shape, 1) * lines + ids % lines
    mine = brick == target
    first = jnp.min(jnp.where(mine, key, ids.shape[1] * lines).astype(F32), 1, keepdims=True)
    second = jnp.max(jnp.where(mine, key, -1).astype(F32), 1, keepdims=True)
    cols = [
        jnp.where(second >= 0.0, code.astype(jnp.int32) % lines, NONE).astype(F32)
        for code in (first, second)
    ]
    rows = [as_row(col) for col in cols]
    return jnp.concatenate(cols, 0).astype(jnp.int32), jnp.concatenate(rows, 1).astype(jnp.int32)


def load_kernel(
    down, across,
    k_hbm, s_hbm, r_hbm, ids_hbm, conc_hbm, sorp_hbm,
    k_ref, s_ref, r_ref, ids_ref, conc_ref, sorp_ref, own_ref,
    inner_ref, ends_ref, sides_ref, edges_ref, pick_ref, slots_ref,
    sems,
):
    refs = (k_ref, s_ref, r_ref)
    copies = fetch(
        [
            (ids_hbm, ids_ref),
            (k_hbm, k_ref),
            (s_hbm, s_ref),
            (r_hbm, r_ref),
            (conc_hbm, conc_ref),
            (sorp_hbm, sorp_ref),
        ],
        sems,
    )
    layers, rows_x = k_ref.shape[:2]
    slots = slots_ref.shape[1]
    lines = layers * rows_x
    me = place()
    gx, gy = me // across, me % across
    copies[0].wait()
    ids = ids_ref[...]
    code, slot = slot_codes(ids, me, lines)
    west, _ = slot_codes(ids, jnp.where(gx > 0, me - across, -1), lines)
    east, _ = slot_codes(ids, jnp.where(gx < down - 1, me + across, -1), lines)
    south, _ = slot_codes(ids, jnp.where(gy > 0, me - 1, -1), lines)
    north, _ = slot_codes(ids, jnp.where(gy < across - 1, me + 1, -1), lines)
    slots_ref[...] = slot
    active = slot >= 0
    layer, row = slot // rows_x, slot % rows_x
    low, high = active & (row == 0), active & (row == rows_x - 1)

    def ones(mask):
        return jnp.where(mask, 1.0, 0.0).astype(BF16)

    inner_ref[:, :slots] = ones((code == slot - 1) & (row != 0))
    inner_ref[:, slots : 2 * slots] = ones((code == slot + 1) & (row != rows_x - 1))
    inner_ref[:, 2 * slots : 3 * slots] = ones(code == slot - rows_x)
    inner_ref[:, 3 * slots :] = ones(code == slot + rows_x)
    ends_ref[:, :slots] = ones((south == slot) & active)
    ends_ref[:, slots:] = ones((north == slot) & active)
    sides_ref[:, :slots] = ones((west == slot + rows_x - 1) & low)
    sides_ref[:, slots:] = ones((east == slot - rows_x + 1) & high)
    at = iota((edges_ref.shape[0], slots), 0)
    edges_ref[:, :slots] = ones((at == layer) & low)
    edges_ref[:, slots:] = ones((at == layer + layers) & high)
    at = iota((slots, pick_ref.shape[1]), 1)
    pick_ref[...] = ones(
        (code >= 0)
        & (
            ((code % rows_x == rows_x - 1) & (code // rows_x == at))
            | ((code % rows_x == 0) & (code // rows_x + layers == at))
        )
    )
    for index, ref in enumerate(refs):
        copies[1 + index].wait()
        own_ref[index] = strip_of(layers, lambda z: ref[z])
    copies[4].wait()
    copies[5].wait()


def load(*arrays):
    rows, width = arrays[0].shape[1:]
    layers = arrays[0].shape[0]
    slots = 2 * arrays[3].shape[0]
    kernel = functools.partial(load_kernel, lax.axis_size("gx"), lax.axis_size("gy"))
    return pl.pallas_call(
        kernel,
        in_specs=[HBM] * 6,
        out_specs=[VMEM] * 13,
        out_shape=[jax.ShapeDtypeStruct(x.shape, x.dtype) for x in arrays]
        + [
            jax.ShapeDtypeStruct((3, rows, width), F32),
            jax.ShapeDtypeStruct((slots, 4 * slots), BF16),
            jax.ShapeDtypeStruct((slots, 2 * slots), BF16),
            jax.ShapeDtypeStruct((slots, 2 * slots), BF16),
            jax.ShapeDtypeStruct((2 * layers, 2 * slots), BF16),
            jax.ShapeDtypeStruct((slots, width), BF16),
            jax.ShapeDtypeStruct((1, slots), jnp.int32),
        ],
        scratch_shapes=[pltpu.SemaphoreType.DMA((6,))],
        compiler_params=params(8),
        name="load",
    )(*pinned(arrays))


def send_kernel(
    across, rows_x, layers, ids_ref, conc_ref, sorp_ref, out_ref, mask_ref
):
    devices, owned = ids_ref.shape
    lines = layers * rows_x
    me = place()
    own = ids_ref[pl.ds(me, 1), :]
    own_brick = own // lines
    own_row = own % lines % rows_x
    brick_col = column(own_brick.astype(F32)).astype(jnp.int32)
    square = (owned, owned)
    same = (brick_col == own_brick) & (iota(square, 0) < iota(square, 1))
    rank = jnp.sum(jnp.where(same, 1.0, 0.0), 0, keepdims=True).astype(jnp.int32)
    back = jnp.where(iota((2 * devices, owned), 0) == own_brick * 2 + rank, 1.0, 0.0)
    mask_ref[...] = back.T.astype(BF16)
    dest = iota((devices, owned), 0)
    conc = conc_ref[...]
    conc_parts = split(conc)
    sorp_parts = split(sorp_ref[...])
    lane = iota((owned, conc.shape[1]), 1)
    misc = jnp.zeros((devices, conc.shape[1]), F32)
    for k in range(2):
        ranked = rank == k
        home = (dest == own_brick) & ranked
        out_ref[pl.ds(k, devices, stride=ROWS), :] = pick(home, conc_parts)
        out_ref[pl.ds(2 + k, devices, stride=ROWS), :] = pick(home, sorp_parts)
        after = (dest == own_brick + across) & ranked & (own_row == rows_x - 1)
        out_ref[pl.ds(4 + k, devices, stride=ROWS), :] = pick(after, conc_parts)
        before = (dest == own_brick - across) & ranked & (own_row == 0)
        out_ref[pl.ds(6 + k, devices, stride=ROWS), :] = pick(before, conc_parts)
        tails = jnp.where(lane // 2 == k, roll(conc, 2 + 2 * k, 1), 0.0)
        heads = jnp.where(lane // 2 == 2 + k, roll(conc, 4 + 2 * k, 1), 0.0)
        north = (dest == own_brick + 1) & ranked & (own_brick % across < across - 1)
        south = (dest == own_brick - 1) & ranked & (own_brick % across > 0)
        misc = misc + pick(north, split(tails)) + pick(south, split(heads))
    out_ref[pl.ds(8, devices, stride=ROWS), :] = misc


def pack_send(ids, concentration, sorption, layers, rows_x):
    devices, owned = ids.shape
    width = concentration.shape[1]
    slots = 2 * devices
    kernel = functools.partial(send_kernel, lax.axis_size("gy"), rows_x, layers)
    return pl.pallas_call(
        kernel,
        out_shape=[
            jax.ShapeDtypeStruct((devices * ROWS, width), F32),
            jax.ShapeDtypeStruct((owned, slots), BF16),
        ],
        compiler_params=params(8),
        name="pack_send",
    )(ids, concentration, sorption)


def harmonic(a, c):
    return jnp.where(jnp.minimum(a, c) > 0.0, 2.0 * a * c / (a + c), jnp.maximum(a, c))


def faces_kernel(k_ref, s_ref, west_ref, east_ref, fw, fs, fb, part):
    layers, rows, width = k_ref.shape
    shape = (rows + 16, width)
    lane = iota(shape, 1)
    fb[0] = jnp.zeros(shape, F32)

    def step(z, carry):
        k = widened(0, z, k_ref, west_ref, east_ref)
        face_w = harmonic(k, roll(k, 1, 0))
        face_s = jnp.where(lane == 0, 0.0, harmonic(k, roll(k, 1, 1)))
        upper = widened(0, jnp.minimum(z + 1, layers - 1), k_ref, west_ref, east_ref)
        face_a = jnp.where(z < layers - 1, VERTICAL * harmonic(k, upper), 0.0)
        s = widened(1, z, s_ref, west_ref, east_ref)
        fw[z] = face_w
        fs[z] = face_s
        part[z] = s + face_w + roll(face_w, -1, 0) + face_s + roll(face_s, -1, 1) + fb[z] + face_a
        fb[z + 1] = face_a
        return carry

    lax.fori_loop(0, layers, step, 0, unroll=8)


def faces_of(conductivity, storage, west, east):
    layers, rows, width = conductivity.shape
    tall = jax.ShapeDtypeStruct((layers, rows + 16, width), F32)
    return pl.pallas_call(
        faces_kernel,
        out_shape=[tall, tall, jax.ShapeDtypeStruct((layers + 1, rows + 16, width), F32), tall],
        compiler_params=params(8),
        name="faces",
    )(conductivity, storage, west, east)


def flow_kernel(
    k_ref, s_ref, r_ref, west_ref, east_ref, strip_ref, first_ref, second_ref, send_ref, slots_ref,
    fw, fs, fb, part,
    d_out, w_out, gath_out, send_out,
    rd, dd, ww, lines_ref,
):
    layers, rows, width = k_ref.shape
    tall = rows + 16
    shape = (tall, width)
    lane = iota(shape, 1)
    slot = lane % 8
    devices = send_ref.shape[0] // ROWS

    send_out[...] = send_ref[...]

    def side(low):
        def joined(index):
            south, north = from_turns("gy", first_ref[...], second_ref[...])
            shift = 2 * index
            if low:
                return jnp.where(slot < 4, roll(south, -shift, 1), strip_ref[index])
            return jnp.where(slot < 4, strip_ref[index], roll(north, shift, 1))

        k, s, r = joined(0), joined(1), joined(2)
        face_w = harmonic(k, roll(k, 1, 0))
        face_s = harmonic(k, roll(k, 1, 1))
        face_b = jnp.where(lane >= 8, VERTICAL * harmonic(k, roll(k, 8, 1)), 0.0)
        diagonal = (
            s + face_w + roll(face_w, -1, 0) + face_s + roll(face_s, -1, 1) + face_b + roll(face_b, -8, 1)
        )
        inverse = jnp.where(k > 0.0, 1.0 / diagonal, 0.0)
        d = r * inverse
        flux_w = face_w * (roll(d, 1, 0) - d)
        flux_s = face_s * (roll(d, 1, 1) - d)
        flux_b = face_b * (roll(d, 8, 1) - d)
        image = (
            s * d
            + (roll(flux_w, -1, 0) - flux_w)
            + (roll(flux_s, -1, 1) - flux_s)
            + (roll(flux_b, -8, 1) - flux_b)
        )
        w = image * inverse
        return face_s, flux_s, face_s * (roll(w, 1, 1) - w)

    low_face, low_d, low_w = side(True)
    high_face, high_d, high_w = side(False)

    def with_low(z, field, strip):
        return jnp.where(lane == 0, roll(strip, width - 4 - z * 8, 1), field)

    def north_of(z, field, strip):
        shift = lax.rem(width - 5 + width - z * 8, width)
        return jnp.where(lane == width - 1, roll(strip, shift, 1), roll(field, -1, 1))

    def scale(z, carry):
        k = widened(0, z, k_ref, west_ref, east_ref)
        r = widened(2, z, r_ref, west_ref, east_ref)
        low = jnp.where(lane == 0, roll(low_face, width - 4 - z * 8, 1), 0.0)
        shift = lax.rem(width - 5 + width - z * 8, width)
        high = jnp.where(lane == width - 1, roll(high_face, shift, 1), 0.0)
        diagonal = part[z] + low + high
        inverse = jnp.where(k > 0.0, 1.0 / diagonal, 0.0)
        rd[z] = inverse
        dd[z] = r * inverse
        return carry

    lax.fori_loop(0, layers, scale, 0, unroll=8)

    def total(x):
        return jnp.sum(x[8 : 8 + rows].reshape(rows // 8, 8, width), 0)

    def apply(z, field, low, high, block):
        h = field[z]
        below = field[jnp.maximum(z - 1, 0)]
        above = field[jnp.minimum(z + 1, layers - 1)]
        flux_w = fw[z] * (roll(h, 1, 0) - h)
        flux_e = roll(flux_w, -1, 0)
        flux_b = fb[z] * (below - h)
        flux_a = fb[z + 1] * (h - above)
        flux_s = with_low(z, fs[z] * (roll(h, 1, 1) - h), low)
        flux_n = north_of(z, flux_s, high)
        for at, flux in enumerate((flux_w, flux_e, flux_b, flux_a, flux_s, flux_n)):
            start = z * (rows * 16) + (block + at)
            lines_ref[pl.ds(start, rows, stride=16), :] = flux[8 : 8 + rows]
        s = widened(1, z, s_ref, west_ref, east_ref)
        return h, s * h + (flux_e - flux_w) + (flux_a - flux_b) + (flux_n - flux_s)

    zero = jnp.zeros((8, width), F32)

    def first(z, sums):
        d, image = apply(z, dd, low_d, high_d, 0)
        w = image * rd[z]
        ww[z] = w
        d_out[z] = d[8 : 8 + rows]
        w_out[z] = w[8 : 8 + rows]
        r = r_ref[z]
        gamma = jnp.sum((r * d[8 : 8 + rows]).reshape(rows // 8, 8, width), 0)
        return sums[0] + gamma, sums[1] + total(d * image), sums[2] + total(image * w)

    gamma, bend, curve = lax.fori_loop(0, layers, first, (zero, zero, zero), unroll=8)

    def second(z, acc):
        w, image = apply(z, ww, low_w, high_w, 6)
        return acc + total(w * image)

    twist = lax.fori_loop(0, layers, second, zero, unroll=8)
    lane_row = iota((devices, width), 1)
    misc = send_ref[pl.ds(8, devices, stride=ROWS), :]
    for at, part in enumerate((gamma, bend, curve, twist)):
        value = jnp.sum(jnp.sum(part, 0, keepdims=True), 1, keepdims=True)
        misc = jnp.where(lane_row == 8 + at, value, misc)
    send_out[pl.ds(8, devices, stride=ROWS), :] = misc
    for k in range(2):

        def gather(i, carry):
            line = pl.multiple_of(jnp.maximum(slots_ref[0, k * devices + i], 0) * 16, 16)
            slot = pl.multiple_of((k * devices + i) * 16, 16)
            gath_out[pl.ds(slot, 16), :] = lines_ref[pl.ds(line, 16), :]
            return carry

        lax.fori_loop(0, devices, gather, 0, unroll=8)


def flow(conductivity, storage, recharge, west, east, strip, first, second, send, slots, faces):
    layers, rows, width = conductivity.shape
    tall = pltpu.VMEM((layers, rows + 16, width), F32)
    return pl.pallas_call(
        flow_kernel,
        out_shape=[
            jax.ShapeDtypeStruct(conductivity.shape, F32),
            jax.ShapeDtypeStruct(conductivity.shape, F32),
            jax.ShapeDtypeStruct((slots.shape[1] * 16, width), F32),
            jax.ShapeDtypeStruct(send.shape, F32),
        ],
        in_specs=[VMEM] * 9 + [SMEM] + [VMEM] * 4,
        out_specs=[VMEM] * 4,
        scratch_shapes=[tall] * 3 + [pltpu.VMEM((layers * rows * 16, width), F32)],
        compiler_params=params(20),
        name="flow",
    )(conductivity, storage, recharge, west, east, strip, first, second, send, slots, *faces)


CHUNK = 16


def minmod(a, d):
    return jnp.maximum(jnp.minimum(a, d), 0.0) + jnp.minimum(jnp.maximum(a, d), 0.0)


def to_cells(lines, scratch):
    half = lines.shape[0] // 2
    count = lines.shape[1] // CHUNK
    for k in range(2):
        scratch[k] = lines[k * half : (k + 1) * half].T
    tiles = [
        jnp.concatenate([scratch[k, pl.ds(j, count, stride=CHUNK), :] for k in range(2)], 1)
        for j in range(CHUNK)
    ]
    return jnp.concatenate(tiles, 0)


def to_lines(tiles, scratch):
    half = tiles[0].shape[1] // 2
    count = tiles[0].shape[0]
    for k in range(2):
        for j, tile in enumerate(tiles):
            scratch[k, pl.ds(j, count, stride=CHUNK), :] = tile[:, k * half : (k + 1) * half]
    return [scratch[k].T for k in range(2)]


def stacked(x):
    return jnp.concatenate(split(x), 0)


def take(parts, chosen):
    out = jnp.dot(parts, chosen, preferred_element_type=F32)
    count = parts.shape[0] // 3
    return (out[2 * count :] + out[count : 2 * count]) + out[:count]


def reduction(side, diagonal, right):
    count = diagonal.shape[0]
    step = 1
    while step < count:
        inverse = 1.0 / diagonal
        scaled = side * inverse
        value = right * inverse
        right = right - side * roll(value, step, 0) - roll(side * value, -step, 0)
        diagonal = diagonal - side * (side * roll(inverse, step, 0)) - roll(side * scaled, -step, 0)
        side = -side * roll(scaled, step, 0)
        step *= 2
    return right / diagonal


def tridiagonal(diagonal, right):
    off = -COUPLING
    last = CHUNK - 1
    one = jnp.ones_like(diagonal[0])
    zero = jnp.zeros_like(one)
    lead, lead_right = [one, diagonal[0]], [right[0]]
    for j in range(1, last):
        lead_right.append(right[j] * lead[j] - off * lead_right[j - 1])
        lead.append(diagonal[j] * lead[j] - (off * off) * lead[j - 1])
    trail, trail_right = {last: one, last + 1: zero}, {last: zero}
    for j in range(last - 1, -1, -1):
        trail_right[j] = right[j] * trail[j + 1] - off * trail_right[j + 1]
        trail[j] = diagonal[j] * trail[j + 1] - (off * off) * trail[j + 2]
    inverse = 1.0 / lead[last]
    sub = iota(one.shape, 0)
    top = sub == one.shape[0] - 1
    far = off * (-off) ** (last - 1)
    side = jnp.where(sub == 0, 0.0, (-off * far) * inverse)
    above = jnp.where(top, 0.0, roll(trail[1] * inverse, -1, 0))
    above_right = jnp.where(top, 0.0, roll(trail_right[0] * inverse, -1, 0))
    z = reduction(
        side,
        diagonal[last] - (off * off) * (lead[last - 1] * inverse + above),
        right[last] - off * (lead_right[last - 1] * inverse + above_right),
    )
    before = jnp.where(sub == 0, 0.0, roll(z, 1, 0))
    out = []
    for j in range(last):
        low = lead_right[j] - (off * (-off) ** j) * before
        high = off * trail_right[j + 1] + (off * (-off) ** (last - 1 - j)) * z
        out.append(inverse * (trail[j + 1] * low - lead[j] * high))
    return out + [z]


def transport(c, sorption, fluxes, west, east, lower, upper, ends):
    q_w, q_e, q_b, q_a, q_s, q_n = fluxes
    south_two, south_one, north_one, north_two = ends
    sub = iota(c[0].shape, 0)
    bottom, top = sub == 0, sub == c[0].shape[0] - 1
    before = [
        jnp.where(bottom, south_two, roll(c[-2], 1, 0)),
        jnp.where(bottom, south_one, roll(c[-1], 1, 0)),
    ]
    after = [
        jnp.where(top, north_one, roll(c[0], -1, 0)),
        jnp.where(top, north_two, roll(c[1], -1, 0)),
    ]
    line = before + c + after

    def face(q, far_left, left, right, far_right):
        rise = right - left
        positive = left + 0.5 * minmod(rise, left - far_left)
        negative = right + 0.5 * minmod(-rise, right - far_right)
        return jnp.maximum(q, 0.0) * positive + jnp.minimum(q, 0.0) * negative

    along = [face(q_s[j], *line[j : j + 4]) for j in range(CHUNK)]
    beyond = face(q_n, *line[CHUNK : CHUNK + 4])
    along.append(jnp.where(top, beyond, roll(along[0], -1, 0)))
    v = list(c)
    source = [None] * CHUNK
    diagonal, right = [None] * CHUNK, [None] * CHUNK
    for sweep in range(PICARD):
        for j in range(CHUNK):
            square = v[j] * v[j] + SOFTEN * SOFTEN
            power = (BULK_DENSITY * sorption[j]) * jnp.exp(
                (0.5 * (EXPONENT - 1.0)) * jnp.log(square)
            )
            retard = POROSITY + power
            root = jnp.sqrt(square)
            if sweep == 0:
                value = c[j]
                advect = along[j] - along[j + 1]
                advect = advect + jnp.maximum(q_w[j], 0.0) * west[j] + jnp.minimum(q_w[j], 0.0) * value
                advect = advect - jnp.maximum(q_e[j], 0.0) * value - jnp.minimum(q_e[j], 0.0) * east[j]
                advect = advect + jnp.maximum(q_b[j], 0.0) * lower[j] + jnp.minimum(q_b[j], 0.0) * value
                advect = advect - jnp.maximum(q_a[j], 0.0) * value - jnp.minimum(q_a[j], 0.0) * upper[j]
                advect = ADVECT * advect
                if j == 0:
                    advect = advect + jnp.where(bottom, COUPLING * south_one, 0.0)
                if j == CHUNK - 1:
                    advect = advect + jnp.where(top, COUPLING * north_one, 0.0)
                source[j] = POROSITY * value + power * root + advect
                right[j] = retard * value + advect
            else:
                right[j] = power * (v[j] - root) + source[j]
            diagonal[j] = retard + 2.0 * COUPLING
        v = tridiagonal(diagonal, right)
    return v


def tiles_of(x):
    count = x.shape[0] // CHUNK
    return [x[j * count : (j + 1) * count] for j in range(CHUNK)]


def inner_neighbours(c, chosen):
    slots = c.shape[1]
    values = take(stacked(c), chosen)
    return [values[:, i * slots : (i + 1) * slots] for i in range(4)]


def end_values(south, north, chosen):
    slots = south.shape[1]
    tails = take(stacked(south), chosen[:, :slots])
    heads = take(stacked(north), chosen[:, slots:])
    return tails[0:1], tails[1:2], heads[2:3], heads[3:4]


def first_kernel(
    recv_ref, gath_ref, inner_ref, ends_ref, sides_ref, pick_ref,
    c_out, s_out, flux_out, edge_out, end_out, scal_out, scratch,
):
    devices = recv_ref.shape[0] // ROWS
    slots = 2 * devices
    width = recv_ref.shape[1]

    def received(at):
        return recv_ref[pl.ds(at, devices, stride=ROWS), :]

    def pair(at):
        return jnp.concatenate([received(at), received(at + 1)], 0)

    misc = received(8)
    sums = jnp.sum(misc, 0, keepdims=True)
    at = iota(sums.shape, 1)
    gamma, bend, curve, twist = (
        jnp.sum(jnp.where(at == 8 + i, sums, 0.0), 1, keepdims=True) for i in range(4)
    )
    alpha = gamma / bend
    gamma_next = alpha * alpha * curve - gamma
    beta = gamma_next / gamma
    cross = bend - alpha * curve
    bend_next = bend - 2.0 * alpha * curve + alpha * alpha * twist + 2.0 * beta * cross + beta * beta * bend
    alpha_next = gamma_next / bend_next
    on_d = alpha + alpha_next * (1.0 + beta)
    on_w = -alpha * alpha_next
    scal_out[...] = jnp.where(iota((8, width), 1) == 0, on_d, on_w)

    c = to_cells(pair(0), scratch.at[0])
    s = to_cells(pair(2), scratch.at[1])
    s_out[...] = s
    beside_w = to_cells(pair(4), scratch.at[2])
    beside_e = to_cells(pair(6), scratch.at[3])
    fluxes = []
    for i in range(6):
        flux = on_d * gath_ref[pl.ds(i, slots, stride=16), :]
        flux = flux + on_w * gath_ref[pl.ds(6 + i, slots, stride=16), :]
        flux = to_cells(flux, scratch.at[4 + i])
        if i == 5:
            flux = flux[width - width // CHUNK :]
            flux_out[5, : flux.shape[0]] = flux
            fluxes.append(flux)
        else:
            flux_out[i] = flux
            fluxes.append(tiles_of(flux))
    west, east, lower, upper = inner_neighbours(c, inner_ref[...])
    west = west + take(stacked(beside_w), sides_ref[:, :slots])
    east = east + take(stacked(beside_e), sides_ref[:, slots:])
    turned = misc.T
    ends = [
        jnp.concatenate([turned[a : a + 1], turned[a + 2 : a + 3]], 1) for a in (0, 1, 4, 5)
    ] + [jnp.zeros((4, slots), F32)]
    ends = jnp.concatenate(ends, 0)
    ends = end_values(ends, ends, ends_ref[...])
    tiles = transport(
        tiles_of(c), tiles_of(s), fluxes, tiles_of(west), tiles_of(east), tiles_of(lower), tiles_of(upper), ends
    )
    c = jnp.concatenate(tiles, 0)
    c_out[...] = c
    count = tiles[0].shape[0]
    end_out[...] = jnp.concatenate(
        [
            tiles[-2][count - 1 :],
            tiles[-1][count - 1 :],
            tiles[0][:1],
            tiles[1][:1],
            jnp.zeros((4, slots), F32),
        ],
        0,
    )
    edge = take(stacked(c), pick_ref[...])
    edge_out[...] = edge.T[: edge_out.shape[0]]


def first_step(received, gathered, inner, ends, sides, picks, layers):
    width = received.shape[1]
    slots = inner.shape[0]
    cells = jax.ShapeDtypeStruct((width, slots), F32)
    return pl.pallas_call(
        first_kernel,
        out_shape=[
            cells,
            cells,
            jax.ShapeDtypeStruct((6, width, slots), F32),
            jax.ShapeDtypeStruct((2 * layers, width), F32),
            jax.ShapeDtypeStruct((8, slots), F32),
            jax.ShapeDtypeStruct((8, width), F32),
        ],
        scratch_shapes=[pltpu.VMEM((10, 2, width, slots // 2), F32)],
        compiler_params=params(16),
        name="first_step",
    )(received, gathered, inner, ends, sides, picks)


def second_kernel(
    c_ref, s_ref, flux_ref, inner_ref, ends_ref, edges_ref, edge1_ref, edge2_ref, end1_ref, end2_ref, out_ref, scratch
):
    c, s = c_ref[...], s_ref[...]
    width, slots = c.shape
    devices = slots // 2
    west, east, lower, upper = inner_neighbours(c, inner_ref[...])
    west_edge, east_edge = from_turns("gx", edge1_ref[...], edge2_ref[...])
    rest = jnp.zeros((width - west_edge.shape[0], width), F32)
    count = west_edge.shape[0]
    west_edge = jnp.concatenate([west_edge, rest], 0).T[:, :count]
    east_edge = jnp.concatenate([east_edge, rest], 0).T[:, :count]
    west = west + take(stacked(west_edge), edges_ref[:, :slots])
    east = east + take(stacked(east_edge), edges_ref[:, slots:])
    south, north = from_turns("gy", end1_ref[...], end2_ref[...])
    ends = end_values(south, north, ends_ref[...])
    fluxes = [tiles_of(flux_ref[i]) for i in range(5)] + [flux_ref[5, : width // CHUNK]]
    tiles = transport(
        tiles_of(c), tiles_of(s), fluxes, tiles_of(west), tiles_of(east), tiles_of(lower), tiles_of(upper), ends
    )
    for k, lines in enumerate(to_lines(tiles, scratch)):
        out_ref[pl.ds(k, devices, stride=2), :] = lines


def second_step(c, s, fluxes, inner, ends, edges, edge, end):
    width, slots = c.shape
    return pl.pallas_call(
        second_kernel,
        out_shape=jax.ShapeDtypeStruct((slots, width), F32),
        scratch_shapes=[pltpu.VMEM((2, width, slots // 2), F32)],
        compiler_params=params(16),
        name="second_step",
    )(c, s, fluxes, inner, ends, edges, *edge, *end)


def owner_kernel(mask_ref, recv_ref, out_ref):
    chosen = mask_ref[...]
    high, middle, low = (
        jnp.dot(chosen, part, preferred_element_type=F32) for part in split(recv_ref[...])
    )
    out_ref[...] = (low + middle) + high


def to_owner(mask, received):
    return pl.pallas_call(
        owner_kernel,
        out_shape=jax.ShapeDtypeStruct((mask.shape[0], received.shape[1]), F32),
        compiler_params=params(4),
        name="to_owner",
    )(mask, received)


def body(conductivity, storage, recharge, block_ids, neighbours, concentration, sorption):
    layers, rows_x, width = conductivity.shape
    devices = lax.axis_size(AXES)
    owned = concentration.shape[0]
    ids = block_ids.reshape(devices, owned)
    first, second = swap("gx", *pack_edges(conductivity, storage, recharge))
    (
        conductivity, storage, recharge, ids, concentration, sorption, own,
        inner, ends, sides, edges, picks, slots,
    ) = load(conductivity, storage, recharge, ids, concentration, sorption)
    strip, west, east, first, second = pack_strip(own, first, second)
    first, second = swap("gy", first, second)
    send, mask = pack_send(ids, concentration, sorption, layers, rows_x)
    faces = faces_of(conductivity, storage, west, east)
    base, image, gathered, send = flow(
        conductivity, storage, recharge, west, east, strip, first, second, send, slots, faces
    )
    received = lax.all_to_all(
        send.reshape(devices, 1, ROWS * width), AXES, split_axis=0, concat_axis=0, tiled=True
    ).reshape(devices * ROWS, width)
    c, s, flux, edge, end, scal = first_step(received, gathered, inner, ends, sides, picks, layers)
    edge = swap("gx", edge, edge)
    end = swap("gy", end, end)
    head = scal[0, 0] * base + scal[0, 1] * image
    result = second_step(c, s, flux, inner, ends, edges, edge, end)
    returned = lax.all_to_all(
        result.reshape(devices, 2, width), AXES, split_axis=0, concat_axis=0, tiled=True
    ).reshape(devices * 2, width)
    return head, to_owner(mask, returned)


def solution(mesh):
    return jax.shard_map(
        body,
        mesh=mesh,
        in_specs=(
            P(None, "gx", "gy"),
            P(None, "gx", "gy"),
            P(None, "gx", "gy"),
            P(),
            P(("gx", "gy"), None),
            P(("gx", "gy"), None),
            P(("gx", "gy"), None),
        ),
        out_specs=(P(None, "gx", "gy"), P(("gx", "gy"), None)),
        check_vma=False,
    )
```
